128 devices in a mesh: ep: 16 (over x_lo, z, core), rep: 8 (over x_hi, y).
Axes of the slice: x: 4 (x_hi: 2, x_lo: 2; x = x_hi * 2 + x_lo), y: 4, z: 4, core: 2. Of those that a mesh axis runs over, the one named last changes fastest.
Arguments:
- tokens: bfloat16 [2048, 4096], P('ep', 'rep'), may hold values from -6 to 6
- cotangent: bfloat16 [2048, 4096], P('ep', 'rep'), may hold values from -6 to 6
- router_weights: float32 [2048, 8], P('ep'), may hold values from 0.02 to 0.3
- routes: int32 [2048, 8], P('ep'), may hold values from 0 to 31, all different within a row; in each aligned block of 128 rows (0 to 127, 128 to 255, ...) at most 96 rows name the same one
- replica_map: int32 [16], replicated, may hold values from 0 to 15
- gate_primary: bfloat16 [16, 4096, 1536], P('ep', None, 'rep'), may hold values from -0.09375 to 0.09375
- up_primary: bfloat16 [16, 4096, 1536], P('ep', None, 'rep'), may hold values from -0.09375 to 0.09375
- down_primary: bfloat16 [16, 1536, 4096], P('ep', None, 'rep'), may hold values from -0.15625 to 0.15625
- gate_replica: bfloat16 [16, 4096, 1536], P('ep', None, 'rep'), may hold values from -0.09375 to 0.09375
- up_replica: bfloat16 [16, 4096, 1536], P('ep', None, 'rep'), may hold values from -0.09375 to 0.09375
- down_replica: bfloat16 [16, 1536, 4096], P('ep', None, 'rep'), may hold values from -0.15625 to 0.15625
- moment1: float32 [16, 1536, 4096], P('ep', None, 'rep'), may hold values from -6 to 6
- moment2: float32 [16, 1536, 4096], P('ep', None, 'rep'), may hold values from 0.5 to 8
Outputs:
- layer_output: bfloat16 [2048, 4096], P('ep', 'rep')
- down_new: bfloat16 [16, 1536, 4096], P('ep', None, 'rep')
- moment1_new: float32 [16, 1536, 4096], P('ep', None, 'rep')
- moment2_new: float32 [16, 1536, 4096], P('ep', None, 'rep')
- replica_down_new: bfloat16 [16, 1536, 4096], P('ep', None, 'rep')
The draws below stay inside these ranges and needn't reach their ends.
Inputs may be any that keep to these rules, and one draw needn't show every extreme that they name: `routes`: each row names 8 different slots; in the rows of one device (aligned blocks of 128 rows) no slot is named by more than 96 rows, a bound that some block reaches.
All inputs are finite; a program needn't handle non-finite values.
Results may differ from the reference program's by a relative error of at most 0.014.
Values may be sent and summed in bfloat16 or wider, within the bound.
No kernel may reach another device: no remote copies, remote signals or barrier semaphores. Data moves between devices by JAX's collectives and lax.ppermute only.
A program may use at most 192 MiB of HBM per device.

```python
import math
import jax
import jax.numpy as jnp
import numpy as np
from jax import lax

D = 4096
FF = 1536
K = 8
TOK_DEV = 128
EXPERTS = 16
SLOTS = 32
CAP = 96
TOKENS = 2048
N_EP = 16


def touch_ends(values, rng, smallest, high):
    dims = values.shape
    place = [jax.random.randint(jax.random.fold_in(rng, axis), (), 0, dims[axis]) for axis in range(len(dims))]
    values = values.at[tuple(place)].set(smallest)
    longest = dims.index(max(dims))
    place[longest] = (place[longest] + 1) % dims[longest]
    return values.at[tuple(place)].set(high)


def levels(own_key, dims, split, low, largest):
    factor_of = 1.0
    for dim, shards_of in split:
        heights = jax.random.uniform(jax.random.fold_in(jax.random.fold_in(own_key, 6), dim), (shards_of,), jnp.float32, low / len(split), largest / len(split))
        factor_of = factor_of * jnp.repeat(jnp.exp(heights), dims[dim] // shards_of).reshape((-1,) + (1,) * (len(dims) - 1 - dim))
    return factor_of


def cumulative_ranks(count, lean):
    loads = [(1 << 20) // math.isqrt(grade ** lean) + 1 for grade in range(1, count + 1)]
    deviation = 1 + sum(loads) // (1 << 30)
    return np.cumsum(np.array([max(1, weight // deviation) for weight in loads]))


def skewed_ids(key, dims, count, slope):
    listing = cumulative_ranks(count, slope)
    pick = jax.random.randint(jax.random.fold_in(key, 1), dims, 0, int(listing[count - 1]))
    rank = jnp.searchsorted(jnp.asarray(listing, jnp.int32), pick, side="right")
    return jax.random.permutation(jax.random.fold_in(key, 2), count)[rank].astype(jnp.int32)


def assign_block(rng, own, number, rows, amount, top, most, slope):
    order = jax.random.permutation(rng, amount)
    heavy_load, usual = shares(amount, rows * top, most, slope, True), shares(amount, rows * top, most, slope, False)
    places = jnp.arange(amount)

    def named(tallies, rotation):
        used = int((tallies > 0).sum())
        fixed = max(1, used // 4)
        shifted = fixed + (places - fixed + rotation * (used - fixed)) % max(1, amount - fixed)
        return jnp.zeros((amount,), jnp.int32).at[order[jnp.where(places < fixed, places, shifted)]].set(jnp.asarray(tallies, jnp.int32))

    tallies = jnp.where(number % 4 == 0, named(heavy_load, number // 4), named(usual, number - number // 4 - 1))
    mixed = jax.random.permutation(jax.random.fold_in(own, 3), amount)
    source_of, sink = mixed[0:amount // 2 * 2:2], mixed[1:amount // 2 * 2:2]
    margin = jnp.minimum(tallies[source_of] - 1, most - tallies[sink]) // 2
    margin = jnp.where((source_of == order[0]) | (sink == order[0]) | (tallies[sink] == 0), 0, jnp.maximum(margin, 0))
    shifted = jax.random.randint(jax.random.fold_in(own, 4), (amount // 2,), 0, 1 << 20) % (margin + 1)
    tallies = tallies.at[source_of].add(-shifted).at[sink].add(shifted)
    members = jnp.searchsorted(jnp.cumsum(tallies), jnp.arange(rows * top), side="right").astype(jnp.int32)
    listing = members.reshape(top, rows).T
    listing = listing[jax.random.permutation(jax.random.fold_in(own, 1), rows)]
    rotation = jax.random.randint(jax.random.fold_in(own, 2), (rows, 1), 0, top)
    return jnp.take_along_axis(listing, (jnp.arange(top)[None, :] + rotation) % top, axis=1)


def shares(amount, total, reach, slope, full):
    portions = [(1 << 20) // math.isqrt(rank ** slope) + 1 for rank in range(1, amount + 1)]
    largest = reach if full else min(reach, max(-(-total // amount), total * portions[0] // sum(portions)))
    least = 1 if total - largest >= amount - 1 else 0
    given, spare = [largest] + [least] * (amount - 1), total - largest - least * (amount - 1)
    while spare > 0:
        free = [i for i in range(1, amount) if given[i] < largest] or [i for i in range(1, amount) if given[i] < reach]
        mass, budget = sum([portions[i] for i in free]), spare
        for i in free:
            addition = min(reach - given[i], max(1, budget * portions[i] // mass), spare)
            given[i] = given[i] + addition
            spare = spare - addition
    return np.array(given)


def bell_draw(rng, extent, scale, limit, pieces=(), kind=jnp.bfloat16):
    loudness = levels(rng, extent, pieces, -0.22, 0.18) if pieces else 1.0
    entries = jax.random.normal(rng, extent, jnp.float32) * scale * loudness
    return jnp.minimum(jnp.maximum(entries, -limit), limit).astype(kind)


def setup_inputs(seed: int = 0) -> dict:
    splits = jax.random.split(jax.random.key(seed), 14)
    tokens = bell_draw(splits[0], (TOKENS, D), 1.0, 6.0, ((0, 16), (1, 8)))
    cotangent = bell_draw(splits[1], (TOKENS, D), 1.0, 6.0, ((0, 16), (1, 8)))
    router_weights = jnp.clip(jnp.exp(math.log(0.3) - 2.7080503 * jax.random.uniform(splits[2], (TOKENS, K), jnp.float32) ** levels(splits[2], (TOKENS, K), ((0, 16),), -0.2, 0.2)), 0.02, 0.3)
    routes_keys = jax.random.split(jax.random.fold_in(splits[3], 1), TOKENS // TOK_DEV)
    routes_turns = jax.random.permutation(jax.random.fold_in(splits[3], 3), TOKENS // TOK_DEV)
    routes = jax.vmap(lambda own, number: assign_block(jax.random.fold_in(splits[3], 2), own, number, TOK_DEV, SLOTS, K, CAP, 2))(routes_keys, routes_turns).reshape((TOKENS, K))
    replica_map = touch_ends(skewed_ids(splits[4], (EXPERTS,), EXPERTS, 2), jax.random.fold_in(splits[4], 3), 0, EXPERTS - 1).astype(jnp.int32)
    gate_primary = bell_draw(splits[5], (EXPERTS, D, FF), D ** -0.5, 0.09375, ((0, 16), (2, 8)))
    up_primary = bell_draw(splits[6], (EXPERTS, D, FF), D ** -0.5, 0.09375, ((0, 16), (2, 8)))
    down_primary = bell_draw(splits[7], (EXPERTS, FF, D), FF ** -0.5, 0.15625, ((0, 16), (2, 8)))
    gate_replica = bell_draw(splits[8], (EXPERTS, D, FF), D ** -0.5, 0.09375, ((0, 16), (2, 8)))
    up_replica = bell_draw(splits[9], (EXPERTS, D, FF), D ** -0.5, 0.09375, ((0, 16), (2, 8)))
    down_replica = bell_draw(splits[10], (EXPERTS, FF, D), FF ** -0.5, 0.15625, ((0, 16), (2, 8)))
    moment1 = bell_draw(splits[11], (EXPERTS, FF, D), 1.0, 6.0, ((0, 16), (2, 8)), jnp.float32)
    moment2 = jnp.clip(jnp.exp(math.log(8.0) - 2.7725887 * jax.random.uniform(splits[12], (EXPERTS, FF, D), jnp.float32) ** levels(splits[12], (EXPERTS, FF, D), ((0, 16), (2, 8)), -0.2, 0.2)), 0.5, 8.0)
    return dict(tokens=tokens, cotangent=cotangent, router_weights=router_weights, routes=routes, replica_map=replica_map, gate_primary=gate_primary, up_primary=up_primary, down_primary=down_primary, gate_replica=gate_replica, up_replica=up_replica, down_replica=down_replica, moment1=moment1, moment2=moment2)


beta_one = 0.9
beta_two = 0.95
learn_rate = 0.001
weight_decay = 0.1
epsilon = 1e-08
correct_one = 1.0 - 0.9 ** 10
correct_two = 1.0 - 0.95 ** 10

def slot_targets(routes):
    blocks = routes.reshape(N_EP, TOK_DEV * K)
    slot_ids = jnp.arange(2 * N_EP, dtype=jnp.int32)

    def block_positions(slot_row):
        onehot = (slot_row[:, None] == slot_ids[None, :]).astype(jnp.int32)
        before = jnp.cumsum(onehot, axis=0) - onehot
        return lax.optimization_barrier(jnp.sum(before * onehot, axis=1))
    position = jax.vmap(block_positions)(blocks)
    source = jnp.arange(N_EP, dtype=jnp.int32)[:, None]
    return (blocks * (N_EP * CAP) + source * CAP + position).reshape(-1).astype(jnp.int32)

def reference(tokens, cotangent, router_weights, routes, replica_map, gate_primary, up_primary, down_primary, gate_replica, up_replica, down_replica, moment1, moment2):
    slot_count = 2 * N_EP
    slot_rows = N_EP * CAP
    target = slot_targets(routes)
    weights = router_weights.reshape(-1)
    token_rows = jnp.repeat(tokens, K, axis=0)
    scaled_rows = (weights[:, None] * jnp.repeat(cotangent, K, axis=0).astype(jnp.float32)).astype(jnp.bfloat16)
    token_buffer = jnp.zeros((slot_count * slot_rows, D), jnp.bfloat16).at[target].set(token_rows).reshape(slot_count, slot_rows, D)
    scaled_buffer = jnp.zeros((slot_count * slot_rows, D), jnp.bfloat16).at[target].set(scaled_rows).reshape(slot_count, slot_rows, D)
    gate_all = jnp.stack([gate_primary, gate_replica], 1).reshape(slot_count, D, FF)
    up_all = jnp.stack([up_primary, up_replica], 1).reshape(slot_count, D, FF)
    down_all = jnp.stack([down_primary, down_replica], 1).reshape(slot_count, FF, D)
    owner_ids = jnp.stack([jnp.arange(N_EP, dtype=jnp.int32), replica_map], 1).reshape(-1)

    def slot_step(gradients, inputs):
        slot_tokens, slot_scaled, gate_cols, up_cols, down_rows, owner_id = inputs
        gate_sum = jnp.dot(slot_tokens, gate_cols, preferred_element_type=jnp.float32)
        up_sum = jnp.dot(slot_tokens, up_cols, preferred_element_type=jnp.float32)
        hidden = (jax.nn.silu(gate_sum) * up_sum).astype(jnp.bfloat16)
        outputs = jnp.dot(hidden, down_rows, preferred_element_type=jnp.float32).astype(jnp.bfloat16)
        partial_value = jnp.dot(hidden.T, slot_scaled, preferred_element_type=jnp.float32)
        gradients = gradients.at[owner_id].add(partial_value)
        return (gradients, outputs)
    gradients, outputs = lax.scan(slot_step, jnp.zeros((N_EP, FF, D), jnp.float32), (token_buffer, scaled_buffer, gate_all, up_all, down_all, owner_ids))
    picked = outputs.reshape(slot_count * slot_rows, D)[target].astype(jnp.float32)
    layer_output = lax.optimization_barrier(jnp.sum(weights.reshape(TOKENS, K, 1) * picked.reshape(TOKENS, K, D), axis=1)).astype(jnp.bfloat16)
    moment1_new = beta_one * moment1 + (1.0 - beta_one) * gradients
    moment2_new = beta_two * moment2 + (1.0 - beta_two) * gradients * gradients
    update = moment1_new / correct_one / (jnp.sqrt(moment2_new / correct_two) + epsilon)
    down_new = (down_primary.astype(jnp.float32) * (1.0 - learn_rate * weight_decay) - learn_rate * update).astype(jnp.bfloat16)
    replica_down_new = down_primary[replica_map]
    return (layer_output, down_new, moment1_new, moment2_new, replica_down_new)
```

```python
import functools

import jax
import jax.numpy as jnp
from jax import lax
from jax.experimental import pallas as pl
from jax.experimental.pallas import tpu as pltpu
from jax.sharding import PartitionSpec as P

beta_one = 0.9
beta_two = 0.95
learn_rate = 0.001
weight_decay = 0.1
epsilon = 1e-08
correct_one = 1.0 - 0.9**10
correct_two = 1.0 - 0.95**10

BF16 = jnp.bfloat16
F32 = jnp.float32
NT = (((1,), (1,)), ((), ()))
NN = (((1,), (0,)), ((), ()))
VMEM_LIMIT = 56 * 1024 * 1024


def ring_perms(axis):
    def build(move):
        if axis == "rep":
            return [(p * 4 + r, move(p, r)[0] * 4 + move(p, r)[1]) for p in range(2) for r in range(4)]
        return [
            ((p * 4 + r) * 2 + c, (move(p, r)[0] * 4 + move(p, r)[1]) * 2 + c)
            for p in range(2)
            for r in range(4)
            for c in range(2)
        ]

    return (
        build(lambda p, r: (p, (r + 1) % 4)),
        build(lambda p, r: (p, (r + 3) % 4)),
        build(lambda p, r: (1 - p, r)),
    )


def offset_perm(dp, dr):
    return [
        ((p * 4 + r) * 2 + c, ((p ^ dp) * 4 + (r + dr) % 4) * 2 + c)
        for p in range(2)
        for r in range(4)
        for c in range(2)
    ]


CORE_PERM = [(i, i ^ 1) for i in range(16)]


def swap_core(x):
    return lax.ppermute(x, "ep", CORE_PERM)


def gather_pieces(x, axis, split_dim):
    up, down, pair = ring_perms(axis)
    move = lambda value, perm: lax.ppermute(value, axis, perm)
    half = x.shape[split_dim] // 2
    below = move(x, up)
    above = move(x, down)
    across = move(x, pair)
    far_low = move(lax.slice_in_dim(below, 0, half, axis=split_dim), up)
    far_high = move(lax.slice_in_dim(above, half, 2 * half, axis=split_dim), down)
    across_below = move(across, up)
    across_above = move(across, down)
    across_far_low = move(far_low, pair)
    across_far_high = move(far_high, pair)
    return [
        (x, 0, 0, None),
        (below, 0, 3, None),
        (above, 0, 1, None),
        (across, 1, 0, None),
        (far_low, 0, 2, 0),
        (far_high, 0, 2, 1),
        (across_below, 1, 3, None),
        (across_above, 1, 1, None),
        (across_far_low, 1, 2, 0),
        (across_far_high, 1, 2, 1),
    ]


ORDER = [(0, 0), (0, 3), (0, 1), (1, 0), (0, 2), (1, 3), (1, 1), (1, 2)]


def whole_blocks(pieces, split_dim):
    found = {}
    for array, dp, dr, half in pieces:
        found.setdefault((dp, dr), []).append(array)
    return [
        found[key][0] if len(found[key]) == 1 else jnp.concatenate(found[key], axis=split_dim)
        for key in ORDER
    ]


def piece_places(pieces, unit):
    return [(ORDER.index((dp, dr)), 0 if half is None else half * unit // 2) for _, dp, dr, half in pieces]


def hidden_kernel(places, share, table, w_ref, *refs):
    x_refs, o_ref = refs[:-1], refs[-1]
    total = None
    for (place, inner), x_ref in zip(places, x_refs):
        start = pl.multiple_of(table[place] * share + inner, 256)
        part = lax.dot_general(
            w_ref[:, pl.ds(start, x_ref.shape[1])], x_ref[...], NT, preferred_element_type=F32
        )
        total = part if total is None else total + part
    units = o_ref.shape[0] // 2
    for slot in range(2):
        gate = total[2 * slot * units : (2 * slot + 1) * units]
        up = total[(2 * slot + 1) * units : (2 * slot + 2) * units]
        o_ref[slot * units : (slot + 1) * units, :] = (jax.nn.silu(gate) * up).astype(BF16)


def hidden_call(weights_t, pieces, table):
    count = pieces[0][0].shape[0]
    share = pieces[0][0].shape[1]
    rows, width = weights_t.shape
    tile = 256
    arrays = [piece[0] for piece in pieces]
    return pl.pallas_call(
        functools.partial(hidden_kernel, piece_places(pieces, share), share),
        grid_spec=pltpu.PrefetchScalarGridSpec(
            num_scalar_prefetch=1,
            grid=(count // tile,),
            in_specs=[pl.BlockSpec((rows, width), lambda i, t: (0, 0))]
            + [pl.BlockSpec((tile, a.shape[1]), lambda i, t: (i, 0)) for a in arrays],
            out_specs=pl.BlockSpec((rows // 2, tile), lambda i, t: (0, i)),
        ),
        out_shape=jax.ShapeDtypeStruct((rows // 2, count), BF16),
        compiler_params=pltpu.CompilerParams(vmem_limit_bytes=VMEM_LIMIT),
        cost_estimate=pl.CostEstimate(
            flops=2 * rows * width * count,
            bytes_accessed=2 * (rows * width + count * width),
            transcendentals=rows * count // 4,
        ),
        name="hidden",
    )(table, weights_t, *arrays)


def compact_kernel(pos_ref, a_ref, b_ref, o_ref):
    tile = o_ref.shape[1]
    half = a_ref.shape[1]
    row = lax.broadcasted_iota(jnp.int32, (tile, half), 0) + pl.program_id(0) * tile
    first = (pos_ref[:, :half] == row).astype(F32).astype(BF16)
    second = (pos_ref[:, half:] == row).astype(F32).astype(BF16)
    o_ref[...] = (
        lax.dot_general(a_ref[...], first, NT, preferred_element_type=F32)
        + lax.dot_general(b_ref[...], second, NT, preferred_element_type=F32)
    ).astype(BF16)


def compact_call(own, other, pos_row, slot, rows):
    units, half = own.shape[0] // 2, own.shape[1]
    tile = 256
    return pl.pallas_call(
        compact_kernel,
        grid=(rows // tile,),
        in_specs=[
            pl.BlockSpec((1, 2 * half), lambda i: (0, 0)),
            pl.BlockSpec((units, half), lambda i: (slot, 0)),
            pl.BlockSpec((units, half), lambda i: (slot, 0)),
        ],
        out_specs=pl.BlockSpec((units, tile), lambda i: (0, i)),
        out_shape=jax.ShapeDtypeStruct((units, rows), BF16),
        compiler_params=pltpu.CompilerParams(vmem_limit_bytes=VMEM_LIMIT),
        cost_estimate=pl.CostEstimate(
            flops=4 * units * half * rows, bytes_accessed=4 * units * (2 * half + rows), transcendentals=0
        ),
        name="compact",
    )(pos_row, own, other)


def scaled_kernel(pos_ref, w_ref, a_ref, b_ref, o_ref, scaled):
    half = a_ref.shape[0]
    tile = o_ref.shape[0]

    @pl.when(pl.program_id(0) == 0)
    def _():
        scaled[:half, :] = (w_ref[:half, :] * a_ref[...].astype(F32)).astype(BF16)
        scaled[half:, :] = (w_ref[half:, :] * b_ref[...].astype(F32)).astype(BF16)

    row = lax.broadcasted_iota(jnp.int32, (tile, 2 * half), 0) + pl.program_id(0) * tile
    chosen = (pos_ref[...] == row).astype(F32).astype(BF16)
    o_ref[...] = jnp.dot(chosen, scaled[...], preferred_element_type=F32).astype(BF16)


def scaled_call(own, other, pos_row, w_col, rows):
    half, share = own.shape
    tile = 256
    return pl.pallas_call(
        scaled_kernel,
        grid=(rows // tile,),
        in_specs=[
            pl.BlockSpec((1, 2 * half), lambda i: (0, 0)),
            pl.BlockSpec((2 * half, 1), lambda i: (0, 0)),
            pl.BlockSpec((half, share), lambda i: (0, 0)),
            pl.BlockSpec((half, share), lambda i: (0, 0)),
        ],
        out_specs=pl.BlockSpec((tile, share), lambda i: (i, 0)),
        out_shape=jax.ShapeDtypeStruct((rows, share), BF16),
        scratch_shapes=[pltpu.VMEM((2 * half, share), BF16)],
        compiler_params=pltpu.CompilerParams(vmem_limit_bytes=VMEM_LIMIT),
        cost_estimate=pl.CostEstimate(
            flops=4 * half * share * rows, bytes_accessed=2 * share * (2 * half + rows), transcendentals=0
        ),
        name="scaled",
    )(pos_row, w_col, own, other)


def piece_copies(places, units, table, refs, hidden, sems):
    copies = []
    for number, ((place, inner), ref) in enumerate(zip(places, refs)):
        start = pl.multiple_of(table[place] * units, units)
        target = hidden.at[pl.ds(start, units), pl.ds(inner, ref.shape[1])]
        copies.append(pltpu.make_async_copy(ref, target, sems.at[number]))
    return copies


def load_hidden(places, units, table, refs, hidden, sems):
    @pl.when(pl.program_id(0) == 0)
    def _():
        copies = piece_copies(places, units, table, refs, hidden, sems)
        for copy in copies:
            copy.start()
        for copy in copies:
            copy.wait()


def replica_gradient_kernel(places, units, table, s_ref, *refs):
    count = len(places)
    pieces, (o_ref, hidden, sems) = refs[:count], refs[count:]
    load_hidden(places, units, table, pieces, hidden, sems)
    tile = o_ref.shape[0]
    start = pl.multiple_of(pl.program_id(0) * tile, tile)
    o_ref[...] = jnp.dot(
        hidden[pl.ds(start, tile), :], s_ref[...], preferred_element_type=F32
    ).astype(BF16)


def replica_gradient_call(pieces, scaled, table):
    units, rows = pieces[0][0].shape
    share = scaled.shape[1]
    total = 8 * units
    tile = 256
    return pl.pallas_call(
        functools.partial(replica_gradient_kernel, piece_places(pieces, rows), units),
        grid_spec=pltpu.PrefetchScalarGridSpec(
            num_scalar_prefetch=1,
            grid=(total // tile,),
            in_specs=[pl.BlockSpec((rows, share), lambda i, t: (0, 0))]
            + [pl.BlockSpec(memory_space=pl.ANY)] * len(pieces),
            out_specs=pl.BlockSpec((tile, share), lambda i, t: (i, 0)),
            scratch_shapes=[
                pltpu.VMEM((total, rows), BF16),
                pltpu.SemaphoreType.DMA((len(pieces),)),
            ],
        ),
        out_shape=jax.ShapeDtypeStruct((total, share), BF16),
        compiler_params=pltpu.CompilerParams(vmem_limit_bytes=VMEM_LIMIT),
        cost_estimate=pl.CostEstimate(
            flops=2 * total * rows * share,
            bytes_accessed=2 * (total * rows + rows * share + total * share),
            transcendentals=0,
        ),
        name="replica_gradient",
    )(table, scaled, *[piece[0] for piece in pieces])


def update_kernel(places, units, table, s_ref, total_ref, one_ref, two_ref, down_ref, *refs):
    count = len(places)
    pieces = refs[:count]
    down_out, one_out, two_out, hidden, sems = refs[count:]
    load_hidden(places, units, table, pieces, hidden, sems)
    tile = down_out.shape[0]
    start = pl.multiple_of(pl.program_id(0) * tile, tile)
    gradient = jnp.dot(
        hidden[pl.ds(start, tile), :], s_ref[...], preferred_element_type=F32
    ) + total_ref[...].astype(F32)
    one = beta_one * one_ref[...] + (1.0 - beta_one) * gradient
    two = beta_two * two_ref[...] + (1.0 - beta_two) * gradient * gradient
    one_out[...] = one
    two_out[...] = two
    update = one / correct_one / (jnp.sqrt(two / correct_two) + epsilon)
    down_out[...] = (
        down_ref[...].astype(F32) * (1.0 - learn_rate * weight_decay) - learn_rate * update
    ).astype(BF16)


def update_call(pieces, scaled, table, total_gradient, moment1, moment2, down):
    units, rows = pieces[0][0].shape
    share = scaled.shape[1]
    total = 8 * units
    tile = 256
    block = pl.BlockSpec((tile, share), lambda i, t: (i, 0))
    return pl.pallas_call(
        functools.partial(update_kernel, piece_places(pieces, rows), units),
        grid_spec=pltpu.PrefetchScalarGridSpec(
            num_scalar_prefetch=1,
            grid=(total // tile,),
            in_specs=[pl.BlockSpec((rows, share), lambda i, t: (0, 0))]
            + [block] * 4
            + [pl.BlockSpec(memory_space=pl.ANY)] * len(pieces),
            out_specs=[block] * 3,
            scratch_shapes=[
                pltpu.VMEM((total, rows), BF16),
                pltpu.SemaphoreType.DMA((len(pieces),)),
            ],
        ),
        out_shape=[
            jax.ShapeDtypeStruct((total, share), BF16),
            jax.ShapeDtypeStruct((total, share), F32),
            jax.ShapeDtypeStruct((total, share), F32),
        ],
        compiler_params=pltpu.CompilerParams(vmem_limit_bytes=VMEM_LIMIT),
        cost_estimate=pl.CostEstimate(
            flops=2 * total * rows * share,
            bytes_accessed=2 * total * rows + 22 * total * share,
            transcendentals=total * share,
        ),
        name="update",
    )(table, scaled, total_gradient, moment1, moment2, down, *[piece[0] for piece in pieces])


def output_kernel(places, units, table, down_ref, pos_ref, w_ref, prior_ref, *refs):
    count = len(places)
    pieces = refs[:count]
    o_ref, hidden, outputs, sems = refs[count:]
    load_hidden(places, units, table, pieces, hidden, sems)
    rows = hidden.shape[1]

    @pl.when(pl.program_id(0) == 0)
    def _():
        @pl.loop(0, rows // 256)
        def _(step):
            columns = pl.ds(pl.multiple_of(step * 256, 256), 256)
            outputs[:, columns] = jnp.dot(
                down_ref[...], hidden[:, columns], preferred_element_type=F32
            ).astype(BF16)

    tile = o_ref.shape[0]
    column = lax.broadcasted_iota(jnp.int32, (tile, rows), 1)
    chosen = (pos_ref[...] == column).astype(F32).astype(BF16)
    picked = lax.dot_general(chosen, outputs[...], NT, preferred_element_type=F32)
    o_ref[...] = (prior_ref[...] + w_ref[...] * picked).astype(o_ref.dtype)


def output_call(pieces, down_t, table, pos_col, w_col, prior, dtype):
    units, rows = pieces[0][0].shape
    share = down_t.shape[0]
    total = 8 * units
    tokens = pos_col.shape[0]
    tile = 256
    return pl.pallas_call(
        functools.partial(output_kernel, piece_places(pieces, rows), units),
        grid_spec=pltpu.PrefetchScalarGridSpec(
            num_scalar_prefetch=1,
            grid=(tokens // tile,),
            in_specs=[
                pl.BlockSpec((share, total), lambda i, t: (0, 0)),
                pl.BlockSpec((tile, 1), lambda i, t: (i, 0)),
                pl.BlockSpec((tile, 1), lambda i, t: (i, 0)),
                pl.BlockSpec((tile, share), lambda i, t: (i, 0)),
            ]
            + [pl.BlockSpec(memory_space=pl.ANY)] * len(pieces),
            out_specs=pl.BlockSpec((tile, share), lambda i, t: (i, 0)),
            scratch_shapes=[
                pltpu.VMEM((total, rows), BF16),
                pltpu.VMEM((share, rows), BF16),
                pltpu.SemaphoreType.DMA((len(pieces),)),
            ],
        ),
        out_shape=jax.ShapeDtypeStruct((tokens, share), dtype),
        compiler_params=pltpu.CompilerParams(vmem_limit_bytes=VMEM_LIMIT),
        cost_estimate=pl.CostEstimate(
            flops=2 * total * rows * share + 2 * tokens * rows * share,
            bytes_accessed=2 * (total * rows + total * share) + 6 * tokens * share,
            transcendentals=0,
        ),
        name="output",
    )(table, down_t, pos_col, w_col, prior, *[piece[0] for piece in pieces])


def per_device(
    tokens,
    cotangent,
    router_weights,
    routes,
    replica_map,
    gate_primary,
    up_primary,
    down_primary,
    gate_replica,
    up_replica,
    down_replica,
    moment1,
    moment2,
):
    groups = lax.axis_size("ep")
    count, top = routes.shape
    hidden_units, share = down_primary.shape[1:]
    rows = groups * (3 * count * top // (2 * groups))
    ep = lax.axis_index("ep")
    rep = lax.axis_index("rep")

    token_blocks = whole_blocks(gather_pieces(tokens, "ep", 0), 0)
    token_table = jnp.concatenate(token_blocks, axis=0)
    token_pieces = gather_pieces(token_table, "rep", 1)
    other_pieces = [(swap_core(array), dp, dr, half) for array, dp, dr, half in token_pieces]
    cot_own = jnp.concatenate(whole_blocks(gather_pieces(cotangent, "ep", 0), 0), axis=0)
    cot_other = swap_core(cot_own)

    slot_ids = jnp.arange(2 * groups, dtype=jnp.int32)
    dense = jnp.sum(
        jnp.where(routes[None] == slot_ids[:, None, None], router_weights[None], 0.0), axis=2
    ).reshape(groups, 2, count)
    served = lax.all_to_all(dense, "ep", split_axis=0, concat_axis=0, tiled=True)
    pair, ring, core = ep // 8, (ep // 2) % 4, ep % 2
    order = jnp.stack(
        [((pair ^ dp) * 4 + (ring + dr) % 4) * 2 + c for c in (core, 1 - core) for dp, dr in ORDER]
    )
    served = jnp.transpose(served[order], (1, 0, 2))
    hit = (served != 0.0).astype(F32)
    earlier = jnp.triu(jnp.ones((count, count), F32), 1)
    blocks_before = jnp.triu(jnp.ones((groups, groups), F32), 1)
    inside = jnp.einsum("lbt,tu->lbu", hit, earlier, precision=lax.Precision.HIGHEST)
    before = jnp.einsum(
        "lb,bc->lc", jnp.sum(hit, axis=2), blocks_before, precision=lax.Precision.HIGHEST
    )
    pos = jnp.where(hit > 0, (inside + before[:, :, None]).astype(jnp.int32), -1)
    pos = pos.reshape(2, groups * count)
    weight = served.reshape(2, groups * count)
    pos_rows = [pos[slot : slot + 1] for slot in range(2)]
    pos_cols = [pos[slot][:, None] for slot in range(2)]
    weight_cols = [weight[slot][:, None] for slot in range(2)]

    rep_pair, rep_ring = rep // 4, rep % 4
    table = jnp.stack([(rep_pair ^ dp) * 4 + (rep_ring + dr) % 4 for dp, dr in ORDER]).astype(jnp.int32)

    weights_t = jnp.concatenate(
        [gate_primary[0].T, up_primary[0].T, gate_replica[0].T, up_replica[0].T], axis=0
    )
    down_t = [down_primary[0].T, down_replica[0].T]

    shares = down_primary[0].reshape(groups, hidden_units // groups, share)
    spread_weights = lax.all_to_all(shares, "ep", split_axis=0, concat_axis=0, tiled=True)
    chosen = jnp.take(spread_weights, replica_map, axis=0)
    refreshed = lax.all_to_all(chosen, "ep", split_axis=0, concat_axis=0, tiled=True).reshape(
        1, hidden_units, share
    )

    hidden_own = hidden_call(weights_t, token_pieces, table)
    hidden_other = hidden_call(weights_t, other_pieces, table)
    scaled = [
        scaled_call(cot_own, cot_other, pos_rows[slot], weight_cols[slot], rows) for slot in range(2)
    ]
    replica_pieces = gather_pieces(
        compact_call(hidden_own, hidden_other, pos_rows[1], 1, rows), "rep", 1
    )
    primary_pieces = gather_pieces(
        compact_call(hidden_own, hidden_other, pos_rows[0], 0, rows), "rep", 1
    )

    replica_gradient = replica_gradient_call(replica_pieces, scaled[1], table)
    spread = lax.all_to_all(
        replica_gradient.reshape(groups, hidden_units // groups, share),
        "ep",
        split_axis=0,
        concat_axis=0,
        tiled=True,
    )
    owners = (replica_map[None, :] == jnp.arange(groups, dtype=jnp.int32)[:, None]).astype(BF16)
    summed = jnp.einsum("pj,jfd->pfd", owners, spread, preferred_element_type=F32)
    replica_total = lax.all_to_all(
        summed.astype(BF16), "ep", split_axis=0, concat_axis=0, tiled=True
    ).reshape(hidden_units, share)

    half_output = output_call(
        replica_pieces,
        down_t[1],
        table,
        pos_cols[1],
        weight_cols[1],
        jnp.zeros((groups * count, share), F32),
        F32,
    )
    outputs = output_call(
        primary_pieces, down_t[0], table, pos_cols[0], weight_cols[0], half_output, BF16
    )
    half_count = groups * count // 2
    mine = (
        outputs[:half_count].astype(F32) + swap_core(outputs[half_count:]).astype(F32)
    ).astype(BF16)
    layer = mine[:count].astype(F32)
    for number, (dp, dr) in enumerate(ORDER):
        if number:
            block = mine[number * count : (number + 1) * count]
            layer = layer + lax.ppermute(block, "ep", offset_perm(dp, dr)).astype(F32)

    down_new, moment1_new, moment2_new = update_call(
        primary_pieces,
        scaled[0],
        table,
        replica_total,
        moment1[0],
        moment2[0],
        down_primary[0],
    )
    return (layer.astype(BF16), down_new[None], moment1_new[None], moment2_new[None], refreshed)


def solution(mesh):
    return jax.shard_map(
        per_device,
        mesh=mesh,
        in_specs=(
            P("ep", "rep"),
            P("ep", "rep"),
            P("ep", None),
            P("ep", None),
            P(),
            P("ep", None, "rep"),
            P("ep", None, "rep"),
            P("ep", None, "rep"),
            P("ep", None, "rep"),
            P("ep", None, "rep"),
            P("ep", None, "rep"),
            P("ep", None, "rep"),
            P("ep", None, "rep"),
        ),
        out_specs=(
            P("ep", "rep"),
            P("ep", None, "rep"),
            P("ep", None, "rep"),
            P("ep", None, "rep"),
            P("ep", None, "rep"),
        ),
        check_vma=False,
    )
```

```python
import functools

import jax
import jax.numpy as jnp
from jax import lax
from jax.experimental import pallas as pl
from jax.experimental.pallas import tpu as pltpu
from jax.sharding import PartitionSpec as P

beta_one = 0.9
beta_two = 0.95
learn_rate = 0.001
weight_decay = 0.1
epsilon = 1e-08
correct_one = 1.0 - 0.9**10
correct_two = 1.0 - 0.95**10

BF16 = jnp.bfloat16
F32 = jnp.float32
NT = (((1,), (1,)), ((), ()))
NN = (((1,), (0,)), ((), ()))
VMEM_LIMIT = 56 * 1024 * 1024


ORDER = [(0, 0), (0, 3), (0, 1), (1, 0), (0, 2), (1, 3), (1, 1), (1, 2)]
PAIRS, RING = 2, 4


def shifted(pair, ring, dp, dr):
    return pair ^ dp, (ring - dr) % RING


def ep_perm(dp, dr):
    perm = []
    for i in range(16):
        pair, ring = shifted(i // 8, (i // 2) % RING, dp, dr)
        perm.append((i, (pair * RING + ring) * 2 + i % 2))
    return perm


def rep_perm(dp, dr):
    perm = []
    for i in range(8):
        pair, ring = shifted(i // RING, i % RING, dp, dr)
        perm.append((i, pair * RING + ring))
    return perm


def joint_perm(stage, dp, dr):
    perm = []
    ep_moves, rep_moves = dict(ep_perm(dp, dr)), dict(rep_perm(dp, dr))
    for i in range(128):
        ep, rep = i // 8, i % 8
        if ep % 2 == stage:
            ep = ep_moves[ep]
        else:
            rep = rep_moves[rep]
        perm.append((i, ep * 8 + rep))
    return perm


def move_rep(x, dp, dr):
    return lax.ppermute(x, "rep", rep_perm(dp, dr))


def move_joint(stage, x, dp, dr):
    return lax.ppermute(x, ("ep", "rep"), joint_perm(stage, dp, dr))


def swap_core(x):
    return lax.ppermute(x, "ep", [(i, i ^ 1) for i in range(16)])


def gather_pieces(x, move, split_dim, far_by_pair):
    half = x.shape[split_dim] // 2
    low = lambda value: lax.slice_in_dim(value, 0, half, axis=split_dim)
    high = lambda value: lax.slice_in_dim(value, half, 2 * half, axis=split_dim)
    across = move(x, 1, 0)
    below = move(x, 0, 3)
    above = move(x, 0, 1)
    far_low = move(low(below), 0, 3)
    far_high = move(high(above), 0, 1)
    across_below = move(across, 0, 3)
    across_above = move(across, 0, 1)
    if far_by_pair:
        across_far_low = move(far_low, 1, 0)
        across_far_high = move(far_high, 1, 0)
    else:
        across_far_low = move(low(across_below), 0, 3)
        across_far_high = move(high(across_above), 0, 1)
    return [
        (x, 0, None),
        (below, 1, None),
        (above, 2, None),
        (across, 3, None),
        (far_low, 4, 0),
        (far_high, 4, 1),
        (across_below, 5, None),
        (across_above, 6, None),
        (across_far_low, 7, 0),
        (across_far_high, 7, 1),
    ]


def one_hot(mask):
    return jnp.where(mask, 1.0, 0.0).astype(BF16)


def hidden_kernel(marks, column, table, pos_ref, w_ref, *refs):
    count = len(marks)
    pieces = refs[:count]
    o_ref, x_ref, total_ref, sems = refs[count:]
    step = pl.program_id(0)
    blocks, parts, depth, share = x_ref.shape
    tiles = blocks // 2

    @pl.when(step == 0)
    def _():
        @pl.when(table[parts] == 0)
        def _():
            for tile in range(tiles):
                for (place, half), piece in zip(marks, pieces):
                    begin = 2 * tile - (0 if half is None else half * blocks // 2)
                    if 0 <= begin < piece.shape[0]:
                        pltpu.make_async_copy(
                            piece.at[pl.ds(begin, 2)],
                            x_ref.at[pl.ds(2 * tile, 2), place],
                            sems.at[tile],
                        ).start()

        @pl.when(table[parts] != 0)
        def _():
            for (place, half), piece in zip(marks, pieces):
                begin = 0 if half is None else half * parts // 2
                pltpu.make_async_copy(
                    piece, x_ref.at[place, pl.ds(begin, piece.shape[0])], sems.at[place // 2]
                ).start()

    ready = x_ref.at[pl.ds(2 * step, 2)]
    pltpu.make_async_copy(ready, ready, sems.at[step]).wait()
    sums = None
    for place in range(parts):
        start = pl.multiple_of(table[place] * share, share)
        tokens = x_ref[pl.ds(2 * step, 2), place].reshape(2 * depth, share)
        part = lax.dot_general(w_ref[:, pl.ds(start, share)], tokens, NT, preferred_element_type=F32)
        sums = part if sums is None else sums + part
    units = o_ref.shape[0]
    hidden = (jax.nn.silu(sums[:units]) * sums[units:]).astype(BF16)
    target = lax.broadcasted_iota(jnp.int32, (2 * depth, o_ref.shape[1]), 1)
    chosen = one_hot(pos_ref[:, column : column + 1] == target)
    picked = jnp.dot(hidden, chosen, preferred_element_type=F32)

    @pl.when(step == 0)
    def _():
        total_ref[...] = picked

    @pl.when(step > 0)
    def _():
        total_ref[...] += picked

    @pl.when(step == pl.num_programs(0) - 1)
    def _():
        o_ref[...] = total_ref[...].astype(BF16)


def hidden_call(weights_t, pieces, table, pos_cols, slot, parity, rows):
    blocks, depth, share = pieces[0][0].shape
    units, width = weights_t.shape[0] // 4, weights_t.shape[1]
    parts = width // share
    tile = 2 * depth
    return pl.pallas_call(
        functools.partial(hidden_kernel, [piece[1:] for piece in pieces], slot * 2 + parity),
        grid_spec=pltpu.PrefetchScalarGridSpec(
            num_scalar_prefetch=1,
            grid=(blocks // 2,),
            in_specs=[
                pl.BlockSpec((tile, pos_cols.shape[1]), lambda i, t: (i, 0)),
                pl.BlockSpec((2 * units, width), lambda i, t: (slot, 0)),
            ]
            + [pl.BlockSpec(memory_space=pl.ANY)] * len(pieces),
            out_specs=pl.BlockSpec((units, rows), lambda i, t: (0, 0)),
            scratch_shapes=[
                pltpu.VMEM((blocks, parts, depth, share), BF16),
                pltpu.VMEM((units, rows), F32),
                pltpu.SemaphoreType.DMA((blocks // 2,)),
            ],
        ),
        out_shape=jax.ShapeDtypeStruct((units, rows), BF16),
        compiler_params=pltpu.CompilerParams(vmem_limit_bytes=VMEM_LIMIT),
        cost_estimate=pl.CostEstimate(
            flops=4 * units * width * blocks * depth,
            bytes_accessed=2 * (2 * units * width + blocks * depth * width),
            transcendentals=units * blocks * depth,
        ),
        name="hidden",
    )(table, pos_cols, weights_t, *[piece[0] for piece in pieces])


def scaled_kernel(column, pos_ref, w_ref, c_ref, o_ref):
    scaled = (w_ref[:, column : column + 1] * c_ref[...].astype(F32)).astype(BF16)
    rows = o_ref.shape[0]
    row = lax.broadcasted_iota(jnp.int32, (rows, c_ref.shape[0]), 0)
    chosen = one_hot(pos_ref[column : column + 1, :] == row)
    o_ref[...] = jnp.dot(chosen, scaled, preferred_element_type=F32).astype(BF16)


def scaled_call(cotangents, pos_rows, weight_cols, slot, parity, rows):
    count, share = cotangents.shape
    return pl.pallas_call(
        functools.partial(scaled_kernel, slot * 2 + parity),
        out_shape=jax.ShapeDtypeStruct((rows, share), BF16),
        compiler_params=pltpu.CompilerParams(vmem_limit_bytes=VMEM_LIMIT),
        cost_estimate=pl.CostEstimate(
            flops=2 * count * share * rows,
            bytes_accessed=2 * share * (count + rows),
            transcendentals=0,
        ),
        name="scaled",
    )(pos_rows, weight_cols, cotangents)


def load_hidden(marks, units, table, refs, hidden, sems):
    @pl.when(pl.program_id(0) == 0)
    def _():
        copies = []
        for number, ((place, half), ref) in enumerate(zip(marks, refs)):
            start = pl.multiple_of(table[place] * units, units)
            begin = 0 if half is None else half * ref.shape[1]
            target = hidden.at[pl.ds(start, units), pl.ds(begin, ref.shape[1])]
            copies.append(pltpu.make_async_copy(ref, target, sems.at[number]))
        for copy in copies:
            copy.start()
        for copy in copies:
            copy.wait()


def gradient_tile(hidden, a_ref, b_ref, tile):
    start = pl.multiple_of(pl.program_id(0) * tile, tile)
    half = a_ref.shape[0]
    return jnp.dot(
        hidden[pl.ds(start, tile), :half], a_ref[...], preferred_element_type=F32
    ) + jnp.dot(hidden[pl.ds(start, tile), half:], b_ref[...], preferred_element_type=F32)


def replica_gradient_kernel(marks, units, table, a_ref, b_ref, *refs):
    count = len(marks)
    pieces, (o_ref, hidden, sems) = refs[:count], refs[count:]
    load_hidden(marks, units, table, pieces, hidden, sems)
    o_ref[...] = gradient_tile(hidden, a_ref, b_ref, o_ref.shape[0]).astype(BF16)


def replica_gradient_call(pieces, scaled, table):
    units, rows = pieces[0][0].shape
    half, share = scaled[0].shape
    total = 8 * units
    tile = 512
    return pl.pallas_call(
        functools.partial(replica_gradient_kernel, [piece[1:] for piece in pieces], units),
        grid_spec=pltpu.PrefetchScalarGridSpec(
            num_scalar_prefetch=1,
            grid=(total // tile,),
            in_specs=[pl.BlockSpec((half, share), lambda i, t: (0, 0))] * 2
            + [pl.BlockSpec(memory_space=pl.ANY)] * len(pieces),
            out_specs=pl.BlockSpec((tile, share), lambda i, t: (i, 0)),
            scratch_shapes=[
                pltpu.VMEM((total, rows), BF16),
                pltpu.SemaphoreType.DMA((len(pieces),)),
            ],
        ),
        out_shape=jax.ShapeDtypeStruct((total, share), BF16),
        compiler_params=pltpu.CompilerParams(vmem_limit_bytes=VMEM_LIMIT),
        cost_estimate=pl.CostEstimate(
            flops=2 * total * rows * share,
            bytes_accessed=2 * (total * rows + rows * share + total * share),
            transcendentals=0,
        ),
        name="replica_gradient",
    )(table, *scaled, *[piece[0] for piece in pieces])


def update_kernel(marks, units, table, a_ref, b_ref, total_ref, one_ref, two_ref, down_ref, *refs):
    count = len(marks)
    pieces = refs[:count]
    down_out, one_out, two_out, hidden, sems = refs[count:]
    load_hidden(marks, units, table, pieces, hidden, sems)
    gradient = gradient_tile(hidden, a_ref, b_ref, down_out.shape[0]) + total_ref[...].astype(F32)
    one = beta_one * one_ref[...] + (1.0 - beta_one) * gradient
    two = beta_two * two_ref[...] + (1.0 - beta_two) * gradient * gradient
    one_out[...] = one
    two_out[...] = two
    update = (learn_rate / correct_one) * one / (jnp.sqrt(two * (1.0 / correct_two)) + epsilon)
    down_out[...] = (
        down_ref[...].astype(F32) * (1.0 - learn_rate * weight_decay) - update
    ).astype(BF16)


def update_call(pieces, scaled, table, total_gradient, moment1, moment2, down):
    units, rows = pieces[0][0].shape
    half, share = scaled[0].shape
    total = 8 * units
    tile = 256
    block = pl.BlockSpec((tile, share), lambda i, t: (i, 0))
    return pl.pallas_call(
        functools.partial(update_kernel, [piece[1:] for piece in pieces], units),
        grid_spec=pltpu.PrefetchScalarGridSpec(
            num_scalar_prefetch=1,
            grid=(total // tile,),
            in_specs=[pl.BlockSpec((half, share), lambda i, t: (0, 0))] * 2
            + [block] * 4
            + [pl.BlockSpec(memory_space=pl.ANY)] * len(pieces),
            out_specs=[block] * 3,
            scratch_shapes=[
                pltpu.VMEM((total, rows), BF16),
                pltpu.SemaphoreType.DMA((len(pieces),)),
            ],
        ),
        out_shape=[
            jax.ShapeDtypeStruct((total, share), BF16),
            jax.ShapeDtypeStruct((total, share), F32),
            jax.ShapeDtypeStruct((total, share), F32),
        ],
        compiler_params=pltpu.CompilerParams(vmem_limit_bytes=VMEM_LIMIT),
        cost_estimate=pl.CostEstimate(
            flops=2 * total * rows * share,
            bytes_accessed=2 * total * rows + 22 * total * share,
            transcendentals=total * share,
        ),
        name="update",
    )(table, *scaled, total_gradient, moment1, moment2, down, *[piece[0] for piece in pieces])


def output_kernel(marks, parity, column, units, with_prior, table, down_ref, pos_ref, w_ref, *refs):
    if with_prior:
        prior_ref, refs = refs[0], refs[1:]
    count = len(marks)
    pieces = refs[:count]
    o_ref, hidden, outputs, sems = refs[count:]
    rows = hidden.shape[1]
    copies = []
    for number, ((place, half), ref) in enumerate(zip(marks, pieces)):
        start = pl.multiple_of(table[place] * units, units)
        source = ref.at[:, pl.ds(parity * rows, rows)] if half is None else ref
        copies.append(
            pltpu.make_async_copy(source, hidden.at[pl.ds(start, units)], sems.at[number])
        )
    for copy in copies:
        copy.start()
    for copy in copies:
        copy.wait()
    for begin in range(0, rows, 256):
        outputs[:, begin : begin + 256] = jnp.dot(
            down_ref[...], hidden[:, begin : begin + 256], preferred_element_type=F32
        ).astype(BF16)
    tile = 256
    for begin in range(0, o_ref.shape[0], tile):
        window = slice(begin, begin + tile)
        target = lax.broadcasted_iota(jnp.int32, (tile, rows), 1)
        chosen = one_hot(pos_ref[window, column : column + 1] == target)
        picked = lax.dot_general(chosen, outputs[...], NT, preferred_element_type=F32)
        value = w_ref[window, column : column + 1] * picked
        if with_prior:
            value = value + prior_ref[window, :]
        o_ref[window, :] = value.astype(o_ref.dtype)


def output_call(pieces, down_t, table, pos_cols, weight_cols, slot, parity, prior):
    pieces = [piece for piece in pieces if piece[2] in (None, parity)]
    units, both = pieces[0][0].shape
    rows = both // 2
    share, total = down_t.shape
    count = pos_cols.shape[0]
    vmem = pl.BlockSpec(memory_space=pltpu.VMEM)
    extra = [] if prior is None else [prior]
    return pl.pallas_call(
        functools.partial(
            output_kernel,
            [piece[1:] for piece in pieces],
            parity,
            slot * 2 + parity,
            units,
            prior is not None,
        ),
        in_specs=[pl.BlockSpec(memory_space=pltpu.SMEM)]
        + [vmem] * (3 + len(extra))
        + [pl.BlockSpec(memory_space=pl.ANY)] * len(pieces),
        out_specs=vmem,
        scratch_shapes=[
            pltpu.VMEM((total, rows), BF16),
            pltpu.VMEM((share, rows), BF16),
            pltpu.SemaphoreType.DMA((len(pieces),)),
        ],
        out_shape=jax.ShapeDtypeStruct((count, share), F32 if prior is None else BF16),
        compiler_params=pltpu.CompilerParams(vmem_limit_bytes=VMEM_LIMIT),
        cost_estimate=pl.CostEstimate(
            flops=2 * total * rows * share + 2 * count * rows * share,
            bytes_accessed=2 * (total * rows + total * share) + 6 * count * share,
            transcendentals=0,
        ),
        name="output",
    )(table, down_t, pos_cols, weight_cols, *extra, *[piece[0] for piece in pieces])


def after(value, *others):
    return lax.optimization_barrier((value, others))[0]


def per_device(
    tokens,
    cotangent,
    router_weights,
    routes,
    replica_map,
    gate_primary,
    up_primary,
    down_primary,
    gate_replica,
    up_replica,
    down_replica,
    moment1,
    moment2,
):
    groups = lax.axis_size("ep")
    count, top = routes.shape
    hidden_units, share = down_primary.shape[1:]
    half_groups = groups // 2
    rows = half_groups * (3 * count * top // (2 * groups))
    ep = lax.axis_index("ep")
    rep = lax.axis_index("rep")
    pair, ring, core = ep // 8, (ep // 2) % RING, ep % 2
    rep_pair, rep_ring = rep // RING, rep % RING

    first = jnp.stack([tokens if order == (0, 0) else move_joint(0, tokens, *order) for order in ORDER])
    own_pieces = gather_pieces(first, functools.partial(move_joint, 1), 0, False)
    other_pieces = [(swap_core(array), place, half) for array, place, half in own_pieces]
    cot_all = lax.all_gather(cotangent, "ep", axis=0)

    slot_ids = jnp.arange(2 * groups, dtype=jnp.int32)
    dense = jnp.sum(
        jnp.where(routes[None] == slot_ids[:, None, None], router_weights[None], 0.0), axis=2
    ).reshape(groups, 2, count)
    served = lax.all_to_all(dense, "ep", split_axis=0, concat_axis=0, tiled=True)
    order = jnp.stack(
        [((pair ^ dp) * RING + (ring + dr) % RING) * 2 + c for c in (core, 1 - core) for dp, dr in ORDER]
    )
    served = jnp.transpose(served[order].reshape(2, half_groups, 2, count), (2, 0, 1, 3)).reshape(
        4, half_groups, count
    )
    hit = (served != 0.0).astype(F32)
    earlier = jnp.triu(jnp.ones((count, count), F32), 1)
    blocks_before = jnp.triu(jnp.ones((half_groups, half_groups), F32), 1)
    inside = jnp.einsum("lbt,tu->lbu", hit, earlier, precision=lax.Precision.HIGHEST)
    before = jnp.einsum(
        "lb,bc->lc", jnp.sum(hit, axis=2), blocks_before, precision=lax.Precision.HIGHEST
    )
    pos_rows = jnp.where(hit > 0, (inside + before[:, :, None]).astype(jnp.int32), -1)
    pos_rows = pos_rows.reshape(4, half_groups * count)
    pos_cols = pos_rows.T
    weight_cols = served.reshape(4, half_groups * count).T
    cot_halves = cot_all[order].reshape(2, half_groups * count, share)

    places = jnp.stack(
        [(rep_pair ^ dp) * RING + (rep_ring + dr) % RING for dp, dr in ORDER]
    ).astype(jnp.int32)
    own_table = jnp.concatenate([places, core[None].astype(jnp.int32)])
    other_table = jnp.concatenate([places, 1 - core[None].astype(jnp.int32)])

    weights_t = jnp.concatenate(
        [gate_primary[0].T, up_primary[0].T, gate_replica[0].T, up_replica[0].T], axis=0
    )
    down_t = [down_primary[0].T, down_replica[0].T]
    scaled = [
        [
            scaled_call(cot_halves[parity], pos_rows, weight_cols, slot, parity, rows)
            for parity in range(2)
        ]
        for slot in range(2)
    ]
    weights_t, pos_cols, scaled, down_t = lax.optimization_barrier(
        (weights_t, pos_cols, scaled, down_t)
    )

    def slot_hidden(slot, weights):
        return jnp.concatenate(
            [
                hidden_call(weights, own_pieces, own_table, pos_cols, slot, 0, rows),
                hidden_call(weights, other_pieces, other_table, pos_cols, slot, 1, rows),
            ],
            axis=1,
        )

    replica_hidden = slot_hidden(1, weights_t)
    replica_pieces = gather_pieces(replica_hidden, move_rep, 1, True)

    shares = after(
        down_primary[0].reshape(groups, hidden_units // groups, share), replica_pieces[1][0]
    )
    spread_weights = lax.all_to_all(shares, "ep", split_axis=0, concat_axis=0, tiled=True)
    picked = jnp.take(spread_weights, replica_map, axis=0)
    refreshed = lax.all_to_all(picked, "ep", split_axis=0, concat_axis=0, tiled=True).reshape(
        1, hidden_units, share
    )

    primary_hidden = slot_hidden(0, after(weights_t, replica_hidden))
    primary_hidden = after(primary_hidden, replica_pieces[6][0], replica_pieces[7][0])
    primary_pieces = gather_pieces(primary_hidden, move_rep, 1, True)

    replica_gradient = replica_gradient_call(replica_pieces, scaled[1], places)
    spread = lax.all_to_all(
        replica_gradient.reshape(groups, hidden_units // groups, share),
        "ep",
        split_axis=0,
        concat_axis=0,
        tiled=True,
    )
    owners = (replica_map[None, :] == jnp.arange(groups, dtype=jnp.int32)[:, None]).astype(BF16)
    summed = jnp.einsum("pj,jfd->pfd", owners, spread, preferred_element_type=F32)
    replica_total = lax.all_to_all(
        summed.astype(BF16), "ep", split_axis=0, concat_axis=0, tiled=True
    ).reshape(hidden_units, share)

    down_replica_t = after(down_t[1], replica_gradient)
    prior = [
        output_call(replica_pieces, down_replica_t, places, pos_cols, weight_cols, 1, parity, None)
        for parity in range(2)
    ]
    theirs = output_call(primary_pieces, down_t[0], places, pos_cols, weight_cols, 0, 1, prior[1])
    arrived = swap_core(theirs)
    mine = output_call(
        primary_pieces, after(down_t[0], theirs), places, pos_cols, weight_cols, 0, 0, prior[0]
    )
    mine = (mine.astype(F32) + arrived.astype(F32)).astype(BF16).reshape(half_groups, count, share)
    layer = mine[0].astype(F32)
    for number, (dp, dr) in enumerate(ORDER):
        if number:
            layer = layer + lax.ppermute(mine[number], "ep", ep_perm(dp, -dr)).astype(F32)

    down_new, moment1_new, moment2_new = update_call(
        primary_pieces,
        [after(part, mine) for part in scaled[0]],
        places,
        replica_total,
        moment1[0],
        moment2[0],
        down_primary[0],
    )
    return (layer.astype(BF16), down_new[None], moment1_new[None], moment2_new[None], refreshed)


def solution(mesh):
    return jax.shard_map(
        per_device,
        mesh=mesh,
        in_specs=(
            P("ep", "rep"),
            P("ep", "rep"),
            P("ep", None),
            P("ep", None),
            P(),
            P("ep", None, "rep"),
            P("ep", None, "rep"),
            P("ep", None, "rep"),
            P("ep", None, "rep"),
            P("ep", None, "rep"),
            P("ep", None, "rep"),
            P("ep", None, "rep"),
            P("ep", None, "rep"),
        ),
        out_specs=(
            P("ep", "rep"),
            P("ep", None, "rep"),
            P("ep", None, "rep"),
            P("ep", None, "rep"),
            P("ep", None, "rep"),
        ),
        check_vma=False,
    )
```

```python
import functools

import jax
import jax.numpy as jnp
from jax import lax
from jax.experimental import pallas as pl
from jax.experimental.pallas import tpu as pltpu
from jax.sharding import PartitionSpec as P

beta_one = 0.9
beta_two = 0.95
learn_rate = 0.001
weight_decay = 0.1
epsilon = 1e-08
correct_one = 1.0 - 0.9**10
correct_two = 1.0 - 0.95**10

BF16 = jnp.bfloat16
F32 = jnp.float32
NT = (((1,), (1,)), ((), ()))
NN = (((1,), (0,)), ((), ()))
VMEM_LIMIT = 56 * 1024 * 1024


ORDER = [(0, 0), (0, 3), (0, 1), (1, 0), (0, 2), (1, 3), (1, 1), (1, 2)]
RING = 4


def torus_place(i):
    ep, rep = i // 8, i % 8
    return 2 * (rep // 4) + ep // 8, rep % 4, (ep // 2) % 4, ep % 2


def torus_index(x, y, z, core):
    return (((x % 2) * 4 + z % 4) * 2 + core) * 8 + (x // 2) * 4 + y % 4


def torus_perm(axes, offset):
    perm = []
    for i in range(128):
        place = list(torus_place(i))
        axis = "xyz".index(axes[place[3]])
        place[axis] = (place[axis] - offset) % RING
        perm.append((i, torus_index(*place)))
    return perm


def move_torus(x, axes, offset):
    return lax.ppermute(x, ("ep", "rep"), torus_perm(axes, offset))


def move_rep(x, pair_offset, ring_offset):
    perm = []
    for i in range(8):
        pair, ring = (i // RING) ^ pair_offset, (i % RING - ring_offset) % RING
        perm.append((i, pair * RING + ring))
    return lax.ppermute(x, "rep", perm)


def swap_core(x):
    return lax.ppermute(x, "ep", [(i, i ^ 1) for i in range(16)])


def together(*values):
    return lax.optimization_barrier(values)


def after(value, *others):
    return lax.optimization_barrier((value, others))[0]


RINGS = [0, 3, 1, 2]


def gather_ring(x, axes):
    found = together(x, *[move_torus(x, axes, offset) for offset in RINGS[1:]])
    return jnp.concatenate(found, axis=0)


def one_hot(mask):
    return jnp.where(mask, 1.0, 0.0).astype(BF16)


def hidden_kernel(column, block_table, part_table, pos_ref, w_ref, *refs):
    pieces = refs[:-4]
    o_ref, x_ref, total_ref, sems = refs[-4:]
    step = pl.program_id(0)
    blocks, depth, width = x_ref.shape

    @pl.when(step == 0)
    def _():
        number = 0
        for piece in pieces:
            share = piece.shape[2]
            for index in range(piece.shape[0]):
                block = block_table[number]
                start = pl.multiple_of(part_table[number] * share, share)
                pltpu.make_async_copy(
                    piece.at[index], x_ref.at[block, :, pl.ds(start, share)], sems.at[block // 2]
                ).start()
                number += 1

    ready = x_ref.at[pl.ds(2 * step, 2)]
    pltpu.make_async_copy(ready, ready, sems.at[step]).wait()
    tokens = x_ref[pl.ds(2 * step, 2)].reshape(2 * depth, width)
    sums = lax.dot_general(w_ref[...], tokens, NT, preferred_element_type=F32)
    units = o_ref.shape[0]
    hidden = (jax.nn.silu(sums[:units]) * sums[units:]).astype(BF16)
    target = lax.broadcasted_iota(jnp.int32, (2 * depth, o_ref.shape[1]), 1)
    chosen = one_hot(pos_ref[:, column : column + 1] == target)
    picked = jnp.dot(hidden, chosen, preferred_element_type=F32)

    @pl.when(step == 0)
    def _():
        total_ref[...] = picked

    @pl.when(step > 0)
    def _():
        total_ref[...] += picked

    @pl.when(step == pl.num_programs(0) - 1)
    def _():
        o_ref[...] = total_ref[...].astype(BF16)


def hidden_call(weights_t, pieces, tables, pos_cols, slot, parity, rows):
    depth, share = pieces[0].shape[1:]
    units, width = weights_t.shape[0] // 4, weights_t.shape[1]
    blocks = pos_cols.shape[0] // depth
    tile = 2 * depth
    return pl.pallas_call(
        functools.partial(hidden_kernel, slot * 2 + parity),
        grid_spec=pltpu.PrefetchScalarGridSpec(
            num_scalar_prefetch=2,
            grid=(blocks // 2,),
            in_specs=[
                pl.BlockSpec((tile, pos_cols.shape[1]), lambda i, s, t: (i, 0)),
                pl.BlockSpec((2 * units, width), lambda i, s, t: (slot, 0)),
            ]
            + [pl.BlockSpec(memory_space=pl.ANY)] * len(pieces),
            out_specs=pl.BlockSpec((units, rows), lambda i, s, t: (0, 0)),
            scratch_shapes=[
                pltpu.VMEM((blocks, depth, width), BF16),
                pltpu.VMEM((units, rows), F32),
                pltpu.SemaphoreType.DMA((blocks // 2,)),
            ],
        ),
        out_shape=jax.ShapeDtypeStruct((units, rows), BF16),
        compiler_params=pltpu.CompilerParams(vmem_limit_bytes=VMEM_LIMIT),
        cost_estimate=pl.CostEstimate(
            flops=4 * units * width * blocks * depth,
            bytes_accessed=2 * (2 * units * width + blocks * depth * width),
            transcendentals=units * blocks * depth,
        ),
        name="hidden",
    )(*tables, pos_cols, weights_t, *pieces)


def scaled_kernel(column, pos_ref, w_ref, c_ref, o_ref):
    scaled = (w_ref[:, column : column + 1] * c_ref[...].astype(F32)).astype(BF16)
    rows = o_ref.shape[0]
    row = lax.broadcasted_iota(jnp.int32, (rows, c_ref.shape[0]), 0)
    chosen = one_hot(pos_ref[column : column + 1, :] == row)
    o_ref[...] = jnp.dot(chosen, scaled, preferred_element_type=F32).astype(BF16)


def scaled_call(cotangents, pos_rows, weight_cols, slot, parity, rows):
    count, share = cotangents.shape
    return pl.pallas_call(
        functools.partial(scaled_kernel, slot * 2 + parity),
        out_shape=jax.ShapeDtypeStruct((rows, share), BF16),
        compiler_params=pltpu.CompilerParams(vmem_limit_bytes=VMEM_LIMIT),
        cost_estimate=pl.CostEstimate(
            flops=2 * count * share * rows,
            bytes_accessed=2 * share * (count + rows),
            transcendentals=0,
        ),
        name="scaled",
    )(pos_rows, weight_cols, cotangents)


def load_hidden(marks, units, table, refs, hidden, sems):
    @pl.when(pl.program_id(0) == 0)
    def _():
        copies = []
        for number, ((place, half), ref) in enumerate(zip(marks, refs)):
            start = pl.multiple_of(table[place] * units, units)
            begin = 0 if half is None else half * ref.shape[1]
            target = hidden.at[pl.ds(start, units), pl.ds(begin, ref.shape[1])]
            copies.append(pltpu.make_async_copy(ref, target, sems.at[number]))
        for copy in copies:
            copy.start()
        for copy in copies:
            copy.wait()


def gradient_tile(hidden, a_ref, b_ref, tile):
    start = pl.multiple_of(pl.program_id(0) * tile, tile)
    half = a_ref.shape[0]
    return jnp.dot(
        hidden[pl.ds(start, tile), :half], a_ref[...], preferred_element_type=F32
    ) + jnp.dot(hidden[pl.ds(start, tile), half:], b_ref[...], preferred_element_type=F32)


def replica_gradient_kernel(marks, units, table, a_ref, b_ref, *refs):
    count = len(marks)
    pieces, (o_ref, hidden, sems) = refs[:count], refs[count:]
    load_hidden(marks, units, table, pieces, hidden, sems)
    o_ref[...] = gradient_tile(hidden, a_ref, b_ref, o_ref.shape[0]).astype(BF16)


def replica_gradient_call(pieces, scaled, table):
    units, rows = pieces[0][0].shape
    half, share = scaled[0].shape
    total = 8 * units
    tile = 512
    return pl.pallas_call(
        functools.partial(replica_gradient_kernel, [piece[1:] for piece in pieces], units),
        grid_spec=pltpu.PrefetchScalarGridSpec(
            num_scalar_prefetch=1,
            grid=(total // tile,),
            in_specs=[pl.BlockSpec((half, share), lambda i, t: (0, 0))] * 2
            + [pl.BlockSpec(memory_space=pl.ANY)] * len(pieces),
            out_specs=pl.BlockSpec((tile, share), lambda i, t: (i, 0)),
            scratch_shapes=[
                pltpu.VMEM((total, rows), BF16),
                pltpu.SemaphoreType.DMA((len(pieces),)),
            ],
        ),
        out_shape=jax.ShapeDtypeStruct((total, share), BF16),
        compiler_params=pltpu.CompilerParams(vmem_limit_bytes=VMEM_LIMIT),
        cost_estimate=pl.CostEstimate(
            flops=2 * total * rows * share,
            bytes_accessed=2 * (total * rows + rows * share + total * share),
            transcendentals=0,
        ),
        name="replica_gradient",
    )(table, *scaled, *[piece[0] for piece in pieces])


def update_kernel(marks, units, table, a_ref, b_ref, total_ref, one_ref, two_ref, down_ref, *refs):
    count = len(marks)
    pieces = refs[:count]
    down_out, one_out, two_out, hidden, sems = refs[count:]
    load_hidden(marks, units, table, pieces, hidden, sems)
    gradient = gradient_tile(hidden, a_ref, b_ref, down_out.shape[0]) + total_ref[...].astype(F32)
    one = beta_one * one_ref[...] + (1.0 - beta_one) * gradient
    two = beta_two * two_ref[...] + (1.0 - beta_two) * gradient * gradient
    one_out[...] = one
    two_out[...] = two
    update = (learn_rate / correct_one) * one / (jnp.sqrt(two * (1.0 / correct_two)) + epsilon)
    down_out[...] = (
        down_ref[...].astype(F32) * (1.0 - learn_rate * weight_decay) - update
    ).astype(BF16)


def update_call(pieces, scaled, table, total_gradient, moment1, moment2, down):
    units, rows = pieces[0][0].shape
    half, share = scaled[0].shape
    total = 8 * units
    tile = 256
    block = pl.BlockSpec((tile, share), lambda i, t: (i, 0))
    return pl.pallas_call(
        functools.partial(update_kernel, [piece[1:] for piece in pieces], units),
        grid_spec=pltpu.PrefetchScalarGridSpec(
            num_scalar_prefetch=1,
            grid=(total // tile,),
            in_specs=[pl.BlockSpec((half, share), lambda i, t: (0, 0))] * 2
            + [block] * 4
            + [pl.BlockSpec(memory_space=pl.ANY)] * len(pieces),
            out_specs=[block] * 3,
            scratch_shapes=[
                pltpu.VMEM((total, rows), BF16),
                pltpu.SemaphoreType.DMA((len(pieces),)),
            ],
        ),
        out_shape=[
            jax.ShapeDtypeStruct((total, share), BF16),
            jax.ShapeDtypeStruct((total, share), F32),
            jax.ShapeDtypeStruct((total, share), F32),
        ],
        compiler_params=pltpu.CompilerParams(vmem_limit_bytes=VMEM_LIMIT),
        cost_estimate=pl.CostEstimate(
            flops=2 * total * rows * share,
            bytes_accessed=2 * total * rows + 22 * total * share,
            transcendentals=total * share,
        ),
        name="update",
    )(table, *scaled, total_gradient, moment1, moment2, down, *[piece[0] for piece in pieces])


def output_kernel(marks, parity, column, units, with_prior, table, down_ref, pos_ref, w_ref, *refs):
    if with_prior:
        prior_ref, refs = refs[0], refs[1:]
    count = len(marks)
    pieces = refs[:count]
    o_ref, hidden, outputs, sems = refs[count:]
    rows = hidden.shape[1]
    copies = []
    for number, ((place, half), ref) in enumerate(zip(marks, pieces)):
        start = pl.multiple_of(table[place] * units, units)
        source = ref.at[:, pl.ds(parity * rows, rows)] if half is None else ref
        copies.append(
            pltpu.make_async_copy(source, hidden.at[pl.ds(start, units)], sems.at[number])
        )
    for copy in copies:
        copy.start()
    for copy in copies:
        copy.wait()
    for begin in range(0, rows, 256):
        outputs[:, begin : begin + 256] = jnp.dot(
            down_ref[...], hidden[:, begin : begin + 256], preferred_element_type=F32
        ).astype(BF16)
    tile = 256
    for begin in range(0, o_ref.shape[0], tile):
        window = slice(begin, begin + tile)
        target = lax.broadcasted_iota(jnp.int32, (tile, rows), 1)
        chosen = one_hot(pos_ref[window, column : column + 1] == target)
        picked = lax.dot_general(chosen, outputs[...], NT, preferred_element_type=F32)
        value = w_ref[window, column : column + 1] * picked
        if with_prior:
            value = value + prior_ref[window, :]
        o_ref[window, :] = value.astype(o_ref.dtype)


def output_call(pieces, down_t, table, pos_cols, weight_cols, slot, parity, prior):
    pieces = [piece for piece in pieces if piece[2] in (None, parity)]
    units, both = pieces[0][0].shape
    rows = both // 2
    share, total = down_t.shape
    count = pos_cols.shape[0]
    vmem = pl.BlockSpec(memory_space=pltpu.VMEM)
    extra = [] if prior is None else [prior]
    return pl.pallas_call(
        functools.partial(
            output_kernel,
            [piece[1:] for piece in pieces],
            parity,
            slot * 2 + parity,
            units,
            prior is not None,
        ),
        in_specs=[pl.BlockSpec(memory_space=pltpu.SMEM)]
        + [vmem] * (3 + len(extra))
        + [pl.BlockSpec(memory_space=pl.ANY)] * len(pieces),
        out_specs=vmem,
        scratch_shapes=[
            pltpu.VMEM((total, rows), BF16),
            pltpu.VMEM((share, rows), BF16),
            pltpu.SemaphoreType.DMA((len(pieces),)),
        ],
        out_shape=jax.ShapeDtypeStruct((count, share), F32 if prior is None else BF16),
        compiler_params=pltpu.CompilerParams(vmem_limit_bytes=VMEM_LIMIT),
        cost_estimate=pl.CostEstimate(
            flops=2 * total * rows * share + 2 * count * rows * share,
            bytes_accessed=2 * (total * rows + total * share) + 6 * count * share,
            transcendentals=0,
        ),
        name="output",
    )(table, down_t, pos_cols, weight_cols, *extra, *[piece[0] for piece in pieces])


def per_device(
    tokens,
    cotangent,
    router_weights,
    routes,
    replica_map,
    gate_primary,
    up_primary,
    down_primary,
    gate_replica,
    up_replica,
    down_replica,
    moment1,
    moment2,
):
    groups = lax.axis_size("ep")
    count, top = routes.shape
    hidden_units, share = down_primary.shape[1:]
    half_groups = groups // 2
    rows = half_groups * (3 * count * top // (2 * groups))
    ep = lax.axis_index("ep")
    rep = lax.axis_index("rep")
    core = ep % 2

    slot_ids = jnp.arange(2 * groups, dtype=jnp.int32)
    dense = jnp.sum(
        jnp.where(routes[None] == slot_ids[:, None, None], router_weights[None], 0.0), axis=2
    ).reshape(groups, 2, count)
    served = lax.all_to_all(dense, "ep", split_axis=0, concat_axis=0, tiled=True)
    cot_all = lax.all_gather(cotangent, "ep", axis=0)

    line = gather_ring(tokens[None], "xx")
    plane = gather_ring(line, "zy")
    plane, served = together(plane, served)
    half = plane.shape[0] // 2
    below = move_torus(plane, "yz", 3)
    above = move_torus(plane, "yz", 1)

    served = served.reshape(half_groups, 2, 2, count)
    served = jnp.stack(
        [lax.dynamic_index_in_dim(served, c, axis=1, keepdims=False) for c in (core, 1 - core)]
    )
    served = jnp.transpose(served, (2, 0, 1, 3)).reshape(4, half_groups, count)
    hit = (served != 0.0).astype(F32)
    earlier = jnp.triu(jnp.ones((count, count), F32), 1)
    blocks_before = jnp.triu(jnp.ones((half_groups, half_groups), F32), 1)
    inside = jnp.einsum("lbt,tu->lbu", hit, earlier, precision=lax.Precision.HIGHEST)
    before = jnp.einsum(
        "lb,bc->lc", jnp.sum(hit, axis=2), blocks_before, precision=lax.Precision.HIGHEST
    )
    pos_rows = jnp.where(hit > 0, (inside + before[:, :, None]).astype(jnp.int32), -1)
    pos_rows = pos_rows.reshape(4, half_groups * count)
    pos_cols = pos_rows.T
    weight_cols = served.reshape(4, half_groups * count).T
    weights_t = jnp.concatenate(
        [gate_primary[0].T, up_primary[0].T, gate_replica[0].T, up_replica[0].T], axis=0
    )

    x, y, z = 2 * (rep // 4) + ep // 8, rep % 4, (ep // 2) % 4

    def tables(other):
        block, part = [], []
        kind = core if other == 0 else 1 - core
        for last in RINGS:
            for second in RINGS:
                for first in RINGS:
                    from_x = (x + first) % RING
                    from_y = (y + jnp.where(kind == 0, last, second)) % RING
                    from_z = (z + jnp.where(kind == 0, second, last)) % RING
                    block.append((from_x % 2) * RING + from_z)
                    part.append((from_x // 2) * RING + from_y)
        return jnp.stack(block).astype(jnp.int32), jnp.stack(part).astype(jnp.int32)

    own_tables, other_tables = tables(0), tables(1)
    rep_pair, rep_ring = rep // RING, rep % RING
    places = jnp.stack(
        [(rep_pair ^ dp) * RING + (rep_ring + dr) % RING for dp, dr in ORDER]
    ).astype(jnp.int32)

    plane_other = swap_core(plane)
    below, above, weights_t, pos_rows, pos_cols, weight_cols, own_tables, other_tables, places, plane_other = (
        together(
            below,
            above,
            weights_t,
            pos_rows,
            pos_cols,
            weight_cols,
            own_tables,
            other_tables,
            places,
            plane_other,
        )
    )
    far_low = move_torus(below[:half], "yz", 3)
    far_high = move_torus(above[half:], "yz", 1)
    below_other, above_other = swap_core(below), swap_core(above)
    down_t = [down_primary[0].T, down_replica[0].T]
    far_low, far_high, below_other, above_other, down_t = together(
        far_low, far_high, below_other, above_other, down_t
    )
    own_pieces = [plane, below, above, far_low, far_high]
    other_pieces = [plane_other, below_other, above_other, swap_core(far_low), swap_core(far_high)]

    def slot_hidden(slot, weights):
        own = hidden_call(weights, own_pieces, own_tables, pos_cols, slot, 0, rows)
        other = hidden_call(
            after(weights, own), other_pieces, other_tables, pos_cols, slot, 1, rows
        )
        return jnp.concatenate([own, other], axis=1)

    def scale(slot):
        return [
            scaled_call(cot_halves[parity], pos_rows, weight_cols, slot, parity, rows)
            for parity in range(2)
        ]

    replica_hidden = slot_hidden(1, weights_t)
    below = move_rep(replica_hidden, 0, 3)
    above = move_rep(replica_hidden, 0, 1)
    across = move_rep(replica_hidden, 1, 0)
    primary_hidden = slot_hidden(0, after(weights_t, replica_hidden))
    below, above, across, primary_hidden = together(below, above, across, primary_hidden)
    far_low = move_rep(below[:, :rows], 0, 3)
    far_high = move_rep(above[:, rows:], 0, 1)
    cot_all, _ = together(cot_all, primary_hidden)
    cot_all = cot_all.reshape(half_groups, 2, count, share)
    cot_halves = [
        lax.dynamic_index_in_dim(cot_all, c, axis=1, keepdims=False).reshape(
            half_groups * count, share
        )
        for c in (core, 1 - core)
    ]
    scaled_replica = scale(1)
    far_low, far_high, across, scaled_replica = together(far_low, far_high, across, scaled_replica)
    across_below = move_rep(across, 0, 3)
    across_above = move_rep(across, 0, 1)
    across_far_low = move_rep(far_low, 1, 0)
    across_far_high = move_rep(far_high, 1, 0)
    cot_halves = after(cot_halves, scaled_replica)
    scaled_primary = scale(0)

    shares = after(down_primary[0], replica_hidden).reshape(
        groups, hidden_units // groups, share
    )
    spread_weights = lax.all_to_all(shares, "ep", split_axis=0, concat_axis=0, tiled=True)
    chosen = jnp.take(spread_weights, replica_map, axis=0)
    refreshed = lax.all_to_all(chosen, "ep", split_axis=0, concat_axis=0, tiled=True).reshape(
        1, hidden_units, share
    )

    across_below, across_above, across_far_low, across_far_high, scaled_primary = together(
        across_below, across_above, across_far_low, across_far_high, scaled_primary
    )
    replica_pieces = [
        (replica_hidden, 0, None),
        (below, 1, None),
        (above, 2, None),
        (across, 3, None),
        (far_low, 4, 0),
        (far_high, 4, 1),
        (across_below, 5, None),
        (across_above, 6, None),
        (across_far_low, 7, 0),
        (across_far_high, 7, 1),
    ]

    primary_hidden = after(primary_hidden, across_below)
    below = move_rep(primary_hidden, 0, 3)
    above = move_rep(primary_hidden, 0, 1)
    across = move_rep(primary_hidden, 1, 0)
    replica_gradient = replica_gradient_call(replica_pieces, scaled_replica, places)
    below, above, across, replica_gradient = together(below, above, across, replica_gradient)
    spread = lax.all_to_all(
        replica_gradient.reshape(groups, hidden_units // groups, share),
        "ep",
        split_axis=0,
        concat_axis=0,
        tiled=True,
    )
    far_low = move_rep(below[:, :rows], 0, 3)
    far_high = move_rep(above[:, rows:], 0, 1)
    prior_other = output_call(
        replica_pieces, after(down_t[1], below), places, pos_cols, weight_cols, 1, 1, None
    )
    far_low, far_high, across, prior_other = together(far_low, far_high, across, prior_other)
    across_below = move_rep(across, 0, 3)
    across_above = move_rep(across, 0, 1)
    across_far_low = move_rep(far_low, 1, 0)
    across_far_high = move_rep(far_high, 1, 0)
    prior_own = output_call(
        replica_pieces, after(down_t[1], prior_other), places, pos_cols, weight_cols, 1, 0, None
    )
    owners = (replica_map[None, :] == jnp.arange(groups, dtype=jnp.int32)[:, None]).astype(BF16)
    summed = jnp.einsum("pj,jfd->pfd", owners, spread, preferred_element_type=F32)
    replica_total = lax.all_to_all(
        summed.astype(BF16), "ep", split_axis=0, concat_axis=0, tiled=True
    ).reshape(hidden_units, share)
    across_below, across_above, across_far_low, across_far_high, prior_own = together(
        across_below, across_above, across_far_low, across_far_high, prior_own
    )
    primary_pieces = [
        (primary_hidden, 0, None),
        (below, 1, None),
        (above, 2, None),
        (across, 3, None),
        (far_low, 4, 0),
        (far_high, 4, 1),
        (across_below, 5, None),
        (across_above, 6, None),
        (across_far_low, 7, 0),
        (across_far_high, 7, 1),
    ]

    theirs = output_call(
        primary_pieces, down_t[0], places, pos_cols, weight_cols, 0, 1, prior_other
    )
    arrived = swap_core(theirs)
    mine = output_call(
        primary_pieces, after(down_t[0], theirs), places, pos_cols, weight_cols, 0, 0, prior_own
    )
    mine = (mine.astype(F32) + arrived.astype(F32)).astype(BF16).reshape(half_groups, count, share)
    returned = lax.all_to_all(
        mine,
        "ep",
        split_axis=0,
        concat_axis=0,
        axis_index_groups=[list(range(0, groups, 2)), list(range(1, groups, 2))],
        tiled=True,
    )
    layer = jnp.sum(returned.astype(F32), axis=0)

    down_new, moment1_new, moment2_new = update_call(
        primary_pieces,
        after(scaled_primary, mine),
        places,
        replica_total,
        moment1[0],
        moment2[0],
        down_primary[0],
    )
    return (layer.astype(BF16), down_new[None], moment1_new[None], moment2_new[None], refreshed)


def solution(mesh):
    return jax.shard_map(
        per_device,
        mesh=mesh,
        in_specs=(
            P("ep", "rep"),
            P("ep", "rep"),
            P("ep", None),
            P("ep", None),
            P(),
            P("ep", None, "rep"),
            P("ep", None, "rep"),
            P("ep", None, "rep"),
            P("ep", None, "rep"),
            P("ep", None, "rep"),
            P("ep", None, "rep"),
            P("ep", None, "rep"),
            P("ep", None, "rep"),
        ),
        out_specs=(
            P("ep", "rep"),
            P("ep", None, "rep"),
            P("ep", None, "rep"),
            P("ep", None, "rep"),
            P("ep", None, "rep"),
        ),
        check_vma=False,
    )
```

```python
import functools

import jax
import jax.numpy as jnp
import numpy as np
from jax import lax
from jax.experimental import pallas as pl
from jax.experimental.pallas import tpu as pltpu
from jax.sharding import PartitionSpec as P

beta_one = 0.9
beta_two = 0.95
learn_rate = 0.001
weight_decay = 0.1
epsilon = 1e-08
correct_one = 1.0 - 0.9**10
correct_two = 1.0 - 0.95**10

BF16 = jnp.bfloat16
F32 = jnp.float32
NT = (((1,), (1,)), ((), ()))
TN = (((0,), (0,)), ((), ()))
VMEM_LIMIT = 56 * 1024 * 1024


ORDER = [(0, 0), (0, 3), (0, 1), (1, 0), (0, 2), (1, 3), (1, 1), (1, 2)]
RING = 4


def torus_place(i):
    ep, rep = i // 8, i % 8
    return 2 * (rep // 4) + ep // 8, rep % 4, (ep // 2) % 4, ep % 2


def torus_index(x, y, z, core):
    return (((x % 2) * 4 + z % 4) * 2 + core) * 8 + (x // 2) * 4 + y % 4


def torus_perm(axes, offset):
    perm = []
    for i in range(128):
        place = list(torus_place(i))
        axis = "xyz".index(axes[place[3]])
        place[axis] = (place[axis] - offset) % RING
        perm.append((i, torus_index(*place)))
    return perm


def move_torus(x, axes, offset):
    return lax.ppermute(x, ("ep", "rep"), torus_perm(axes, offset))


def move_rep(x, pair_offset, ring_offset):
    perm = []
    for i in range(8):
        pair, ring = (i // RING) ^ pair_offset, (i % RING - ring_offset) % RING
        perm.append((i, pair * RING + ring))
    return lax.ppermute(x, "rep", perm)


def swap_core(x):
    return lax.ppermute(x, "ep", [(i, i ^ 1) for i in range(16)])


def together(*values):
    return lax.optimization_barrier(values)


def after(value, *others):
    return lax.optimization_barrier((value, others))[0]


RINGS = [0, 3, 1, 2]


def gather_ring(x, axes):
    return together(x, *[move_torus(x, axes, offset) for offset in RINGS[1:]])


HALVES = [(0, 0), (0, 1), (3, 0), (1, 1), (3, 1), (1, 0), (2, 0), (2, 1)]
OFFSETS = [
    (first, second, last)
    for last, half in HALVES
    for second in RINGS[2 * half : 2 * half + 2]
    for first in RINGS
]


def block_slot(number, kind):
    first, second, last = OFFSETS[number]
    return (first % 2) * RING + (second if kind == 0 else last)


def one_hot(mask):
    return jnp.where(mask, 1.0, 0.0).astype(BF16)


def hidden_kernel(column, table, part_table, a_ref, b_ref, w_ref, *refs):
    pieces = refs[:-4]
    o_ref, x_ref, total_ref, sems = refs[-4:]
    step = pl.program_id(0)
    blocks, depth, width = x_ref.shape
    per_piece, _, share = pieces[0].shape

    @pl.when(step == 0)
    def _():
        for kind in range(2):

            @pl.when(table[blocks] == kind)
            def _():
                for number in sorted(range(len(OFFSETS)), key=lambda n: block_slot(n, kind)):
                    slot = block_slot(number, kind)
                    start = pl.multiple_of(part_table[number] * share, share)
                    pltpu.make_async_copy(
                        pieces[number // per_piece].at[number % per_piece],
                        x_ref.at[slot, :, pl.ds(start, share)],
                        sems.at[slot // 2],
                    ).start()

    ready = x_ref.at[pl.ds(2 * step, 2)]
    pltpu.make_async_copy(ready, ready, sems.at[step]).wait()
    tokens = x_ref[pl.ds(2 * step, 2)].reshape(2 * depth, width)
    sums = lax.dot_general(w_ref[...], tokens, NT, preferred_element_type=F32)
    units = o_ref.shape[0]
    hidden = (jax.nn.silu(sums[:units]) * sums[units:]).astype(BF16)
    target = lax.broadcasted_iota(jnp.int32, (depth, o_ref.shape[1]), 1)
    chosen = jnp.concatenate(
        [one_hot(ref[:, column : column + 1] == target) for ref in (a_ref, b_ref)], axis=0
    )
    picked = jnp.dot(hidden, chosen, preferred_element_type=F32)

    @pl.when(step == 0)
    def _():
        total_ref[...] = picked

    @pl.when(step > 0)
    def _():
        total_ref[...] += picked

    @pl.when(step == pl.num_programs(0) - 1)
    def _():
        o_ref[...] = total_ref[...].astype(BF16)


def hidden_call(weights_t, pieces, tables, pos_cols, slot, parity, rows):
    depth, share = pieces[0].shape[1:]
    units, width = weights_t.shape[0] // 4, weights_t.shape[1]
    blocks = pos_cols.shape[0] // depth
    return pl.pallas_call(
        functools.partial(hidden_kernel, slot * 2 + parity),
        grid_spec=pltpu.PrefetchScalarGridSpec(
            num_scalar_prefetch=2,
            grid=(blocks // 2,),
            in_specs=[
                pl.BlockSpec((depth, pos_cols.shape[1]), lambda i, s, t: (s[2 * i], 0)),
                pl.BlockSpec((depth, pos_cols.shape[1]), lambda i, s, t: (s[2 * i + 1], 0)),
                pl.BlockSpec((2 * units, width), lambda i, s, t: (slot, 0)),
            ]
            + [pl.BlockSpec(memory_space=pl.ANY)] * len(pieces),
            out_specs=pl.BlockSpec((units, rows), lambda i, s, t: (0, 0)),
            scratch_shapes=[
                pltpu.VMEM((blocks, depth, width), BF16),
                pltpu.VMEM((units, rows), F32),
                pltpu.SemaphoreType.DMA((blocks // 2,)),
            ],
        ),
        out_shape=jax.ShapeDtypeStruct((units, rows), BF16),
        compiler_params=pltpu.CompilerParams(vmem_limit_bytes=VMEM_LIMIT),
        cost_estimate=pl.CostEstimate(
            flops=4 * units * width * blocks * depth,
            bytes_accessed=2 * (2 * units * width + blocks * depth * width),
            transcendentals=units * blocks * depth,
        ),
        name="hidden",
    )(*tables, pos_cols, pos_cols, weights_t, *pieces)


def scaled_kernel(column, pos_ref, w_ref, c_ref, o_ref):
    scaled = (w_ref[:, column : column + 1] * c_ref[...].astype(F32)).astype(BF16)
    rows = o_ref.shape[0]
    row = lax.broadcasted_iota(jnp.int32, (rows, c_ref.shape[0]), 0)
    chosen = one_hot(pos_ref[column : column + 1, :] == row)
    o_ref[...] = jnp.dot(chosen, scaled, preferred_element_type=F32).astype(BF16)


def scaled_call(cotangents, pos_rows, weight_cols, slot, parity, rows):
    count, share = cotangents.shape
    return pl.pallas_call(
        functools.partial(scaled_kernel, slot * 2 + parity),
        out_shape=jax.ShapeDtypeStruct((rows, share), BF16),
        compiler_params=pltpu.CompilerParams(vmem_limit_bytes=VMEM_LIMIT),
        cost_estimate=pl.CostEstimate(
            flops=2 * count * share * rows,
            bytes_accessed=2 * share * (count + rows),
            transcendentals=0,
        ),
        name="scaled",
    )(pos_rows, weight_cols, cotangents)


def load_hidden(units, table, refs, hidden, sems, begin=0):
    columns = pl.ds(begin, hidden.shape[1])
    copies = []
    for place, ref in enumerate(refs):
        start = pl.multiple_of(table[place] * units, units)
        copies.append(
            pltpu.make_async_copy(
                ref.at[:, columns], hidden.at[pl.ds(start, units)], sems.at[place]
            )
        )
    for copy in copies:
        copy.start()
    for copy in copies:
        copy.wait()


def gradient_tile(hidden, a_ref, b_ref, tile):
    start = pl.multiple_of(pl.program_id(0) * tile, tile)
    half = a_ref.shape[0]
    return jnp.dot(
        hidden[pl.ds(start, tile), :half], a_ref[...], preferred_element_type=F32
    ) + jnp.dot(hidden[pl.ds(start, tile), half:], b_ref[...], preferred_element_type=F32)


def replica_gradient_kernel(units, table, a_ref, b_ref, *refs):
    pieces, (o_ref, hidden, sems) = refs[:-3], refs[-3:]

    @pl.when(pl.program_id(0) == 0)
    def _():
        load_hidden(units, table, pieces, hidden, sems)

    o_ref[...] = gradient_tile(hidden, a_ref, b_ref, o_ref.shape[0]).astype(BF16)


def replica_gradient_call(pieces, scaled, table):
    units, rows = pieces[0].shape
    half, share = scaled[0].shape
    total = 8 * units
    tile = 512
    return pl.pallas_call(
        functools.partial(replica_gradient_kernel, units),
        grid_spec=pltpu.PrefetchScalarGridSpec(
            num_scalar_prefetch=1,
            grid=(total // tile,),
            in_specs=[pl.BlockSpec((half, share), lambda i, t: (0, 0))] * 2
            + [pl.BlockSpec(memory_space=pl.ANY)] * len(pieces),
            out_specs=pl.BlockSpec((tile, share), lambda i, t: (i, 0)),
            scratch_shapes=[
                pltpu.VMEM((total, rows), BF16),
                pltpu.SemaphoreType.DMA((len(pieces),)),
            ],
        ),
        out_shape=jax.ShapeDtypeStruct((total, share), BF16),
        compiler_params=pltpu.CompilerParams(vmem_limit_bytes=VMEM_LIMIT),
        cost_estimate=pl.CostEstimate(
            flops=2 * total * rows * share,
            bytes_accessed=2 * (total * rows + rows * share + total * share),
            transcendentals=0,
        ),
        name="replica_gradient",
    )(table, *scaled, *pieces)


def update_kernel(units, table, a_ref, b_ref, total_ref, one_ref, two_ref, down_ref, *refs):
    pieces = refs[:-5]
    down_out, one_out, two_out, hidden, sems = refs[-5:]

    @pl.when(pl.program_id(0) == 0)
    def _():
        load_hidden(units, table, pieces, hidden, sems)

    gradient = gradient_tile(hidden, a_ref, b_ref, down_out.shape[0]) + total_ref[...].astype(F32)
    one = beta_one * one_ref[...] + (1.0 - beta_one) * gradient
    two = beta_two * two_ref[...] + (1.0 - beta_two) * gradient * gradient
    one_out[...] = one
    two_out[...] = two
    update = (learn_rate / correct_one) * one / (jnp.sqrt(two * (1.0 / correct_two)) + epsilon)
    down_out[...] = (
        down_ref[...].astype(F32) * (1.0 - learn_rate * weight_decay) - update
    ).astype(BF16)


def update_call(pieces, scaled, table, total_gradient, moment1, moment2, down):
    units, rows = pieces[0].shape
    half, share = scaled[0].shape
    total = 8 * units
    tile = 256
    block = pl.BlockSpec((tile, share), lambda i, t: (i, 0))
    return pl.pallas_call(
        functools.partial(update_kernel, units),
        grid_spec=pltpu.PrefetchScalarGridSpec(
            num_scalar_prefetch=1,
            grid=(total // tile,),
            in_specs=[pl.BlockSpec((half, share), lambda i, t: (0, 0))] * 2
            + [block] * 4
            + [pl.BlockSpec(memory_space=pl.ANY)] * len(pieces),
            out_specs=[block] * 3,
            scratch_shapes=[
                pltpu.VMEM((total, rows), BF16),
                pltpu.SemaphoreType.DMA((len(pieces),)),
            ],
        ),
        out_shape=[
            jax.ShapeDtypeStruct((total, share), BF16),
            jax.ShapeDtypeStruct((total, share), F32),
            jax.ShapeDtypeStruct((total, share), F32),
        ],
        compiler_params=pltpu.CompilerParams(vmem_limit_bytes=VMEM_LIMIT),
        cost_estimate=pl.CostEstimate(
            flops=2 * total * rows * share,
            bytes_accessed=2 * total * rows + 22 * total * share,
            transcendentals=total * share,
        ),
        name="update",
    )(table, *scaled, total_gradient, moment1, moment2, down, *pieces)


def output_kernel(parity, column, units, with_prior, table, down_ref, pos_ref, w_ref, *refs):
    if with_prior:
        prior_ref, refs = refs[0], refs[1:]
    pieces = refs[:-4]
    o_ref, hidden, outputs, sems = refs[-4:]
    rows = hidden.shape[1]
    load_hidden(units, table, pieces, hidden, sems, parity * rows)
    for begin in range(0, rows, 256):
        outputs[begin : begin + 256, :] = lax.dot_general(
            hidden[:, begin : begin + 256], down_ref[...], TN, preferred_element_type=F32
        ).astype(BF16)
    tile = 256
    for begin in range(0, o_ref.shape[0], tile):
        window = slice(begin, begin + tile)
        target = lax.broadcasted_iota(jnp.int32, (tile, rows), 1)
        chosen = one_hot(pos_ref[window, column : column + 1] == target)
        picked = jnp.dot(chosen, outputs[...], preferred_element_type=F32)
        value = w_ref[window, column : column + 1] * picked
        if with_prior:
            value = value + prior_ref[window, :]
        o_ref[window, :] = value.astype(o_ref.dtype)


def output_call(pieces, down, table, pos_cols, weight_cols, slot, parity, prior):
    units, both = pieces[0].shape
    rows = both // 2
    total, share = down.shape
    count = pos_cols.shape[0]
    vmem = pl.BlockSpec(memory_space=pltpu.VMEM)
    extra = [] if prior is None else [prior]
    return pl.pallas_call(
        functools.partial(output_kernel, parity, slot * 2 + parity, units, prior is not None),
        in_specs=[pl.BlockSpec(memory_space=pltpu.SMEM)]
        + [vmem] * (3 + len(extra))
        + [pl.BlockSpec(memory_space=pl.ANY)] * len(pieces),
        out_specs=vmem,
        scratch_shapes=[
            pltpu.VMEM((total, rows), BF16),
            pltpu.VMEM((rows, share), BF16),
            pltpu.SemaphoreType.DMA((len(pieces),)),
        ],
        out_shape=jax.ShapeDtypeStruct((count, share), F32 if prior is None else BF16),
        compiler_params=pltpu.CompilerParams(vmem_limit_bytes=VMEM_LIMIT),
        cost_estimate=pl.CostEstimate(
            flops=2 * total * rows * share + 2 * count * rows * share,
            bytes_accessed=2 * (total * rows + total * share) + 6 * count * share,
            transcendentals=0,
        ),
        name="output",
    )(table, down, pos_cols, weight_cols, *extra, *pieces)


def per_device(
    tokens,
    cotangent,
    router_weights,
    routes,
    replica_map,
    gate_primary,
    up_primary,
    down_primary,
    gate_replica,
    up_replica,
    down_replica,
    moment1,
    moment2,
):
    groups = lax.axis_size("ep")
    count, top = routes.shape
    hidden_units, share = down_primary.shape[1:]
    half_groups = groups // 2
    rows = half_groups * (3 * count * top // (2 * groups))
    ep = lax.axis_index("ep")
    rep = lax.axis_index("rep")
    core = ep % 2

    slot_ids = jnp.arange(2 * groups, dtype=jnp.int32)
    dense = jnp.sum(
        jnp.where(routes[None] == slot_ids[:, None, None], router_weights[None], 0.0), axis=2
    ).reshape(groups, 2, count)
    served = lax.all_to_all(dense, "ep", split_axis=0, concat_axis=0, tiled=True)
    cot_all = lax.all_gather(cotangent, "ep", axis=0)

    line = jnp.concatenate(gather_ring(tokens[None], "xx"), axis=0)
    plane = gather_ring(line, "zy")
    low, high = jnp.concatenate(plane[:2], axis=0), jnp.concatenate(plane[2:], axis=0)
    low, high, served = together(low, high, served)
    below_low = move_torus(low, "yz", 3)
    above_high = move_torus(high, "yz", 1)

    served = served.reshape(half_groups, 2, 2, count)
    served = jnp.stack(
        [lax.dynamic_index_in_dim(served, c, axis=1, keepdims=False) for c in (core, 1 - core)]
    )
    served = jnp.transpose(served, (2, 0, 1, 3)).reshape(4, half_groups, count)
    hit = (served != 0.0).astype(F32)
    earlier = jnp.triu(jnp.ones((count, count), F32), 1)
    blocks_before = jnp.triu(jnp.ones((half_groups, half_groups), F32), 1)
    inside = jnp.einsum("lbt,tu->lbu", hit, earlier, precision=lax.Precision.HIGHEST)
    before = jnp.einsum(
        "lb,bc->lc", jnp.sum(hit, axis=2), blocks_before, precision=lax.Precision.HIGHEST
    )
    pos_rows = jnp.where(hit > 0, (inside + before[:, :, None]).astype(jnp.int32), -1)
    pos_rows = pos_rows.reshape(4, half_groups * count)
    pos_cols = pos_rows.T
    weight_cols = served.reshape(4, half_groups * count).T
    weights_t = jnp.concatenate(
        [gate_primary[0].T, up_primary[0].T, gate_replica[0].T, up_replica[0].T], axis=0
    )

    x, y, z = 2 * (rep // 4) + ep // 8, rep % 4, (ep // 2) % 4
    offsets = np.array(OFFSETS, np.int32)
    slots = np.arange(half_groups, dtype=np.int32)

    def tables(kind):
        from_y = (y + jnp.where(kind == 0, offsets[:, 2], offsets[:, 1])) % RING
        part = (((x + offsets[:, 0]) % RING) // 2) * RING + from_y
        block = ((x + slots // RING) % 2) * RING + (z + slots % RING) % RING
        return (
            jnp.concatenate([block, kind[None]]).astype(jnp.int32),
            part.astype(jnp.int32),
        )

    own_tables, other_tables = tables(core), tables(1 - core)
    rep_pair, rep_ring = rep // RING, rep % RING
    order = np.array(ORDER, np.int32)
    places = ((rep_pair ^ order[:, 0]) * RING + (rep_ring + order[:, 1]) % RING).astype(jnp.int32)

    low_other, high_other = swap_core(low), swap_core(high)
    below_low, above_high, weights_t = together(below_low, above_high, weights_t)
    below_high = move_torus(high, "yz", 3)
    above_low = move_torus(low, "yz", 1)
    far_low = move_torus(below_low, "yz", 3)
    far_high = move_torus(above_high, "yz", 1)
    below_low_other, above_high_other = swap_core(below_low), swap_core(above_high)

    cot_all = cot_all.reshape(half_groups, 2, count, share)
    cot_halves = [
        lax.dynamic_index_in_dim(cot_all, c, axis=1, keepdims=False).reshape(
            half_groups * count, share
        )
        for c in (core, 1 - core)
    ]

    def scale(slot):
        return [
            scaled_call(cot_halves[parity], pos_rows, weight_cols, slot, parity, rows)
            for parity in range(2)
        ]

    scaled_replica, scaled_primary = scale(1), scale(0)
    (
        below_high,
        above_low,
        far_low,
        far_high,
        scaled_replica,
        scaled_primary,
        pos_cols,
        weight_cols,
        own_tables,
        other_tables,
        places,
    ) = together(
        below_high,
        above_low,
        far_low,
        far_high,
        scaled_replica,
        scaled_primary,
        pos_cols,
        weight_cols,
        own_tables,
        other_tables,
        places,
    )
    own_pieces = [low, high, below_low, above_high, below_high, above_low, far_low, far_high]
    other_pieces = [low_other, high_other, below_low_other, above_high_other] + [
        swap_core(piece) for piece in own_pieces[4:]
    ]

    def slot_hidden(slot, weights):
        own = hidden_call(weights, own_pieces, own_tables, pos_cols, slot, 0, rows)
        other = hidden_call(
            after(weights, own), other_pieces, other_tables, pos_cols, slot, 1, rows
        )
        return jnp.concatenate([own, other], axis=1)

    def first_level(hidden):
        return [move_rep(hidden, dp, dr) for dp, dr in ((0, 2), (0, 3), (0, 1), (1, 0))]

    def second_level(far, across):
        return [move_rep(across, 0, 3), move_rep(across, 0, 1), move_rep(far, 1, 0)]

    replica_hidden = slot_hidden(1, weights_t)
    near = first_level(replica_hidden)

    shares = after(down_primary[0], replica_hidden).reshape(
        groups, hidden_units // groups, share
    )
    spread_weights = lax.all_to_all(shares, "ep", split_axis=0, concat_axis=0, tiled=True)

    primary_hidden = slot_hidden(0, after(weights_t, replica_hidden))
    near, primary_hidden, spread_weights = together(near, primary_hidden, spread_weights)
    chosen = jnp.take(spread_weights, replica_map, axis=0)
    refreshed = lax.all_to_all(chosen, "ep", split_axis=0, concat_axis=0, tiled=True).reshape(
        1, hidden_units, share
    )
    away = second_level(near[0], near[3])
    away, near, primary_hidden = together(away, near, primary_hidden)
    replica_pieces = [replica_hidden, near[1], near[2], near[3], near[0], *away]

    near = first_level(primary_hidden)
    replica_gradient = replica_gradient_call(replica_pieces, scaled_replica, places)
    replica_gradient, refreshed = together(replica_gradient, refreshed)
    spread = lax.all_to_all(
        replica_gradient.reshape(groups, hidden_units // groups, share),
        "ep",
        split_axis=0,
        concat_axis=0,
        tiled=True,
    )
    prior_other = output_call(
        replica_pieces,
        after(down_replica[0], replica_gradient),
        places,
        pos_cols,
        weight_cols,
        1,
        1,
        None,
    )
    near, prior_other = together(near, prior_other)
    away = second_level(near[0], near[3])
    prior_own = output_call(
        replica_pieces,
        after(down_replica[0], prior_other),
        places,
        pos_cols,
        weight_cols,
        1,
        0,
        None,
    )
    spread, prior_own = together(spread, prior_own)
    owners = (replica_map[None, :] == jnp.arange(groups, dtype=jnp.int32)[:, None]).astype(BF16)
    summed = jnp.einsum("pj,jfd->pfd", owners, spread, preferred_element_type=F32).astype(BF16)
    replica_total = lax.all_to_all(
        summed, "ep", split_axis=0, concat_axis=0, tiled=True
    ).reshape(hidden_units, share)
    away, near, summed = together(away, near, summed)
    primary_pieces = [primary_hidden, near[1], near[2], near[3], near[0], *away]

    theirs = output_call(
        primary_pieces, down_primary[0], places, pos_cols, weight_cols, 0, 1, prior_other
    )
    arrived = swap_core(theirs)
    mine = output_call(
        primary_pieces,
        after(down_primary[0], theirs),
        places,
        pos_cols,
        weight_cols,
        0,
        0,
        prior_own,
    )
    mine = (mine.astype(F32) + arrived.astype(F32)).astype(BF16).reshape(half_groups, count, share)
    mine, replica_total = together(mine, replica_total)
    returned = lax.all_to_all(
        mine,
        "ep",
        split_axis=0,
        concat_axis=0,
        axis_index_groups=[list(range(0, groups, 2)), list(range(1, groups, 2))],
        tiled=True,
    )
    layer = jnp.sum(returned.astype(F32), axis=0)

    down_new, moment1_new, moment2_new = update_call(
        primary_pieces,
        scaled_primary,
        places,
        replica_total,
        moment1[0],
        moment2[0],
        down_primary[0],
    )
    return (layer.astype(BF16), down_new[None], moment1_new[None], moment2_new[None], refreshed)


def solution(mesh):
    return jax.shard_map(
        per_device,
        mesh=mesh,
        in_specs=(
            P("ep", "rep"),
            P("ep", "rep"),
            P("ep", None),
            P("ep", None),
            P(),
            P("ep", None, "rep"),
            P("ep", None, "rep"),
            P("ep", None, "rep"),
            P("ep", None, "rep"),
            P("ep", None, "rep"),
            P("ep", None, "rep"),
            P("ep", None, "rep"),
            P("ep", None, "rep"),
        ),
        out_specs=(
            P("ep", "rep"),
            P("ep", None, "rep"),
            P("ep", None, "rep"),
            P("ep", None, "rep"),
            P("ep", None, "rep"),
        ),
        check_vma=False,
    )
```

```python
import functools

import jax
import jax.numpy as jnp
import numpy as np
from jax import lax
from jax.experimental import pallas as pl
from jax.experimental.pallas import tpu as pltpu
from jax.sharding import PartitionSpec as P

beta_one = 0.9
beta_two = 0.95
learn_rate = 0.001
weight_decay = 0.1
epsilon = 1e-08
correct_one = 1.0 - 0.9**10
correct_two = 1.0 - 0.95**10

BF16 = jnp.bfloat16
F32 = jnp.float32
NT = (((1,), (1,)), ((), ()))
TN = (((0,), (0,)), ((), ()))
VMEM_LIMIT = 20 * 1024 * 1024
HIDDEN_VMEM_LIMIT = 28 * 1024 * 1024


ORDER = [(0, 0), (0, 3), (0, 1), (1, 0), (0, 2), (1, 3), (1, 1), (1, 2)]
RING = 4


def torus_place(i):
    ep, rep = i // 8, i % 8
    return 2 * (rep // 4) + ep // 8, rep % 4, (ep // 2) % 4, ep % 2


def torus_index(x, y, z, core):
    return (((x % 2) * 4 + z % 4) * 2 + core) * 8 + (x // 2) * 4 + y % 4


def torus_perm(axes, offset):
    perm = []
    for i in range(128):
        place = list(torus_place(i))
        axis = "xyz".index(axes[place[3]])
        place[axis] = (place[axis] - offset) % RING
        perm.append((i, torus_index(*place)))
    return perm


def move_torus(x, axes, offset):
    return lax.ppermute(x, ("ep", "rep"), torus_perm(axes, offset))


def move_rep(x, pair_offset, ring_offset):
    perm = []
    for i in range(8):
        pair, ring = (i // RING) ^ pair_offset, (i % RING - ring_offset) % RING
        perm.append((i, pair * RING + ring))
    return lax.ppermute(x, "rep", perm)


def move_ep(x, pair_offset, ring_offset):
    perm = []
    for i in range(16):
        pair, ring = (i // 8) ^ pair_offset, ((i // 2) % RING - ring_offset) % RING
        perm.append((i, (pair * RING + ring) * 2 + i % 2))
    return lax.ppermute(x, "ep", perm)


def swap_core(x):
    return lax.ppermute(x, "ep", [(i, i ^ 1) for i in range(16)])


def together(*values):
    return lax.optimization_barrier(values)


def after(value, *others):
    return lax.optimization_barrier((value, others))[0]


RINGS = [0, 3, 1, 2]


def gather_ring(x, axes):
    return together(x, *[move_torus(x, axes, offset) for offset in RINGS[1:]])


HALVES = [(0, 0), (0, 1), (3, 0), (1, 1), (3, 1), (1, 0), (2, 0), (2, 1)]
OFFSETS = [
    (first, second, last)
    for last, half in HALVES
    for second in RINGS[2 * half : 2 * half + 2]
    for first in RINGS
]


def block_slot(number, kind):
    first, second, last = OFFSETS[number]
    return (first % 2) * RING + (second if kind == 0 else last)


def one_hot(mask):
    return jnp.where(mask, 1.0, 0.0).astype(BF16)


def hidden_kernel(column, table, pos_ref, w_ref, *refs):
    pieces = refs[:-4]
    o_ref, x_ref, total_ref, sems = refs[-4:]
    step = pl.program_id(0)
    blocks, depth, width = x_ref.shape
    per_piece, _, share = pieces[0].shape

    @pl.when(step == 0)
    def _():
        for kind in range(2):

            @pl.when(table[len(OFFSETS)] == kind)
            def _():
                for number in sorted(range(len(OFFSETS)), key=lambda n: block_slot(n, kind)):
                    slot = block_slot(number, kind)
                    start = pl.multiple_of(table[number] * share, share)
                    pltpu.make_async_copy(
                        pieces[number // per_piece].at[number % per_piece],
                        x_ref.at[slot, :, pl.ds(start, share)],
                        sems.at[slot // 2],
                    ).start()

    ready = x_ref.at[pl.ds(2 * step, 2)]
    pltpu.make_async_copy(ready, ready, sems.at[step]).wait()
    tokens = x_ref[pl.ds(2 * step, 2)].reshape(2 * depth, width)
    sums = lax.dot_general(w_ref[...], tokens, NT, preferred_element_type=F32)
    units = o_ref.shape[0]
    hidden = (jax.nn.silu(sums[:units]) * sums[units:]).astype(BF16)
    target = lax.broadcasted_iota(jnp.int32, (2 * depth, o_ref.shape[1]), 1)
    chosen = one_hot(pos_ref[:, column : column + 1] == target)
    picked = jnp.dot(hidden, chosen, preferred_element_type=F32)

    @pl.when(step == 0)
    def _():
        total_ref[...] = picked

    @pl.when(step > 0)
    def _():
        total_ref[...] += picked

    @pl.when(step == pl.num_programs(0) - 1)
    def _():
        o_ref[...] = total_ref[...].astype(BF16)


def hidden_call(weights_t, pieces, table, pos_cols, slot, parity, rows):
    depth, share = pieces[0].shape[1:]
    units, width = weights_t.shape[0] // 4, weights_t.shape[1]
    blocks = pos_cols.shape[0] // depth
    return pl.pallas_call(
        functools.partial(hidden_kernel, slot * 2 + parity),
        grid_spec=pltpu.PrefetchScalarGridSpec(
            num_scalar_prefetch=1,
            grid=(blocks // 2,),
            in_specs=[
                pl.BlockSpec((2 * depth, pos_cols.shape[1]), lambda i, t: (i, 0)),
                pl.BlockSpec((2 * units, width), lambda i, t: (slot, 0)),
            ]
            + [pl.BlockSpec(memory_space=pl.ANY)] * len(pieces),
            out_specs=pl.BlockSpec((units, rows), lambda i, t: (0, 0)),
            scratch_shapes=[
                pltpu.VMEM((blocks, depth, width), BF16),
                pltpu.VMEM((units, rows), F32),
                pltpu.SemaphoreType.DMA((blocks // 2,)),
            ],
        ),
        out_shape=jax.ShapeDtypeStruct((units, rows), BF16),
        compiler_params=pltpu.CompilerParams(vmem_limit_bytes=HIDDEN_VMEM_LIMIT),
        cost_estimate=pl.CostEstimate(
            flops=4 * units * width * blocks * depth,
            bytes_accessed=2 * (2 * units * width + blocks * depth * width),
            transcendentals=units * blocks * depth,
        ),
        name="hidden",
    )(table, pos_cols, weights_t, *pieces)


def scaled_kernel(column, pos_ref, w_ref, c_ref, o_ref):
    scaled = (w_ref[:, column : column + 1] * c_ref[...].astype(F32)).astype(BF16)
    rows = o_ref.shape[0]
    row = lax.broadcasted_iota(jnp.int32, (rows, c_ref.shape[0]), 0)
    chosen = one_hot(pos_ref[column : column + 1, :] == row)
    o_ref[...] = jnp.dot(chosen, scaled, preferred_element_type=F32).astype(BF16)


def scaled_call(cotangents, pos_rows, weight_cols, slot, parity, rows):
    count, share = cotangents.shape
    return pl.pallas_call(
        functools.partial(scaled_kernel, slot * 2 + parity),
        out_shape=jax.ShapeDtypeStruct((rows, share), BF16),
        compiler_params=pltpu.CompilerParams(vmem_limit_bytes=VMEM_LIMIT),
        cost_estimate=pl.CostEstimate(
            flops=2 * count * share * rows,
            bytes_accessed=2 * share * (count + rows),
            transcendentals=0,
        ),
        name="scaled",
    )(pos_rows, weight_cols, cotangents)


def load_hidden(units, table, refs, hidden, sems, begin=0):
    columns = pl.ds(begin, hidden.shape[1])
    copies = []
    for place, ref in enumerate(refs):
        start = pl.multiple_of(table[place] * units, units)
        copies.append(
            pltpu.make_async_copy(
                ref.at[:, columns], hidden.at[pl.ds(start, units)], sems.at[place]
            )
        )
    for copy in copies:
        copy.start()
    for copy in copies:
        copy.wait()


def gradient_tile(hidden, a_ref, b_ref, tile):
    start = pl.multiple_of(pl.program_id(0) * tile, tile)
    half = a_ref.shape[0]
    return jnp.dot(
        hidden[pl.ds(start, tile), :half], a_ref[...], preferred_element_type=F32
    ) + jnp.dot(hidden[pl.ds(start, tile), half:], b_ref[...], preferred_element_type=F32)


def replica_gradient_kernel(units, table, a_ref, b_ref, *refs):
    pieces, (o_ref, hidden, sems) = refs[:-3], refs[-3:]

    @pl.when(pl.program_id(0) == 0)
    def _():
        load_hidden(units, table, pieces, hidden, sems)

    o_ref[...] = gradient_tile(hidden, a_ref, b_ref, o_ref.shape[0]).astype(BF16)


def replica_gradient_call(pieces, scaled, table):
    units, rows = pieces[0].shape
    half, share = scaled[0].shape
    total = 8 * units
    tile = 512
    return pl.pallas_call(
        functools.partial(replica_gradient_kernel, units),
        grid_spec=pltpu.PrefetchScalarGridSpec(
            num_scalar_prefetch=1,
            grid=(total // tile,),
            in_specs=[pl.BlockSpec((half, share), lambda i, t: (0, 0))] * 2
            + [pl.BlockSpec(memory_space=pl.ANY)] * len(pieces),
            out_specs=pl.BlockSpec((tile, share), lambda i, t: (i, 0)),
            scratch_shapes=[
                pltpu.VMEM((total, rows), BF16),
                pltpu.SemaphoreType.DMA((len(pieces),)),
            ],
        ),
        out_shape=jax.ShapeDtypeStruct((total, share), BF16),
        compiler_params=pltpu.CompilerParams(vmem_limit_bytes=VMEM_LIMIT),
        cost_estimate=pl.CostEstimate(
            flops=2 * total * rows * share,
            bytes_accessed=2 * (total * rows + rows * share + total * share),
            transcendentals=0,
        ),
        name="replica_gradient",
    )(table, *scaled, *pieces)


def update_kernel(units, table, a_ref, b_ref, total_ref, one_ref, two_ref, down_ref, *refs):
    pieces = refs[:-5]
    down_out, one_out, two_out, hidden, sems = refs[-5:]

    @pl.when(pl.program_id(0) == 0)
    def _():
        load_hidden(units, table, pieces, hidden, sems)

    gradient = gradient_tile(hidden, a_ref, b_ref, down_out.shape[0]) + total_ref[...].astype(F32)
    one = beta_one * one_ref[...] + (1.0 - beta_one) * gradient
    two = beta_two * two_ref[...] + (1.0 - beta_two) * gradient * gradient
    one_out[...] = one
    two_out[...] = two
    update = (learn_rate / correct_one) * one / (jnp.sqrt(two * (1.0 / correct_two)) + epsilon)
    down_out[...] = (
        down_ref[...].astype(F32) * (1.0 - learn_rate * weight_decay) - update
    ).astype(BF16)


def update_call(pieces, scaled, table, total_gradient, moment1, moment2, down):
    units, rows = pieces[0].shape
    half, share = scaled[0].shape
    total = 8 * units
    tile = 256
    block = pl.BlockSpec((tile, share), lambda i, t: (i, 0))
    return pl.pallas_call(
        functools.partial(update_kernel, units),
        grid_spec=pltpu.PrefetchScalarGridSpec(
            num_scalar_prefetch=1,
            grid=(total // tile,),
            in_specs=[pl.BlockSpec((half, share), lambda i, t: (0, 0))] * 2
            + [block] * 4
            + [pl.BlockSpec(memory_space=pl.ANY)] * len(pieces),
            out_specs=[block] * 3,
            scratch_shapes=[
                pltpu.VMEM((total, rows), BF16),
                pltpu.SemaphoreType.DMA((len(pieces),)),
            ],
        ),
        out_shape=[
            jax.ShapeDtypeStruct((total, share), BF16),
            jax.ShapeDtypeStruct((total, share), F32),
            jax.ShapeDtypeStruct((total, share), F32),
        ],
        compiler_params=pltpu.CompilerParams(vmem_limit_bytes=VMEM_LIMIT),
        cost_estimate=pl.CostEstimate(
            flops=2 * total * rows * share,
            bytes_accessed=2 * total * rows + 22 * total * share,
            transcendentals=total * share,
        ),
        name="update",
    )(table, *scaled, total_gradient, moment1, moment2, down, *pieces)


def output_kernel(parity, column, units, with_prior, table, down_ref, pos_ref, w_ref, *refs):
    if with_prior:
        prior_ref, refs = refs[0], refs[1:]
    pieces = refs[:-4]
    o_ref, hidden, outputs, sems = refs[-4:]
    rows = hidden.shape[1]
    load_hidden(units, table, pieces, hidden, sems, parity * rows)
    for begin in range(0, rows, 256):
        outputs[begin : begin + 256, :] = lax.dot_general(
            hidden[:, begin : begin + 256], down_ref[...], TN, preferred_element_type=F32
        ).astype(BF16)
    tile = 256
    for begin in range(0, o_ref.shape[0], tile):
        window = slice(begin, begin + tile)
        target = lax.broadcasted_iota(jnp.int32, (tile, rows), 1)
        chosen = one_hot(pos_ref[window, column : column + 1] == target)
        picked = jnp.dot(chosen, outputs[...], preferred_element_type=F32)
        value = w_ref[window, column : column + 1] * picked
        if with_prior:
            value = value + prior_ref[window, :]
        o_ref[window, :] = value.astype(o_ref.dtype)


def output_call(pieces, down, table, pos_cols, weight_cols, slot, parity, prior):
    units, both = pieces[0].shape
    rows = both // 2
    total, share = down.shape
    count = pos_cols.shape[0]
    vmem = pl.BlockSpec(memory_space=pltpu.VMEM)
    extra = [] if prior is None else [prior]
    return pl.pallas_call(
        functools.partial(output_kernel, parity, slot * 2 + parity, units, prior is not None),
        in_specs=[pl.BlockSpec(memory_space=pltpu.SMEM)]
        + [vmem] * (3 + len(extra))
        + [pl.BlockSpec(memory_space=pl.ANY)] * len(pieces),
        out_specs=vmem,
        scratch_shapes=[
            pltpu.VMEM((total, rows), BF16),
            pltpu.VMEM((rows, share), BF16),
            pltpu.SemaphoreType.DMA((len(pieces),)),
        ],
        out_shape=jax.ShapeDtypeStruct((count, share), F32 if prior is None else BF16),
        compiler_params=pltpu.CompilerParams(vmem_limit_bytes=VMEM_LIMIT),
        cost_estimate=pl.CostEstimate(
            flops=2 * total * rows * share + 2 * count * rows * share,
            bytes_accessed=2 * (total * rows + total * share) + 6 * count * share,
            transcendentals=0,
        ),
        name="output",
    )(table, down, pos_cols, weight_cols, *extra, *pieces)


def per_device(
    tokens,
    cotangent,
    router_weights,
    routes,
    replica_map,
    gate_primary,
    up_primary,
    down_primary,
    gate_replica,
    up_replica,
    down_replica,
    moment1,
    moment2,
):
    groups = lax.axis_size("ep")
    count, top = routes.shape
    hidden_units, share = down_primary.shape[1:]
    half_groups = groups // 2
    rows = half_groups * (3 * count * top // (2 * groups))
    ep = lax.axis_index("ep")
    rep = lax.axis_index("rep")
    core = ep % 2

    line = gather_ring(tokens[None], "xx")
    cot_line = together(cotangent, *[move_ep(cotangent, 0, dr) for dr in range(1, RING)])
    line, cot_line = together(jnp.concatenate(line, axis=0), cot_line)
    cot_line = jnp.concatenate(cot_line, axis=0)
    plane = gather_ring(line, "zy")
    cot_own = jnp.concatenate([cot_line, move_ep(cot_line, 1, 0)], axis=0)
    low, high = jnp.concatenate(plane[:2], axis=0), jnp.concatenate(plane[2:], axis=0)
    low, high, cot_own = together(low, high, cot_own)
    below_low = move_torus(low, "yz", 3)
    above_high = move_torus(high, "yz", 1)
    cot_other = swap_core(cot_own)
    cot_halves = [cot_own, cot_other]

    slot_ids = jnp.arange(2 * groups, dtype=jnp.int32)
    dense = jnp.sum(
        jnp.where(routes[None] == slot_ids[:, None, None], router_weights[None], 0.0), axis=2
    ).reshape(groups, 2, count)
    served = lax.all_to_all(
        after(dense, low), "ep", split_axis=0, concat_axis=0, tiled=True
    )
    x, y, z = 2 * (rep // 4) + ep // 8, rep % 4, (ep // 2) % 4
    slots = np.arange(half_groups, dtype=np.int32)
    blocks = 2 * ((((ep // 8) + slots // RING) % 2) * RING + (z + slots % RING) % RING)
    served = served[jnp.concatenate([blocks + core, blocks + 1 - core])]
    served = jnp.transpose(served.reshape(2, half_groups, 2, count), (2, 0, 1, 3)).reshape(
        4, half_groups, count
    )
    hit = (served != 0.0).astype(F32)
    earlier = jnp.triu(jnp.ones((count, count), F32), 1)
    blocks_before = jnp.triu(jnp.ones((half_groups, half_groups), F32), 1)
    inside = jnp.einsum("lbt,tu->lbu", hit, earlier, precision=lax.Precision.HIGHEST)
    before = jnp.einsum(
        "lb,bc->lc", jnp.sum(hit, axis=2), blocks_before, precision=lax.Precision.HIGHEST
    )
    pos_rows = jnp.where(hit > 0, (inside + before[:, :, None]).astype(jnp.int32), -1)
    pos_rows = pos_rows.reshape(4, half_groups * count)
    pos_cols = pos_rows.T
    weight_cols = served.reshape(4, half_groups * count).T
    weights_t = jnp.concatenate(
        [gate_primary[0].T, up_primary[0].T, gate_replica[0].T, up_replica[0].T], axis=0
    )

    offsets = np.array(OFFSETS, np.int32)

    def part_table(kind):
        from_y = (y + jnp.where(kind == 0, offsets[:, 2], offsets[:, 1])) % RING
        part = (((x + offsets[:, 0]) % RING) // 2) * RING + from_y
        return jnp.concatenate([part, kind[None]]).astype(jnp.int32)

    own_table, other_table = part_table(core), part_table(1 - core)
    rep_pair, rep_ring = rep // RING, rep % RING
    order = np.array(ORDER, np.int32)
    places = ((rep_pair ^ order[:, 0]) * RING + (rep_ring + order[:, 1]) % RING).astype(jnp.int32)

    low_other, high_other = swap_core(low), swap_core(high)
    below_low, above_high, weights_t = together(below_low, above_high, weights_t)
    below_high = move_torus(high, "yz", 3)
    above_low = move_torus(low, "yz", 1)
    far_low = move_torus(below_low, "yz", 3)
    far_high = move_torus(above_high, "yz", 1)
    below_low_other, above_high_other = swap_core(below_low), swap_core(above_high)

    def scale(slot):
        return [
            scaled_call(cot_halves[parity], pos_rows, weight_cols, slot, parity, rows)
            for parity in range(2)
        ]

    scaled_replica, scaled_primary = scale(1), scale(0)
    (
        below_high,
        above_low,
        far_low,
        far_high,
        scaled_replica,
        scaled_primary,
        pos_cols,
        weight_cols,
        own_table,
        other_table,
        places,
    ) = together(
        below_high,
        above_low,
        far_low,
        far_high,
        scaled_replica,
        scaled_primary,
        pos_cols,
        weight_cols,
        own_table,
        other_table,
        places,
    )
    own_pieces = [low, high, below_low, above_high, below_high, above_low, far_low, far_high]
    other_pieces = [low_other, high_other, below_low_other, above_high_other] + [
        swap_core(piece) for piece in own_pieces[4:]
    ]

    def own_hidden(slot, weights):
        return hidden_call(weights, own_pieces, own_table, pos_cols, slot, 0, rows)

    def other_hidden(slot, weights):
        return hidden_call(weights, other_pieces, other_table, pos_cols, slot, 1, rows)

    def first_level(hidden):
        return [move_rep(hidden, dp, dr) for dp, dr in ((0, 2), (0, 3), (0, 1), (1, 0))]

    def second_level(far, across):
        return [move_rep(across, 0, 3), move_rep(across, 0, 1), move_rep(far, 1, 0)]

    replica_hidden = own_hidden(1, weights_t)
    replica_hidden = jnp.concatenate(
        [replica_hidden, other_hidden(1, after(weights_t, replica_hidden))], axis=1
    )
    near = first_level(replica_hidden)

    shares = after(down_primary[0], replica_hidden).reshape(
        groups, hidden_units // groups, share
    )
    spread_weights = lax.all_to_all(shares, "ep", split_axis=0, concat_axis=0, tiled=True)

    primary_hidden = own_hidden(0, after(weights_t, replica_hidden))
    near, primary_hidden, spread_weights = together(near, primary_hidden, spread_weights)
    away = second_level(near[0], near[3])
    primary_hidden = jnp.concatenate(
        [primary_hidden, other_hidden(0, after(weights_t, primary_hidden))], axis=1
    )
    away, near, primary_hidden = together(away, near, primary_hidden)
    replica_pieces = [replica_hidden, near[1], near[2], near[3], near[0], *away]

    near = first_level(primary_hidden)
    replica_gradient = replica_gradient_call(replica_pieces, scaled_replica, places)
    spread = lax.all_to_all(
        replica_gradient.reshape(groups, hidden_units // groups, share),
        "ep",
        split_axis=0,
        concat_axis=0,
        tiled=True,
    )
    prior_other = output_call(
        replica_pieces,
        after(down_replica[0], replica_gradient),
        places,
        pos_cols,
        weight_cols,
        1,
        1,
        None,
    )
    near, prior_other = together(near, prior_other)
    away = second_level(near[0], near[3])
    prior_own = output_call(
        replica_pieces,
        after(down_replica[0], prior_other),
        places,
        pos_cols,
        weight_cols,
        1,
        0,
        None,
    )
    chosen = jnp.take(after(spread_weights, prior_other), replica_map, axis=0)
    spread, prior_own, chosen = together(spread, prior_own, chosen)
    owners = (replica_map[None, :] == jnp.arange(groups, dtype=jnp.int32)[:, None]).astype(BF16)
    summed = jnp.einsum("pj,jfd->pfd", owners, spread, preferred_element_type=F32).astype(BF16)
    replica_total = lax.all_to_all(
        summed, "ep", split_axis=0, concat_axis=0, tiled=True
    ).reshape(hidden_units, share)
    away, near, summed = together(away, near, summed)
    primary_pieces = [primary_hidden, near[1], near[2], near[3], near[0], *away]

    theirs = output_call(
        primary_pieces, down_primary[0], places, pos_cols, weight_cols, 0, 1, prior_other
    )
    arrived = swap_core(theirs)
    mine = output_call(
        primary_pieces,
        after(down_primary[0], theirs),
        places,
        pos_cols,
        weight_cols,
        0,
        0,
        prior_own,
    )
    mine = (mine.astype(F32) + arrived.astype(F32)).astype(BF16).reshape(half_groups, count, share)
    layer = mine[0].astype(F32)
    for number in range(1, half_groups):
        layer = layer + move_ep(mine[number], number // RING, -(number % RING)).astype(F32)

    replica_total, chosen = together(replica_total, chosen)
    refreshed = lax.all_to_all(chosen, "ep", split_axis=0, concat_axis=0, tiled=True).reshape(
        1, hidden_units, share
    )
    down_new, moment1_new, moment2_new = update_call(
        primary_pieces,
        scaled_primary,
        places,
        replica_total,
        moment1[0],
        moment2[0],
        down_primary[0],
    )
    return (layer.astype(BF16), down_new[None], moment1_new[None], moment2_new[None], refreshed)


def solution(mesh):
    return jax.shard_map(
        per_device,
        mesh=mesh,
        in_specs=(
            P("ep", "rep"),
            P("ep", "rep"),
            P("ep", None),
            P("ep", None),
            P(),
            P("ep", None, "rep"),
            P("ep", None, "rep"),
            P("ep", None, "rep"),
            P("ep", None, "rep"),
            P("ep", None, "rep"),
            P("ep", None, "rep"),
            P("ep", None, "rep"),
            P("ep", None, "rep"),
        ),
        out_specs=(
            P("ep", "rep"),
            P("ep", None, "rep"),
            P("ep", None, "rep"),
            P("ep", None, "rep"),
            P("ep", None, "rep"),
        ),
        check_vma=False,
    )
```

```python
import functools

import jax
import jax.numpy as jnp
import numpy as np
from jax import lax
from jax.experimental import pallas as pl
from jax.experimental.pallas import tpu as pltpu
from jax.sharding import PartitionSpec as P

beta_one = 0.9
beta_two = 0.95
learn_rate = 0.001
weight_decay = 0.1
epsilon = 1e-08
correct_one = 1.0 - 0.9**10
correct_two = 1.0 - 0.95**10

BF16 = jnp.bfloat16
F32 = jnp.float32
NT = (((1,), (1,)), ((), ()))
TN = (((0,), (0,)), ((), ()))
VMEM_LIMIT = 58 * 1024 * 1024
HIDDEN_VMEM_LIMIT = 20 * 1024 * 1024
SCALED_VMEM_LIMIT = 12 * 1024 * 1024
SMALL_COST = pl.CostEstimate(flops=1000, bytes_accessed=1000, transcendentals=0)


ORDER = [(0, 0), (0, 3), (0, 1), (1, 0), (0, 2), (1, 3), (1, 1), (1, 2)]
RING = 4


def torus_place(i):
    ep, rep = i // 8, i % 8
    return 2 * (rep // 4) + ep // 8, rep % 4, (ep // 2) % 4, ep % 2


def torus_index(x, y, z, core):
    return (((x % 2) * 4 + z % 4) * 2 + core) * 8 + (x // 2) * 4 + y % 4


def torus_perm(axes, offset):
    perm = []
    for i in range(128):
        place = list(torus_place(i))
        axis = "xyz".index(axes[place[3]])
        place[axis] = (place[axis] - offset) % RING
        perm.append((i, torus_index(*place)))
    return perm


def move_torus(x, axes, offset):
    return lax.ppermute(x, ("ep", "rep"), torus_perm(axes, offset))


def move_rep(x, pair_offset, ring_offset):
    perm = []
    for i in range(8):
        pair, ring = (i // RING) ^ pair_offset, (i % RING - ring_offset) % RING
        perm.append((i, pair * RING + ring))
    return lax.ppermute(x, "rep", perm)


def move_ep(x, pair_offset, ring_offset):
    perm = []
    for i in range(16):
        pair, ring = (i // 8) ^ pair_offset, ((i // 2) % RING - ring_offset) % RING
        perm.append((i, (pair * RING + ring) * 2 + i % 2))
    return lax.ppermute(x, "ep", perm)


def swap_core(x):
    return lax.ppermute(x, "ep", [(i, i ^ 1) for i in range(16)])


def together(*values):
    return lax.optimization_barrier(values)


def after(value, *others):
    return lax.optimization_barrier((value, others))[0]


RINGS = [0, 3, 1, 2]


def gather_ring(x, axes):
    return together(x, *[move_torus(x, axes, offset) for offset in RINGS[1:]])


HALVES = [(0, 0), (0, 1), (3, 0), (1, 1), (3, 1), (1, 0), (2, 0), (2, 1)]
OFFSETS = [
    (first, second, last)
    for last, half in HALVES
    for second in RINGS[2 * half : 2 * half + 2]
    for first in RINGS
]


def block_slot(number, kind):
    first, second, last = OFFSETS[number]
    return (first % 2) * RING + (second if kind == 0 else last)


def one_hot(mask):
    return jnp.where(mask, 1.0, 0.0).astype(BF16)


def hidden_kernel(column, table, pos_ref, w_ref, *refs):
    pieces = refs[:-4]
    o_ref, x_ref, total_ref, sems = refs[-4:]
    step = pl.program_id(0)
    blocks, depth, width = x_ref.shape
    per_piece, _, share = pieces[0].shape

    @pl.when(step == 0)
    def _():
        for kind in range(2):

            @pl.when(table[len(OFFSETS)] == kind)
            def _():
                for number in sorted(range(len(OFFSETS)), key=lambda n: block_slot(n, kind)):
                    slot = block_slot(number, kind)
                    start = pl.multiple_of(table[number] * share, share)
                    pltpu.make_async_copy(
                        pieces[number // per_piece].at[number % per_piece],
                        x_ref.at[slot, :, pl.ds(start, share)],
                        sems.at[slot // 2],
                    ).start()

    ready = x_ref.at[pl.ds(2 * step, 2)]
    pltpu.make_async_copy(ready, ready, sems.at[step]).wait()
    tokens = x_ref[pl.ds(2 * step, 2)].reshape(2 * depth, width)
    sums = lax.dot_general(w_ref[...], tokens, NT, preferred_element_type=F32)
    units = o_ref.shape[0]
    hidden = (jax.nn.silu(sums[:units]) * sums[units:]).astype(BF16)
    target = lax.broadcasted_iota(jnp.int32, (2 * depth, o_ref.shape[1]), 1)
    chosen = one_hot(pos_ref[:, column : column + 1] == target)
    picked = jnp.dot(hidden, chosen, preferred_element_type=F32)

    @pl.when(step == 0)
    def _():
        total_ref[...] = picked

    @pl.when(step > 0)
    def _():
        total_ref[...] += picked

    @pl.when(step == pl.num_programs(0) - 1)
    def _():
        o_ref[...] = total_ref[...].astype(BF16)


def hidden_call(weights_t, pieces, table, pos_cols, slot, parity, rows):
    depth, share = pieces[0].shape[1:]
    units, width = weights_t.shape[0] // 2, weights_t.shape[1]
    blocks = pos_cols.shape[0] // depth
    return pl.pallas_call(
        functools.partial(hidden_kernel, slot * 2 + parity),
        grid_spec=pltpu.PrefetchScalarGridSpec(
            num_scalar_prefetch=1,
            grid=(blocks // 2,),
            in_specs=[
                pl.BlockSpec((2 * depth, pos_cols.shape[1]), lambda i, t: (i, 0)),
                pl.BlockSpec((2 * units, width), lambda i, t: (0, 0)),
            ]
            + [pl.BlockSpec(memory_space=pl.ANY)] * len(pieces),
            out_specs=pl.BlockSpec((units, rows), lambda i, t: (0, 0)),
            scratch_shapes=[
                pltpu.VMEM((blocks, depth, width), BF16),
                pltpu.VMEM((units, rows), F32),
                pltpu.SemaphoreType.DMA((blocks // 2,)),
            ],
        ),
        out_shape=jax.ShapeDtypeStruct((units, rows), BF16),
        compiler_params=pltpu.CompilerParams(vmem_limit_bytes=HIDDEN_VMEM_LIMIT if slot else VMEM_LIMIT),
        cost_estimate=SMALL_COST,
        name="hidden",
    )(table, pos_cols, weights_t, *pieces)


def scaled_kernel(column, pos_ref, w_ref, c_ref, o_ref):
    scaled = (w_ref[:, column : column + 1] * c_ref[...].astype(F32)).astype(BF16)
    rows = o_ref.shape[0]
    row = lax.broadcasted_iota(jnp.int32, (rows, c_ref.shape[0]), 0)
    chosen = one_hot(pos_ref[column : column + 1, :] == row)
    o_ref[...] = jnp.dot(chosen, scaled, preferred_element_type=F32).astype(BF16)


def scaled_call(cotangents, pos_rows, weight_cols, slot, parity, rows):
    count, share = cotangents.shape
    return pl.pallas_call(
        functools.partial(scaled_kernel, slot * 2 + parity),
        out_shape=jax.ShapeDtypeStruct((rows, share), BF16),
        compiler_params=pltpu.CompilerParams(vmem_limit_bytes=SCALED_VMEM_LIMIT),
        cost_estimate=SMALL_COST,
        name="scaled",
    )(pos_rows, weight_cols, cotangents)


def load_hidden(units, table, refs, hidden, sems):
    copies = []
    for place, ref in enumerate(refs):
        start = pl.multiple_of(table[place] * units, units)
        copies.append(
            pltpu.make_async_copy(
                ref, hidden.at[pl.ds(start, units)], sems.at[place]
            )
        )
    for copy in copies:
        copy.start()
    for copy in copies:
        copy.wait()


def gradient_tile(hidden, a_ref, b_ref, tile):
    start = pl.multiple_of(pl.program_id(0) * tile, tile)
    half = a_ref.shape[0]
    return jnp.dot(
        hidden[pl.ds(start, tile), :half], a_ref[...], preferred_element_type=F32
    ) + jnp.dot(hidden[pl.ds(start, tile), half:], b_ref[...], preferred_element_type=F32)


def replica_gradient_kernel(units, table, a_ref, b_ref, *refs):
    pieces, (o_ref, hidden, sems) = refs[:-3], refs[-3:]

    @pl.when(pl.program_id(0) == 0)
    def _():
        load_hidden(units, table, pieces, hidden, sems)

    o_ref[...] = gradient_tile(hidden, a_ref, b_ref, o_ref.shape[0]).astype(BF16)


def replica_gradient_call(pieces, scaled, table):
    units, rows = pieces[0].shape
    half, share = scaled[0].shape
    total = 8 * units
    tile = 512
    return pl.pallas_call(
        functools.partial(replica_gradient_kernel, units),
        grid_spec=pltpu.PrefetchScalarGridSpec(
            num_scalar_prefetch=1,
            grid=(total // tile,),
            in_specs=[pl.BlockSpec((half, share), lambda i, t: (0, 0))] * 2
            + [pl.BlockSpec(memory_space=pl.ANY)] * len(pieces),
            out_specs=pl.BlockSpec((tile, share), lambda i, t: (i, 0)),
            scratch_shapes=[
                pltpu.VMEM((total, rows), BF16),
                pltpu.SemaphoreType.DMA((len(pieces),)),
            ],
        ),
        out_shape=jax.ShapeDtypeStruct((total, share), BF16),
        compiler_params=pltpu.CompilerParams(vmem_limit_bytes=VMEM_LIMIT),
        cost_estimate=SMALL_COST,
        name="replica_gradient",
    )(table, *scaled, *pieces)


def update_kernel(units, table, a_ref, b_ref, total_ref, one_ref, two_ref, down_ref, *refs):
    pieces = refs[:-5]
    down_out, one_out, two_out, hidden, sems = refs[-5:]

    @pl.when(pl.program_id(0) == 0)
    def _():
        load_hidden(units, table, pieces, hidden, sems)

    gradient = gradient_tile(hidden, a_ref, b_ref, down_out.shape[0]) + total_ref[...].astype(F32)
    one = beta_one * one_ref[...] + (1.0 - beta_one) * gradient
    two = beta_two * two_ref[...] + (1.0 - beta_two) * gradient * gradient
    one_out[...] = one
    two_out[...] = two
    update = (learn_rate / correct_one) * one / (jnp.sqrt(two * (1.0 / correct_two)) + epsilon)
    down_out[...] = (
        down_ref[...].astype(F32) * (1.0 - learn_rate * weight_decay) - update
    ).astype(BF16)


def update_call(pieces, scaled, table, total_gradient, moment1, moment2, down):
    units, rows = pieces[0].shape
    half, share = scaled[0].shape
    total = 8 * units
    tile = 256
    block = pl.BlockSpec((tile, share), lambda i, t: (i, 0))
    return pl.pallas_call(
        functools.partial(update_kernel, units),
        grid_spec=pltpu.PrefetchScalarGridSpec(
            num_scalar_prefetch=1,
            grid=(total // tile,),
            in_specs=[pl.BlockSpec((half, share), lambda i, t: (0, 0))] * 2
            + [block] * 4
            + [pl.BlockSpec(memory_space=pl.ANY)] * len(pieces),
            out_specs=[block] * 3,
            scratch_shapes=[
                pltpu.VMEM((total, rows), BF16),
                pltpu.SemaphoreType.DMA((len(pieces),)),
            ],
        ),
        out_shape=[
            jax.ShapeDtypeStruct((total, share), BF16),
            jax.ShapeDtypeStruct((total, share), F32),
            jax.ShapeDtypeStruct((total, share), F32),
        ],
        compiler_params=pltpu.CompilerParams(vmem_limit_bytes=VMEM_LIMIT),
        cost_estimate=SMALL_COST,
        name="update",
    )(table, *scaled, total_gradient, moment1, moment2, down, *pieces)


def output_kernel(slot, units, with_prior, table, down_ref, pos_ref, w_ref, *refs):
    if with_prior:
        priors, refs = refs[:2], refs[2:]
    pieces = refs[:-5]
    results, (hidden, outputs, sems) = refs[-5:-3], refs[-3:]
    rows = hidden.shape[1] // 2
    load_hidden(units, table, pieces, hidden, sems)
    tile = 256
    for half in (1, 0):
        column = slot * 2 + half
        o_ref = results[half]
        for begin in range(half * rows, (half + 1) * rows, 256):
            outputs[begin : begin + 256, :] = lax.dot_general(
                hidden[:, begin : begin + 256], down_ref[...], TN, preferred_element_type=F32
            ).astype(BF16)
        for begin in range(0, o_ref.shape[0], tile):
            window = slice(begin, begin + tile)
            target = lax.broadcasted_iota(jnp.int32, (tile, rows), 1)
            chosen = one_hot(pos_ref[window, column : column + 1] == target)
            picked = jnp.dot(
                chosen, outputs[half * rows : (half + 1) * rows, :], preferred_element_type=F32
            )
            value = w_ref[window, column : column + 1] * picked
            if with_prior:
                value = value + priors[half][window, :]
            o_ref[window, :] = value.astype(o_ref.dtype)


def output_call(pieces, down, table, pos_cols, weight_cols, slot, priors):
    units, both = pieces[0].shape
    total, share = down.shape
    count = pos_cols.shape[0]
    vmem = pl.BlockSpec(memory_space=pltpu.VMEM)
    result = jax.ShapeDtypeStruct((count, share), BF16 if priors else F32)
    return pl.pallas_call(
        functools.partial(output_kernel, slot, units, bool(priors)),
        in_specs=[pl.BlockSpec(memory_space=pltpu.SMEM)]
        + [vmem] * (3 + len(priors))
        + [pl.BlockSpec(memory_space=pl.ANY)] * len(pieces),
        out_specs=[vmem] * 2,
        scratch_shapes=[
            pltpu.VMEM((total, both), BF16),
            pltpu.VMEM((both, share), BF16),
            pltpu.SemaphoreType.DMA((len(pieces),)),
        ],
        out_shape=[result] * 2,
        compiler_params=pltpu.CompilerParams(vmem_limit_bytes=VMEM_LIMIT),
        cost_estimate=pl.CostEstimate(
            flops=2 * total * both * share + 2 * count * both * share,
            bytes_accessed=2 * (total * both + total * share) + 12 * count * share,
            transcendentals=0,
        ),
        name="output",
    )(table, down, pos_cols, weight_cols, *priors, *pieces)


def per_device(
    tokens,
    cotangent,
    router_weights,
    routes,
    replica_map,
    gate_primary,
    up_primary,
    down_primary,
    gate_replica,
    up_replica,
    down_replica,
    moment1,
    moment2,
):
    groups = lax.axis_size("ep")
    count, top = routes.shape
    hidden_units, share = down_primary.shape[1:]
    half_groups = groups // 2
    rows = half_groups * (3 * count * top // (2 * groups))
    ep = lax.axis_index("ep")
    rep = lax.axis_index("rep")
    core = ep % 2

    line = gather_ring(tokens[None], "xx")
    cot_line = together(cotangent, *[move_ep(cotangent, 0, dr) for dr in range(1, RING)])
    line, cot_line = together(jnp.concatenate(line, axis=0), cot_line)
    cot_line = jnp.concatenate(cot_line, axis=0)
    plane = gather_ring(line, "zy")
    cot_own = jnp.concatenate([cot_line, move_ep(cot_line, 1, 0)], axis=0)
    low, high = jnp.concatenate(plane[:2], axis=0), jnp.concatenate(plane[2:], axis=0)
    low, high, cot_own = together(low, high, cot_own)
    below_low = move_torus(low, "yz", 3)
    above_high = move_torus(high, "yz", 1)
    cot_other = swap_core(cot_own)
    cot_halves = [cot_own, cot_other]

    slot_ids = jnp.arange(2 * groups, dtype=jnp.int32)
    dense = jnp.sum(
        jnp.where(routes[None] == slot_ids[:, None, None], router_weights[None], 0.0), axis=2
    ).reshape(groups, 2, count)
    served = lax.all_to_all(
        after(dense, low), "ep", split_axis=0, concat_axis=0, tiled=True
    )
    x, y, z = 2 * (rep // 4) + ep // 8, rep % 4, (ep // 2) % 4
    slots = np.arange(half_groups, dtype=np.int32)
    blocks = 2 * ((((ep // 8) + slots // RING) % 2) * RING + (z + slots % RING) % RING)
    served = served[jnp.concatenate([blocks + core, blocks + 1 - core])]
    served = jnp.transpose(served.reshape(2, half_groups, 2, count), (2, 0, 1, 3)).reshape(
        4, half_groups, count
    )
    hit = (served != 0.0).astype(F32)
    earlier = jnp.triu(jnp.ones((count, count), F32), 1)
    blocks_before = jnp.triu(jnp.ones((half_groups, half_groups), F32), 1)
    inside = jnp.einsum("lbt,tu->lbu", hit, earlier, precision=lax.Precision.HIGHEST)
    before = jnp.einsum(
        "lb,bc->lc", jnp.sum(hit, axis=2), blocks_before, precision=lax.Precision.HIGHEST
    )
    pos_rows = jnp.where(hit > 0, (inside + before[:, :, None]).astype(jnp.int32), -1)
    pos_rows = pos_rows.reshape(4, half_groups * count)
    pos_cols = pos_rows.T
    weight_cols = served.reshape(4, half_groups * count).T
    weights_t = [
        jnp.concatenate([gate[0].T, up[0].T], axis=0)
        for gate, up in after(((gate_primary, up_primary), (gate_replica, up_replica)), low)
    ]

    offsets = np.array(OFFSETS, np.int32)

    def part_table(kind):
        from_y = (y + jnp.where(kind == 0, offsets[:, 2], offsets[:, 1])) % RING
        part = (((x + offsets[:, 0]) % RING) // 2) * RING + from_y
        return jnp.concatenate([part, kind[None]]).astype(jnp.int32)

    own_table, other_table = part_table(core), part_table(1 - core)
    rep_pair, rep_ring = rep // RING, rep % RING
    order = np.array(ORDER, np.int32)
    places = ((rep_pair ^ order[:, 0]) * RING + (rep_ring + order[:, 1]) % RING).astype(jnp.int32)

    low_other, high_other = swap_core(low), swap_core(high)
    below_low, above_high, weights_t, pos_cols = together(
        below_low, above_high, weights_t, pos_cols
    )
    below_high = move_torus(high, "yz", 3)
    above_low = move_torus(low, "yz", 1)
    far_low = move_torus(below_low, "yz", 3)
    far_high = move_torus(above_high, "yz", 1)
    below_low_other, above_high_other = swap_core(below_low), swap_core(above_high)

    def scale(slot):
        return [
            scaled_call(cot_halves[parity], pos_rows, weight_cols, slot, parity, rows)
            for parity in range(2)
        ]

    scaled_replica, scaled_primary = scale(1), scale(0)
    (
        below_high,
        above_low,
        far_low,
        far_high,
        scaled_replica,
        scaled_primary,
        pos_cols,
        weight_cols,
        own_table,
        other_table,
        places,
    ) = together(
        below_high,
        above_low,
        far_low,
        far_high,
        scaled_replica,
        scaled_primary,
        pos_cols,
        weight_cols,
        own_table,
        other_table,
        places,
    )
    own_pieces = [low, high, below_low, above_high, below_high, above_low, far_low, far_high]
    other_pieces = [low_other, high_other, below_low_other, above_high_other] + [
        swap_core(piece) for piece in own_pieces[4:]
    ]

    def own_hidden(slot, weights):
        return hidden_call(weights, own_pieces, own_table, pos_cols, slot, 0, rows)

    def other_hidden(slot, weights):
        return hidden_call(weights, other_pieces, other_table, pos_cols, slot, 1, rows)

    def first_level(hidden):
        return [move_rep(hidden, dp, dr) for dp, dr in ((0, 2), (0, 3), (0, 1), (1, 0))]

    def second_level(far, across):
        return [move_rep(across, 0, 3), move_rep(across, 0, 1), move_rep(far, 1, 0)]

    replica_hidden = own_hidden(1, weights_t[1])
    replica_hidden = jnp.concatenate(
        [replica_hidden, other_hidden(1, after(weights_t[1], replica_hidden))], axis=1
    )
    near = first_level(replica_hidden)

    shares = after(down_primary[0], scaled_primary).reshape(
        groups, hidden_units // groups, share
    )
    spread_weights = lax.all_to_all(shares, "ep", split_axis=0, concat_axis=0, tiled=True)

    primary_hidden = own_hidden(0, after(weights_t[0], replica_hidden))
    near, primary_hidden, spread_weights = together(near, primary_hidden, spread_weights)
    away = second_level(near[0], near[3])
    primary_hidden = jnp.concatenate(
        [primary_hidden, other_hidden(0, after(weights_t[0], primary_hidden))], axis=1
    )
    away, near, primary_hidden = together(away, near, primary_hidden)
    replica_pieces = [replica_hidden, near[1], near[2], near[3], near[0], *away]

    near = first_level(primary_hidden)
    replica_gradient = replica_gradient_call(replica_pieces, scaled_replica, places)
    spread = lax.all_to_all(
        replica_gradient.reshape(groups, hidden_units // groups, share),
        "ep",
        split_axis=0,
        concat_axis=0,
        tiled=True,
    )
    chosen = jnp.take(after(spread_weights, replica_gradient), replica_map, axis=0)
    near, replica_gradient, chosen = together(near, replica_gradient, chosen)
    away = second_level(near[0], near[3])
    priors = output_call(
        replica_pieces, after(down_replica[0], near), places, pos_cols, weight_cols, 1, []
    )
    spread, priors = together(spread, priors)
    owners = (replica_map[None, :] == jnp.arange(groups, dtype=jnp.int32)[:, None]).astype(BF16)
    summed = jnp.einsum("pj,jfd->pfd", owners, spread, preferred_element_type=F32).astype(BF16)
    replica_total = lax.all_to_all(
        summed, "ep", split_axis=0, concat_axis=0, tiled=True
    ).reshape(hidden_units, share)
    away, near, summed = together(away, near, summed)
    primary_pieces = [primary_hidden, near[1], near[2], near[3], near[0], *away]

    mine, theirs = output_call(
        primary_pieces, down_primary[0], places, pos_cols, weight_cols, 0, priors
    )
    arrived = swap_core(theirs)
    mine = (mine.astype(F32) + arrived.astype(F32)).astype(BF16).reshape(half_groups, count, share)
    received = [
        move_ep(mine[number], number // RING, -(number % RING)) for number in range(1, half_groups)
    ]
    layer = mine[0].astype(F32)
    for block in received:
        layer = layer + block.astype(F32)

    replica_total, chosen, _ = together(replica_total, chosen, received[:5])
    refreshed = lax.all_to_all(chosen, "ep", split_axis=0, concat_axis=0, tiled=True).reshape(
        1, hidden_units, share
    )

    down_new, moment1_new, moment2_new = update_call(
        primary_pieces,
        scaled_primary,
        places,
        replica_total,
        moment1[0],
        moment2[0],
        down_primary[0],
    )
    return (layer.astype(BF16), down_new[None], moment1_new[None], moment2_new[None], refreshed)


def solution(mesh):
    return jax.shard_map(
        per_device,
        mesh=mesh,
        in_specs=(
            P("ep", "rep"),
            P("ep", "rep"),
            P("ep", None),
            P("ep", None),
            P(),
            P("ep", None, "rep"),
            P("ep", None, "rep"),
            P("ep", None, "rep"),
            P("ep", None, "rep"),
            P("ep", None, "rep"),
            P("ep", None, "rep"),
            P("ep", None, "rep"),
            P("ep", None, "rep"),
        ),
        out_specs=(
            P("ep", "rep"),
            P("ep", None, "rep"),
            P("ep", None, "rep"),
            P("ep", None, "rep"),
            P("ep", None, "rep"),
        ),
        check_vma=False,
    )
```

```python
import functools

import jax
import jax.numpy as jnp
import numpy as np
from jax import lax
from jax.experimental import pallas as pl
from jax.experimental.pallas import tpu as pltpu
from jax.sharding import PartitionSpec as P

beta_one = 0.9
beta_two = 0.95
learn_rate = 0.001
weight_decay = 0.1
epsilon = 1e-08
correct_one = 1.0 - 0.9**10
correct_two = 1.0 - 0.95**10

BF16 = jnp.bfloat16
F32 = jnp.float32
NT = (((1,), (1,)), ((), ()))
TN = (((0,), (0,)), ((), ()))
VMEM_LIMIT = 58 * 1024 * 1024
HIDDEN_VMEM_LIMIT = 20 * 1024 * 1024
SCALED_VMEM_LIMIT = 12 * 1024 * 1024
SMALL_COST = pl.CostEstimate(flops=1000, bytes_accessed=1000, transcendentals=0)


ORDER = [(0, 0), (0, 3), (0, 1), (1, 0), (0, 2), (1, 3), (1, 1), (1, 2)]
RING = 4


def torus_place(i):
    ep, rep = i // 8, i % 8
    return 2 * (rep // 4) + ep // 8, rep % 4, (ep // 2) % 4, ep % 2


def torus_index(x, y, z, core):
    return (((x % 2) * 4 + z % 4) * 2 + core) * 8 + (x // 2) * 4 + y % 4


def torus_perm(axes, offset):
    perm = []
    for i in range(128):
        place = list(torus_place(i))
        axis = "xyz".index(axes[place[3]])
        place[axis] = (place[axis] - offset) % RING
        perm.append((i, torus_index(*place)))
    return perm


def move_torus(x, axes, offset):
    return lax.ppermute(x, ("ep", "rep"), torus_perm(axes, offset))


def move_rep(x, pair_offset, ring_offset):
    perm = []
    for i in range(8):
        pair, ring = (i // RING) ^ pair_offset, (i % RING - ring_offset) % RING
        perm.append((i, pair * RING + ring))
    return lax.ppermute(x, "rep", perm)


def move_ep(x, pair_offset, ring_offset):
    perm = []
    for i in range(16):
        pair, ring = (i // 8) ^ pair_offset, ((i // 2) % RING - ring_offset) % RING
        perm.append((i, (pair * RING + ring) * 2 + i % 2))
    return lax.ppermute(x, "ep", perm)


def swap_core(x):
    return lax.ppermute(x, "ep", [(i, i ^ 1) for i in range(16)])


def together(*values):
    return lax.optimization_barrier(values)


def after(value, *others):
    return lax.optimization_barrier((value, others))[0]


RINGS = [0, 3, 1, 2]


def gather_ring(x, axes):
    return together(x, *[move_torus(x, axes, offset) for offset in RINGS[1:]])


HALVES = [(0, 0), (0, 1), (3, 0), (1, 1), (3, 1), (1, 0), (2, 0), (2, 1)]
OFFSETS = [
    (first, second, last)
    for last, half in HALVES
    for second in RINGS[2 * half : 2 * half + 2]
    for first in RINGS
]


def block_slot(number, kind):
    first, second, last = OFFSETS[number]
    return (first % 2) * RING + (second if kind == 0 else last)


def one_hot(mask):
    return jnp.where(mask, 1.0, 0.0).astype(BF16)


def hidden_kernel(column, table, pos_ref, w_ref, *refs):
    pieces = refs[:-4]
    o_ref, x_ref, total_ref, sems = refs[-4:]
    step = pl.program_id(0)
    blocks, depth, width = x_ref.shape
    per_piece, _, share = pieces[0].shape

    @pl.when(step == 0)
    def _():
        for kind in range(2):

            @pl.when(table[len(OFFSETS)] == kind)
            def _():
                for number in sorted(range(len(OFFSETS)), key=lambda n: block_slot(n, kind)):
                    slot = block_slot(number, kind)
                    start = pl.multiple_of(table[number] * share, share)
                    pltpu.make_async_copy(
                        pieces[number // per_piece].at[number % per_piece],
                        x_ref.at[slot, :, pl.ds(start, share)],
                        sems.at[slot // 2],
                    ).start()

    ready = x_ref.at[pl.ds(2 * step, 2)]
    pltpu.make_async_copy(ready, ready, sems.at[step]).wait()
    tokens = x_ref[pl.ds(2 * step, 2)].reshape(2 * depth, width)
    sums = lax.dot_general(w_ref[...], tokens, NT, preferred_element_type=F32)
    units = o_ref.shape[0]
    hidden = (jax.nn.silu(sums[:units]) * sums[units:]).astype(BF16)
    target = lax.broadcasted_iota(jnp.int32, (2 * depth, o_ref.shape[1]), 1)
    chosen = one_hot(pos_ref[:, column : column + 1] == target)
    picked = jnp.dot(hidden, chosen, preferred_element_type=F32)

    @pl.when(step == 0)
    def _():
        total_ref[...] = picked

    @pl.when(step > 0)
    def _():
        total_ref[...] += picked

    @pl.when(step == pl.num_programs(0) - 1)
    def _():
        o_ref[...] = total_ref[...].astype(BF16)


def hidden_call(weights_t, pieces, table, pos_cols, slot, parity, rows):
    depth, share = pieces[0].shape[1:]
    units, width = weights_t.shape[0] // 4, weights_t.shape[1]
    blocks = pos_cols.shape[0] // depth
    return pl.pallas_call(
        functools.partial(hidden_kernel, slot * 2 + parity),
        grid_spec=pltpu.PrefetchScalarGridSpec(
            num_scalar_prefetch=1,
            grid=(blocks // 2,),
            in_specs=[
                pl.BlockSpec((2 * depth, pos_cols.shape[1]), lambda i, t: (i, 0)),
                pl.BlockSpec((2 * units, width), lambda i, t: (slot, 0)),
            ]
            + [pl.BlockSpec(memory_space=pl.ANY)] * len(pieces),
            out_specs=pl.BlockSpec((units, rows), lambda i, t: (0, 0)),
            scratch_shapes=[
                pltpu.VMEM((blocks, depth, width), BF16),
                pltpu.VMEM((units, rows), F32),
                pltpu.SemaphoreType.DMA((blocks // 2,)),
            ],
        ),
        out_shape=jax.ShapeDtypeStruct((units, rows), BF16),
        compiler_params=pltpu.CompilerParams(vmem_limit_bytes=HIDDEN_VMEM_LIMIT if slot else VMEM_LIMIT),
        cost_estimate=SMALL_COST,
        name="hidden",
    )(table, pos_cols, weights_t, *pieces)


def scaled_kernel(column, pos_ref, w_ref, c_ref, o_ref):
    scaled = (w_ref[:, column : column + 1] * c_ref[...].astype(F32)).astype(BF16)
    rows = o_ref.shape[0]
    row = lax.broadcasted_iota(jnp.int32, (rows, c_ref.shape[0]), 0)
    chosen = one_hot(pos_ref[column : column + 1, :] == row)
    o_ref[...] = jnp.dot(chosen, scaled, preferred_element_type=F32).astype(BF16)


def scaled_call(cotangents, pos_rows, weight_cols, slot, parity, rows):
    count, share = cotangents.shape
    return pl.pallas_call(
        functools.partial(scaled_kernel, slot * 2 + parity),
        out_shape=jax.ShapeDtypeStruct((rows, share), BF16),
        compiler_params=pltpu.CompilerParams(vmem_limit_bytes=SCALED_VMEM_LIMIT),
        cost_estimate=SMALL_COST,
        name="scaled",
    )(pos_rows, weight_cols, cotangents)


def load_hidden(units, table, refs, hidden, sems):
    copies = []
    for place, ref in enumerate(refs):
        start = pl.multiple_of(table[place] * units, units)
        copies.append(
            pltpu.make_async_copy(
                ref, hidden.at[pl.ds(start, units)], sems.at[place]
            )
        )
    for copy in copies:
        copy.start()
    for copy in copies:
        copy.wait()


def gradient_tile(hidden, a_ref, b_ref, tile):
    start = pl.multiple_of(pl.program_id(0) * tile, tile)
    half = a_ref.shape[0]
    return jnp.dot(
        hidden[pl.ds(start, tile), :half], a_ref[...], preferred_element_type=F32
    ) + jnp.dot(hidden[pl.ds(start, tile), half:], b_ref[...], preferred_element_type=F32)


def replica_gradient_kernel(units, table, a_ref, b_ref, *refs):
    pieces, (o_ref, hidden, sems) = refs[:-3], refs[-3:]

    @pl.when(pl.program_id(0) == 0)
    def _():
        load_hidden(units, table, pieces, hidden, sems)

    o_ref[...] = gradient_tile(hidden, a_ref, b_ref, o_ref.shape[0]).astype(BF16)


def replica_gradient_call(pieces, scaled, table):
    units, rows = pieces[0].shape
    half, share = scaled[0].shape
    total = 8 * units
    tile = 512
    return pl.pallas_call(
        functools.partial(replica_gradient_kernel, units),
        grid_spec=pltpu.PrefetchScalarGridSpec(
            num_scalar_prefetch=1,
            grid=(total // tile,),
            in_specs=[pl.BlockSpec((half, share), lambda i, t: (0, 0))] * 2
            + [pl.BlockSpec(memory_space=pl.ANY)] * len(pieces),
            out_specs=pl.BlockSpec((tile, share), lambda i, t: (i, 0)),
            scratch_shapes=[
                pltpu.VMEM((total, rows), BF16),
                pltpu.SemaphoreType.DMA((len(pieces),)),
            ],
        ),
        out_shape=jax.ShapeDtypeStruct((total, share), BF16),
        compiler_params=pltpu.CompilerParams(vmem_limit_bytes=VMEM_LIMIT),
        cost_estimate=SMALL_COST,
        name="replica_gradient",
    )(table, *scaled, *pieces)


def update_kernel(units, table, a_ref, b_ref, total_ref, one_ref, two_ref, down_ref, *refs):
    pieces = refs[:-5]
    down_out, one_out, two_out, hidden, sems = refs[-5:]

    @pl.when(pl.program_id(0) == 0)
    def _():
        load_hidden(units, table, pieces, hidden, sems)

    gradient = gradient_tile(hidden, a_ref, b_ref, down_out.shape[0]) + total_ref[...].astype(F32)
    one = beta_one * one_ref[...] + (1.0 - beta_one) * gradient
    two = beta_two * two_ref[...] + (1.0 - beta_two) * gradient * gradient
    one_out[...] = one
    two_out[...] = two
    update = (learn_rate / correct_one) * one / (jnp.sqrt(two * (1.0 / correct_two)) + epsilon)
    down_out[...] = (
        down_ref[...].astype(F32) * (1.0 - learn_rate * weight_decay) - update
    ).astype(BF16)


def update_call(pieces, scaled, table, total_gradient, moment1, moment2, down):
    units, rows = pieces[0].shape
    half, share = scaled[0].shape
    total = 8 * units
    tile = 256
    block = pl.BlockSpec((tile, share), lambda i, t: (i, 0))
    return pl.pallas_call(
        functools.partial(update_kernel, units),
        grid_spec=pltpu.PrefetchScalarGridSpec(
            num_scalar_prefetch=1,
            grid=(total // tile,),
            in_specs=[pl.BlockSpec((half, share), lambda i, t: (0, 0))] * 2
            + [block] * 4
            + [pl.BlockSpec(memory_space=pl.ANY)] * len(pieces),
            out_specs=[block] * 3,
            scratch_shapes=[
                pltpu.VMEM((total, rows), BF16),
                pltpu.SemaphoreType.DMA((len(pieces),)),
            ],
        ),
        out_shape=[
            jax.ShapeDtypeStruct((total, share), BF16),
            jax.ShapeDtypeStruct((total, share), F32),
            jax.ShapeDtypeStruct((total, share), F32),
        ],
        compiler_params=pltpu.CompilerParams(vmem_limit_bytes=VMEM_LIMIT),
        cost_estimate=SMALL_COST,
        name="update",
    )(table, *scaled, total_gradient, moment1, moment2, down, *pieces)


def output_kernel(slot, units, with_prior, table, down_ref, pos_ref, w_ref, *refs):
    if with_prior:
        priors, refs = refs[:2], refs[2:]
    pieces = refs[:-5]
    results, (hidden, outputs, sems) = refs[-5:-3], refs[-3:]
    rows = hidden.shape[1] // 2
    load_hidden(units, table, pieces, hidden, sems)
    tile = 256
    for half in (1, 0):
        column = slot * 2 + half
        o_ref = results[half]
        for begin in range(half * rows, (half + 1) * rows, 256):
            outputs[begin : begin + 256, :] = lax.dot_general(
                hidden[:, begin : begin + 256], down_ref[...], TN, preferred_element_type=F32
            ).astype(BF16)
        for begin in range(0, o_ref.shape[0], tile):
            window = slice(begin, begin + tile)
            target = lax.broadcasted_iota(jnp.int32, (tile, rows), 1)
            chosen = one_hot(pos_ref[window, column : column + 1] == target)
            picked = jnp.dot(
                chosen, outputs[half * rows : (half + 1) * rows, :], preferred_element_type=F32
            )
            value = w_ref[window, column : column + 1] * picked
            if with_prior:
                value = value + priors[half][window, :]
            o_ref[window, :] = value.astype(o_ref.dtype)


def output_call(pieces, down, table, pos_cols, weight_cols, slot, priors):
    units, both = pieces[0].shape
    total, share = down.shape
    count = pos_cols.shape[0]
    vmem = pl.BlockSpec(memory_space=pltpu.VMEM)
    result = jax.ShapeDtypeStruct((count, share), BF16 if priors else F32)
    return pl.pallas_call(
        functools.partial(output_kernel, slot, units, bool(priors)),
        in_specs=[pl.BlockSpec(memory_space=pltpu.SMEM)]
        + [vmem] * (3 + len(priors))
        + [pl.BlockSpec(memory_space=pl.ANY)] * len(pieces),
        out_specs=[vmem] * 2,
        scratch_shapes=[
            pltpu.VMEM((total, both), BF16),
            pltpu.VMEM((both, share), BF16),
            pltpu.SemaphoreType.DMA((len(pieces),)),
        ],
        out_shape=[result] * 2,
        compiler_params=pltpu.CompilerParams(vmem_limit_bytes=VMEM_LIMIT),
        cost_estimate=pl.CostEstimate(
            flops=2 * total * both * share + 2 * count * both * share,
            bytes_accessed=2 * (total * both + total * share) + 12 * count * share,
            transcendentals=0,
        ),
        name="output",
    )(table, down, pos_cols, weight_cols, *priors, *pieces)


def per_device(
    tokens,
    cotangent,
    router_weights,
    routes,
    replica_map,
    gate_primary,
    up_primary,
    down_primary,
    gate_replica,
    up_replica,
    down_replica,
    moment1,
    moment2,
):
    groups = lax.axis_size("ep")
    count, top = routes.shape
    hidden_units, share = down_primary.shape[1:]
    half_groups = groups // 2
    rows = half_groups * (3 * count * top // (2 * groups))
    ep = lax.axis_index("ep")
    rep = lax.axis_index("rep")
    core = ep % 2

    line = gather_ring(tokens[None], "xx")
    cot_line = together(cotangent, *[move_ep(cotangent, 0, dr) for dr in range(1, RING)])
    line, cot_line = together(jnp.concatenate(line, axis=0), cot_line)
    cot_line = jnp.concatenate(cot_line, axis=0)
    plane = gather_ring(line, "zy")
    cot_own = jnp.concatenate([cot_line, move_ep(cot_line, 1, 0)], axis=0)
    low, high = jnp.concatenate(plane[:2], axis=0), jnp.concatenate(plane[2:], axis=0)
    low, high, cot_own = together(low, high, cot_own)
    below_low = move_torus(low, "yz", 3)
    above_high = move_torus(high, "yz", 1)
    cot_other = swap_core(cot_own)
    cot_halves = [cot_own, cot_other]

    slot_ids = jnp.arange(2 * groups, dtype=jnp.int32)
    dense = jnp.sum(
        jnp.where(routes[None] == slot_ids[:, None, None], router_weights[None], 0.0), axis=2
    ).reshape(groups, 2, count)
    served = lax.all_to_all(
        after(dense, low), "ep", split_axis=0, concat_axis=0, tiled=True
    )
    x, y, z = 2 * (rep // 4) + ep // 8, rep % 4, (ep // 2) % 4
    slots = np.arange(half_groups, dtype=np.int32)
    blocks = 2 * ((((ep // 8) + slots // RING) % 2) * RING + (z + slots % RING) % RING)
    served = served[jnp.concatenate([blocks + core, blocks + 1 - core])]
    served = jnp.transpose(served.reshape(2, half_groups, 2, count), (2, 0, 1, 3)).reshape(
        4, half_groups, count
    )
    hit = (served != 0.0).astype(F32)
    earlier = jnp.triu(jnp.ones((count, count), F32), 1)
    blocks_before = jnp.triu(jnp.ones((half_groups, half_groups), F32), 1)
    inside = jnp.einsum("lbt,tu->lbu", hit, earlier, precision=lax.Precision.HIGHEST)
    before = jnp.einsum(
        "lb,bc->lc", jnp.sum(hit, axis=2), blocks_before, precision=lax.Precision.HIGHEST
    )
    pos_rows = jnp.where(hit > 0, (inside + before[:, :, None]).astype(jnp.int32), -1)
    pos_rows = pos_rows.reshape(4, half_groups * count)
    pos_cols = pos_rows.T
    weight_cols = served.reshape(4, half_groups * count).T
    projections = after((gate_primary, up_primary, gate_replica, up_replica), low)
    weights_t = jnp.concatenate([projection[0].T for projection in projections], axis=0)

    offsets = np.array(OFFSETS, np.int32)

    def part_table(kind):
        from_y = (y + jnp.where(kind == 0, offsets[:, 2], offsets[:, 1])) % RING
        part = (((x + offsets[:, 0]) % RING) // 2) * RING + from_y
        return jnp.concatenate([part, kind[None]]).astype(jnp.int32)

    own_table, other_table = part_table(core), part_table(1 - core)
    rep_pair, rep_ring = rep // RING, rep % RING
    order = np.array(ORDER, np.int32)
    places = ((rep_pair ^ order[:, 0]) * RING + (rep_ring + order[:, 1]) % RING).astype(jnp.int32)

    low_other, high_other = swap_core(low), swap_core(high)
    below_low, above_high, weights_t, pos_cols, low_other, high_other = together(
        below_low, above_high, weights_t, pos_cols, low_other, high_other
    )
    below_high = move_torus(high, "yz", 3)
    above_low = move_torus(low, "yz", 1)
    far_low = move_torus(below_low, "yz", 3)
    far_high = move_torus(above_high, "yz", 1)

    def scale(slot):
        return [
            scaled_call(cot_halves[parity], pos_rows, weight_cols, slot, parity, rows)
            for parity in range(2)
        ]

    scaled_replica, scaled_primary = scale(1), scale(0)
    below_low_other, above_high_other = [
        swap_core(piece) for piece in after((below_low, above_high), scaled_replica, scaled_primary)
    ]
    (
        below_high,
        above_low,
        far_low,
        far_high,
        scaled_replica,
        scaled_primary,
        pos_cols,
        weight_cols,
        own_table,
        other_table,
        places,
    ) = together(
        below_high,
        above_low,
        far_low,
        far_high,
        scaled_replica,
        scaled_primary,
        pos_cols,
        weight_cols,
        own_table,
        other_table,
        places,
    )
    own_pieces = [low, high, below_low, above_high, below_high, above_low, far_low, far_high]
    other_pieces = [low_other, high_other, below_low_other, above_high_other] + [
        swap_core(piece) for piece in own_pieces[4:]
    ]

    def own_hidden(slot, weights):
        return hidden_call(weights, own_pieces, own_table, pos_cols, slot, 0, rows)

    def other_hidden(slot, weights):
        return hidden_call(weights, other_pieces, other_table, pos_cols, slot, 1, rows)

    def first_level(hidden):
        return [move_rep(hidden, dp, dr) for dp, dr in ((0, 2), (0, 3), (0, 1), (1, 0))]

    def second_level(far, across):
        return [move_rep(across, 0, 3), move_rep(across, 0, 1), move_rep(far, 1, 0)]

    replica_hidden = own_hidden(1, weights_t)
    replica_hidden = jnp.concatenate(
        [replica_hidden, other_hidden(1, after(weights_t, replica_hidden))], axis=1
    )
    near = first_level(replica_hidden)

    shares = after(down_primary[0], scaled_primary).reshape(
        groups, hidden_units // groups, share
    )
    spread_weights = lax.all_to_all(shares, "ep", split_axis=0, concat_axis=0, tiled=True)

    primary_hidden = own_hidden(0, after(weights_t, replica_hidden))
    chosen = jnp.take(after(spread_weights, primary_hidden), replica_map, axis=0)
    near, primary_hidden, chosen = together(near, primary_hidden, chosen)
    away = second_level(near[0], near[3])
    primary_hidden = jnp.concatenate(
        [primary_hidden, other_hidden(0, after(weights_t, primary_hidden))], axis=1
    )
    away, near, primary_hidden = together(away, near, primary_hidden)
    replica_pieces = [replica_hidden, near[1], near[2], near[3], near[0], *away]

    near = first_level(primary_hidden)
    replica_gradient = replica_gradient_call(replica_pieces, scaled_replica, places)
    spread = lax.all_to_all(
        replica_gradient.reshape(groups, hidden_units // groups, share),
        "ep",
        split_axis=0,
        concat_axis=0,
        tiled=True,
    )
    near, spread, chosen = together(near, spread, chosen)
    refreshed = lax.all_to_all(chosen, "ep", split_axis=0, concat_axis=0, tiled=True).reshape(
        1, hidden_units, share
    )
    away = second_level(near[0], near[3])
    priors = output_call(
        replica_pieces, after(down_replica[0], near), places, pos_cols, weight_cols, 1, []
    )
    spread, priors, refreshed = together(spread, priors, refreshed)
    owners = (replica_map[None, :] == jnp.arange(groups, dtype=jnp.int32)[:, None]).astype(BF16)
    summed = jnp.einsum("pj,jfd->pfd", owners, spread, preferred_element_type=F32).astype(BF16)
    replica_total = lax.all_to_all(
        summed, "ep", split_axis=0, concat_axis=0, tiled=True
    ).reshape(hidden_units, share)
    away, near, summed = together(away, near, summed)
    primary_pieces = [primary_hidden, near[1], near[2], near[3], near[0], *away]

    mine, theirs = output_call(
        primary_pieces, down_primary[0], places, pos_cols, weight_cols, 0, priors
    )
    arrived = swap_core(theirs)
    mine = (mine.astype(F32) + arrived.astype(F32)).astype(BF16).reshape(half_groups, count, share)
    mine = mine[((slots // RING) ^ (ep // 8)) * RING + (slots % RING - z) % RING]
    mine, replica_total = together(mine, replica_total)
    returned = lax.all_to_all(
        mine,
        "ep",
        split_axis=0,
        concat_axis=0,
        axis_index_groups=[list(range(0, groups, 2)), list(range(1, groups, 2))],
        tiled=True,
    )
    layer = jnp.sum(returned.astype(F32), axis=0)

    down_new, moment1_new, moment2_new = update_call(
        primary_pieces,
        scaled_primary,
        places,
        replica_total,
        moment1[0],
        moment2[0],
        down_primary[0],
    )
    return (layer.astype(BF16), down_new[None], moment1_new[None], moment2_new[None], refreshed)


def solution(mesh):
    return jax.shard_map(
        per_device,
        mesh=mesh,
        in_specs=(
            P("ep", "rep"),
            P("ep", "rep"),
            P("ep", None),
            P("ep", None),
            P(),
            P("ep", None, "rep"),
            P("ep", None, "rep"),
            P("ep", None, "rep"),
            P("ep", None, "rep"),
            P("ep", None, "rep"),
            P("ep", None, "rep"),
            P("ep", None, "rep"),
            P("ep", None, "rep"),
        ),
        out_specs=(
            P("ep", "rep"),
            P("ep", None, "rep"),
            P("ep", None, "rep"),
            P("ep", None, "rep"),
            P("ep", None, "rep"),
        ),
        check_vma=False,
    )
```

```python
import functools

import jax
import jax.numpy as jnp
import numpy as np
from jax import lax
from jax.experimental import pallas as pl
from jax.experimental.pallas import tpu as pltpu
from jax.sharding import PartitionSpec as P

beta_one = 0.9
beta_two = 0.95
learn_rate = 0.001
weight_decay = 0.1
epsilon = 1e-08
correct_one = 1.0 - 0.9**10
correct_two = 1.0 - 0.95**10

BF16 = jnp.bfloat16
F32 = jnp.float32
NT = (((1,), (1,)), ((), ()))
TN = (((0,), (0,)), ((), ()))
VMEM_LIMIT = 58 * 1024 * 1024
HIDDEN_VMEM_LIMIT = 20 * 1024 * 1024
SCALED_VMEM_LIMIT = 12 * 1024 * 1024
SMALL_COST = pl.CostEstimate(flops=1000, bytes_accessed=1000, transcendentals=0)


ORDER = [(0, 0), (0, 3), (0, 1), (1, 0), (0, 2), (1, 3), (1, 1), (1, 2)]
RING = 4


def torus_place(i):
    ep, rep = i // 8, i % 8
    return 2 * (rep // 4) + ep // 8, rep % 4, (ep // 2) % 4, ep % 2


def torus_index(x, y, z, core):
    return (((x % 2) * 4 + z % 4) * 2 + core) * 8 + (x // 2) * 4 + y % 4


def torus_perm(axes, offset):
    perm = []
    for i in range(128):
        place = list(torus_place(i))
        axis = "xyz".index(axes[place[3]])
        place[axis] = (place[axis] - offset) % RING
        perm.append((i, torus_index(*place)))
    return perm


def move_torus(x, axes, offset):
    return lax.ppermute(x, ("ep", "rep"), torus_perm(axes, offset))


def move_rep(x, pair_offset, ring_offset):
    perm = []
    for i in range(8):
        pair, ring = (i // RING) ^ pair_offset, (i % RING - ring_offset) % RING
        perm.append((i, pair * RING + ring))
    return lax.ppermute(x, "rep", perm)


def move_ep(x, pair_offset, ring_offset):
    perm = []
    for i in range(16):
        pair, ring = (i // 8) ^ pair_offset, ((i // 2) % RING - ring_offset) % RING
        perm.append((i, (pair * RING + ring) * 2 + i % 2))
    return lax.ppermute(x, "ep", perm)


def swap_core(x):
    return lax.ppermute(x, "ep", [(i, i ^ 1) for i in range(16)])


def together(*values):
    return lax.optimization_barrier(values)


def after(value, *others):
    return lax.optimization_barrier((value, others))[0]


RINGS = [0, 3, 1, 2]


def gather_ring(x, axes):
    return together(x, *[move_torus(x, axes, offset) for offset in RINGS[1:]])


HALVES = [(0, 0), (0, 1), (3, 0), (1, 1), (3, 1), (1, 0), (2, 0), (2, 1)]
OFFSETS = [
    (first, second, last)
    for last, half in HALVES
    for second in RINGS[2 * half : 2 * half + 2]
    for first in RINGS
]


def block_slot(number, kind):
    first, second, last = OFFSETS[number]
    return (first % 2) * RING + (second if kind == 0 else last)


def one_hot(mask):
    return jnp.where(mask, 1.0, 0.0).astype(BF16)


def hidden_kernel(column, table, pos_ref, w_ref, *refs):
    pieces = refs[:-4]
    o_ref, x_ref, total_ref, sems = refs[-4:]
    step = pl.program_id(0)
    blocks, depth, width = x_ref.shape
    per_piece, _, share = pieces[0].shape

    @pl.when(step == 0)
    def _():
        for kind in range(2):

            @pl.when(table[len(OFFSETS)] == kind)
            def _():
                for number in sorted(range(len(OFFSETS)), key=lambda n: block_slot(n, kind)):
                    slot = block_slot(number, kind)
                    start = pl.multiple_of(table[number] * share, share)
                    pltpu.make_async_copy(
                        pieces[number // per_piece].at[number % per_piece],
                        x_ref.at[slot, :, pl.ds(start, share)],
                        sems.at[slot // 2],
                    ).start()

    ready = x_ref.at[pl.ds(2 * step, 2)]
    pltpu.make_async_copy(ready, ready, sems.at[step]).wait()
    tokens = x_ref[pl.ds(2 * step, 2)].reshape(2 * depth, width)
    sums = lax.dot_general(w_ref[...], tokens, NT, preferred_element_type=F32)
    units = o_ref.shape[0]
    hidden = (jax.nn.silu(sums[:units]) * sums[units:]).astype(BF16)
    target = lax.broadcasted_iota(jnp.int32, (2 * depth, o_ref.shape[1]), 1)
    chosen = one_hot(pos_ref[:, column : column + 1] == target)
    picked = jnp.dot(hidden, chosen, preferred_element_type=F32)

    @pl.when(step == 0)
    def _():
        total_ref[...] = picked

    @pl.when(step > 0)
    def _():
        total_ref[...] += picked

    @pl.when(step == pl.num_programs(0) - 1)
    def _():
        o_ref[...] = total_ref[...].astype(BF16)


def hidden_call(weights_t, pieces, table, pos_cols, slot, parity, rows):
    depth, share = pieces[0].shape[1:]
    units, width = weights_t.shape[0] // 4, weights_t.shape[1]
    blocks = pos_cols.shape[0] // depth
    return pl.pallas_call(
        functools.partial(hidden_kernel, slot * 2 + parity),
        grid_spec=pltpu.PrefetchScalarGridSpec(
            num_scalar_prefetch=1,
            grid=(blocks // 2,),
            in_specs=[
                pl.BlockSpec((2 * depth, pos_cols.shape[1]), lambda i, t: (i, 0)),
                pl.BlockSpec((2 * units, width), lambda i, t: (slot, 0)),
            ]
            + [pl.BlockSpec(memory_space=pl.ANY)] * len(pieces),
            out_specs=pl.BlockSpec((units, rows), lambda i, t: (0, 0)),
            scratch_shapes=[
                pltpu.VMEM((blocks, depth, width), BF16),
                pltpu.VMEM((units, rows), F32),
                pltpu.SemaphoreType.DMA((blocks // 2,)),
            ],
        ),
        out_shape=jax.ShapeDtypeStruct((units, rows), BF16),
        compiler_params=pltpu.CompilerParams(vmem_limit_bytes=HIDDEN_VMEM_LIMIT if slot else VMEM_LIMIT),
        cost_estimate=SMALL_COST,
        name="hidden",
    )(table, pos_cols, weights_t, *pieces)


def scaled_kernel(column, pos_ref, w_ref, c_ref, o_ref):
    scaled = (w_ref[:, column : column + 1] * c_ref[...].astype(F32)).astype(BF16)
    rows = o_ref.shape[0]
    row = lax.broadcasted_iota(jnp.int32, (rows, c_ref.shape[0]), 0)
    chosen = one_hot(pos_ref[column : column + 1, :] == row)
    o_ref[...] = jnp.dot(chosen, scaled, preferred_element_type=F32).astype(BF16)


def scaled_call(cotangents, pos_rows, weight_cols, slot, parity, rows):
    count, share = cotangents.shape
    return pl.pallas_call(
        functools.partial(scaled_kernel, slot * 2 + parity),
        out_shape=jax.ShapeDtypeStruct((rows, share), BF16),
        compiler_params=pltpu.CompilerParams(vmem_limit_bytes=SCALED_VMEM_LIMIT),
        cost_estimate=SMALL_COST,
        name="scaled",
    )(pos_rows, weight_cols, cotangents)


def load_hidden(units, table, refs, hidden, sems):
    copies = []
    for place, ref in enumerate(refs):
        start = pl.multiple_of(table[place] * units, units)
        copies.append(
            pltpu.make_async_copy(
                ref, hidden.at[pl.ds(start, units)], sems.at[place]
            )
        )
    for copy in copies:
        copy.start()
    for copy in copies:
        copy.wait()


def gradient_tile(hidden, a_ref, b_ref, tile):
    start = pl.multiple_of(pl.program_id(0) * tile, tile)
    half = a_ref.shape[0]
    return jnp.dot(
        hidden[pl.ds(start, tile), :half], a_ref[...], preferred_element_type=F32
    ) + jnp.dot(hidden[pl.ds(start, tile), half:], b_ref[...], preferred_element_type=F32)


def replica_gradient_kernel(units, table, a_ref, b_ref, *refs):
    pieces, (o_ref, hidden, sems) = refs[:-3], refs[-3:]

    @pl.when(pl.program_id(0) == 0)
    def _():
        load_hidden(units, table, pieces, hidden, sems)

    o_ref[...] = gradient_tile(hidden, a_ref, b_ref, o_ref.shape[0]).astype(BF16)


def replica_gradient_call(pieces, scaled, table):
    units, rows = pieces[0].shape
    half, share = scaled[0].shape
    total = 8 * units
    tile = 512
    return pl.pallas_call(
        functools.partial(replica_gradient_kernel, units),
        grid_spec=pltpu.PrefetchScalarGridSpec(
            num_scalar_prefetch=1,
            grid=(total // tile,),
            in_specs=[pl.BlockSpec((half, share), lambda i, t: (0, 0))] * 2
            + [pl.BlockSpec(memory_space=pl.ANY)] * len(pieces),
            out_specs=pl.BlockSpec((tile, share), lambda i, t: (i, 0)),
            scratch_shapes=[
                pltpu.VMEM((total, rows), BF16),
                pltpu.SemaphoreType.DMA((len(pieces),)),
            ],
        ),
        out_shape=jax.ShapeDtypeStruct((total, share), BF16),
        compiler_params=pltpu.CompilerParams(vmem_limit_bytes=VMEM_LIMIT),
        cost_estimate=SMALL_COST,
        name="replica_gradient",
    )(table, *scaled, *pieces)


def update_kernel(units, table, a_ref, b_ref, total_ref, one_ref, two_ref, down_ref, *refs):
    pieces = refs[:-5]
    down_out, one_out, two_out, hidden, sems = refs[-5:]

    @pl.when(pl.program_id(0) == 0)
    def _():
        load_hidden(units, table, pieces, hidden, sems)

    gradient = gradient_tile(hidden, a_ref, b_ref, down_out.shape[0]) + total_ref[...].astype(F32)
    one = beta_one * one_ref[...] + (1.0 - beta_one) * gradient
    two = beta_two * two_ref[...] + (1.0 - beta_two) * gradient * gradient
    one_out[...] = one
    two_out[...] = two
    update = (learn_rate / correct_one) * one / (jnp.sqrt(two * (1.0 / correct_two)) + epsilon)
    down_out[...] = (
        down_ref[...].astype(F32) * (1.0 - learn_rate * weight_decay) - update
    ).astype(BF16)


def update_call(pieces, scaled, table, total_gradient, moment1, moment2, down):
    units, rows = pieces[0].shape
    half, share = scaled[0].shape
    total = 8 * units
    tile = 256
    block = pl.BlockSpec((tile, share), lambda i, t: (i, 0))
    return pl.pallas_call(
        functools.partial(update_kernel, units),
        grid_spec=pltpu.PrefetchScalarGridSpec(
            num_scalar_prefetch=1,
            grid=(total // tile,),
            in_specs=[pl.BlockSpec((half, share), lambda i, t: (0, 0))] * 2
            + [block] * 4
            + [pl.BlockSpec(memory_space=pl.ANY)] * len(pieces),
            out_specs=[block] * 3,
            scratch_shapes=[
                pltpu.VMEM((total, rows), BF16),
                pltpu.SemaphoreType.DMA((len(pieces),)),
            ],
        ),
        out_shape=[
            jax.ShapeDtypeStruct((total, share), BF16),
            jax.ShapeDtypeStruct((total, share), F32),
            jax.ShapeDtypeStruct((total, share), F32),
        ],
        compiler_params=pltpu.CompilerParams(vmem_limit_bytes=VMEM_LIMIT),
        cost_estimate=SMALL_COST,
        name="update",
    )(table, *scaled, total_gradient, moment1, moment2, down, *pieces)


def output_kernel(slot, units, with_prior, table, down_ref, pos_ref, w_ref, *refs):
    if with_prior:
        priors, refs = refs[:2], refs[2:]
    pieces = refs[:-5]
    results, (hidden, outputs, sems) = refs[-5:-3], refs[-3:]
    rows = hidden.shape[1] // 2
    load_hidden(units, table, pieces, hidden, sems)
    tile = 256
    for half in (1, 0):
        column = slot * 2 + half
        o_ref = results[half]
        for begin in range(half * rows, (half + 1) * rows, 256):
            outputs[begin : begin + 256, :] = lax.dot_general(
                hidden[:, begin : begin + 256], down_ref[...], TN, preferred_element_type=F32
            ).astype(BF16)
        for begin in range(0, o_ref.shape[0], tile):
            window = slice(begin, begin + tile)
            target = lax.broadcasted_iota(jnp.int32, (tile, rows), 1)
            chosen = one_hot(pos_ref[window, column : column + 1] == target)
            picked = jnp.dot(
                chosen, outputs[half * rows : (half + 1) * rows, :], preferred_element_type=F32
            )
            value = w_ref[window, column : column + 1] * picked
            if with_prior:
                value = value + priors[half][window, :]
            o_ref[window, :] = value.astype(o_ref.dtype)


def output_call(pieces, down, table, pos_cols, weight_cols, slot, priors):
    units, both = pieces[0].shape
    total, share = down.shape
    count = pos_cols.shape[0]
    vmem = pl.BlockSpec(memory_space=pltpu.VMEM)
    result = jax.ShapeDtypeStruct((count, share), BF16 if priors else F32)
    return pl.pallas_call(
        functools.partial(output_kernel, slot, units, bool(priors)),
        in_specs=[pl.BlockSpec(memory_space=pltpu.SMEM)]
        + [vmem] * (3 + len(priors))
        + [pl.BlockSpec(memory_space=pl.ANY)] * len(pieces),
        out_specs=[vmem] * 2,
        scratch_shapes=[
            pltpu.VMEM((total, both), BF16),
            pltpu.VMEM((both, share), BF16),
            pltpu.SemaphoreType.DMA((len(pieces),)),
        ],
        out_shape=[result] * 2,
        compiler_params=pltpu.CompilerParams(vmem_limit_bytes=VMEM_LIMIT),
        cost_estimate=pl.CostEstimate(
            flops=2 * total * both * share + 2 * count * both * share,
            bytes_accessed=2 * (total * both + total * share) + 12 * count * share,
            transcendentals=0,
        ),
        name="output",
    )(table, down, pos_cols, weight_cols, *priors, *pieces)


def per_device(
    tokens,
    cotangent,
    router_weights,
    routes,
    replica_map,
    gate_primary,
    up_primary,
    down_primary,
    gate_replica,
    up_replica,
    down_replica,
    moment1,
    moment2,
):
    groups = lax.axis_size("ep")
    count, top = routes.shape
    hidden_units, share = down_primary.shape[1:]
    half_groups = groups // 2
    rows = half_groups * (3 * count * top // (2 * groups))
    ep = lax.axis_index("ep")
    rep = lax.axis_index("rep")
    core = ep % 2

    line = gather_ring(tokens[None], "xx")
    cot_line = together(cotangent, *[move_ep(cotangent, 0, dr) for dr in range(1, RING)])
    line, cot_line = together(jnp.concatenate(line, axis=0), cot_line)
    cot_line = jnp.concatenate(cot_line, axis=0)
    plane = gather_ring(line, "zy")
    cot_own = jnp.concatenate([cot_line, move_ep(cot_line, 1, 0)], axis=0)
    low, high = jnp.concatenate(plane[:2], axis=0), jnp.concatenate(plane[2:], axis=0)
    low, high, cot_own = together(low, high, cot_own)
    below_low = move_torus(low, "yz", 3)
    above_high = move_torus(high, "yz", 1)
    cot_other = swap_core(cot_own)
    cot_halves = [cot_own, cot_other]

    shares = after(down_primary[0], line).reshape(groups, hidden_units // groups, share)
    spread_weights = lax.all_to_all(shares, "ep", split_axis=0, concat_axis=0, tiled=True)

    x, y, z = 2 * (rep // 4) + ep // 8, rep % 4, (ep // 2) % 4
    slots = np.arange(half_groups, dtype=np.int32)
    projections = after((gate_primary, up_primary, gate_replica, up_replica), low)
    weights_t = jnp.concatenate([projection[0].T for projection in projections], axis=0)

    offsets = np.array(OFFSETS, np.int32)

    def part_table(kind):
        from_y = (y + jnp.where(kind == 0, offsets[:, 2], offsets[:, 1])) % RING
        part = (((x + offsets[:, 0]) % RING) // 2) * RING + from_y
        return jnp.concatenate([part, kind[None]]).astype(jnp.int32)

    own_table, other_table = part_table(core), part_table(1 - core)
    rep_pair, rep_ring = rep // RING, rep % RING
    order = np.array(ORDER, np.int32)
    places = ((rep_pair ^ order[:, 0]) * RING + (rep_ring + order[:, 1]) % RING).astype(jnp.int32)

    low_other, high_other = swap_core(low), swap_core(high)
    below_low, above_high, weights_t, low_other, high_other = together(
        below_low, above_high, weights_t, low_other, high_other
    )
    below_high = move_torus(high, "yz", 3)
    above_low = move_torus(low, "yz", 1)
    far_low = move_torus(below_low, "yz", 3)
    far_high = move_torus(above_high, "yz", 1)

    slot_ids = jnp.arange(2 * groups, dtype=jnp.int32)
    dense = jnp.sum(
        jnp.where(routes[None] == slot_ids[:, None, None], router_weights[None], 0.0), axis=2
    ).reshape(groups, 2, count)
    served = lax.all_to_all(
        after(dense, below_low, spread_weights), "ep", split_axis=0, concat_axis=0, tiled=True
    )
    blocks = 2 * ((((ep // 8) + slots // RING) % 2) * RING + (z + slots % RING) % RING)
    served = served[jnp.concatenate([blocks + core, blocks + 1 - core])]
    served = jnp.transpose(served.reshape(2, half_groups, 2, count), (2, 0, 1, 3)).reshape(
        4, half_groups, count
    )
    hit = (served != 0.0).astype(F32)
    earlier = jnp.triu(jnp.ones((count, count), F32), 1)
    blocks_before = jnp.triu(jnp.ones((half_groups, half_groups), F32), 1)
    inside = jnp.einsum("lbt,tu->lbu", hit, earlier, precision=lax.Precision.HIGHEST)
    before = jnp.einsum(
        "lb,bc->lc", jnp.sum(hit, axis=2), blocks_before, precision=lax.Precision.HIGHEST
    )
    pos_rows = jnp.where(hit > 0, (inside + before[:, :, None]).astype(jnp.int32), -1)
    pos_rows = pos_rows.reshape(4, half_groups * count)
    pos_cols = pos_rows.T
    weight_cols = served.reshape(4, half_groups * count).T


    def scale(slot):
        return [
            scaled_call(cot_halves[parity], pos_rows, weight_cols, slot, parity, rows)
            for parity in range(2)
        ]

    scaled_replica, scaled_primary = scale(1), scale(0)
    below_low_other, above_high_other = [
        swap_core(piece) for piece in after((below_low, above_high), scaled_replica, scaled_primary)
    ]
    (
        below_high,
        above_low,
        far_low,
        far_high,
        scaled_replica,
        scaled_primary,
        pos_cols,
        weight_cols,
        own_table,
        other_table,
        places,
    ) = together(
        below_high,
        above_low,
        far_low,
        far_high,
        scaled_replica,
        scaled_primary,
        pos_cols,
        weight_cols,
        own_table,
        other_table,
        places,
    )
    own_pieces = [low, high, below_low, above_high, below_high, above_low, far_low, far_high]
    other_pieces = [low_other, high_other, below_low_other, above_high_other] + [
        swap_core(piece) for piece in own_pieces[4:]
    ]

    def own_hidden(slot, weights):
        return hidden_call(weights, own_pieces, own_table, pos_cols, slot, 0, rows)

    def other_hidden(slot, weights):
        return hidden_call(weights, other_pieces, other_table, pos_cols, slot, 1, rows)

    def first_level(hidden):
        return [move_rep(hidden, dp, dr) for dp, dr in ((0, 2), (0, 3), (0, 1), (1, 0))]

    def second_level(far, across):
        return [move_rep(across, 0, 3), move_rep(across, 0, 1), move_rep(far, 1, 0)]

    chosen = after(jnp.take(spread_weights, replica_map, axis=0), scaled_primary)
    refreshed = lax.all_to_all(chosen, "ep", split_axis=0, concat_axis=0, tiled=True).reshape(
        1, hidden_units, share
    )

    replica_hidden = own_hidden(1, weights_t)
    replica_hidden = jnp.concatenate(
        [replica_hidden, other_hidden(1, after(weights_t, replica_hidden))], axis=1
    )
    near = first_level(replica_hidden)

    primary_hidden = own_hidden(0, after(weights_t, replica_hidden))
    near, primary_hidden, refreshed = together(near, primary_hidden, refreshed)
    away = second_level(near[0], near[3])
    primary_hidden = jnp.concatenate(
        [primary_hidden, other_hidden(0, after(weights_t, primary_hidden))], axis=1
    )
    away, near, primary_hidden = together(away, near, primary_hidden)
    replica_pieces = [replica_hidden, near[1], near[2], near[3], near[0], *away]

    near = first_level(primary_hidden)
    replica_gradient = replica_gradient_call(replica_pieces, scaled_replica, places)
    spread = lax.all_to_all(
        replica_gradient.reshape(groups, hidden_units // groups, share),
        "ep",
        split_axis=0,
        concat_axis=0,
        tiled=True,
    )
    away = second_level(near[0], near[3])
    priors = output_call(
        replica_pieces, after(down_replica[0], near), places, pos_cols, weight_cols, 1, []
    )
    spread, priors = together(spread, priors)
    owners = (replica_map[None, :] == jnp.arange(groups, dtype=jnp.int32)[:, None]).astype(BF16)
    summed = jnp.einsum("pj,jfd->pfd", owners, spread, preferred_element_type=F32).astype(BF16)
    replica_total = lax.all_to_all(
        summed, "ep", split_axis=0, concat_axis=0, tiled=True
    ).reshape(hidden_units, share)
    away, near, summed = together(away, near, summed)
    primary_pieces = [primary_hidden, near[1], near[2], near[3], near[0], *away]

    mine, theirs = output_call(
        primary_pieces, down_primary[0], places, pos_cols, weight_cols, 0, priors
    )
    arrived = swap_core(theirs)
    mine = (mine.astype(F32) + arrived.astype(F32)).astype(BF16).reshape(half_groups, count, share)
    mine = mine[((slots // RING) ^ (ep // 8)) * RING + (slots % RING - z) % RING]
    mine, replica_total = together(mine, replica_total)
    returned = lax.all_to_all(
        mine,
        "ep",
        split_axis=0,
        concat_axis=0,
        axis_index_groups=[list(range(0, groups, 2)), list(range(1, groups, 2))],
        tiled=True,
    )
    layer = jnp.sum(returned.astype(F32), axis=0)

    down_new, moment1_new, moment2_new = update_call(
        primary_pieces,
        scaled_primary,
        places,
        replica_total,
        moment1[0],
        moment2[0],
        down_primary[0],
    )
    return (layer.astype(BF16), down_new[None], moment1_new[None], moment2_new[None], refreshed)


def solution(mesh):
    return jax.shard_map(
        per_device,
        mesh=mesh,
        in_specs=(
            P("ep", "rep"),
            P("ep", "rep"),
            P("ep", None),
            P("ep", None),
            P(),
            P("ep", None, "rep"),
            P("ep", None, "rep"),
            P("ep", None, "rep"),
            P("ep", None, "rep"),
            P("ep", None, "rep"),
            P("ep", None, "rep"),
            P("ep", None, "rep"),
            P("ep", None, "rep"),
        ),
        out_specs=(
            P("ep", "rep"),
            P("ep", None, "rep"),
            P("ep", None, "rep"),
            P("ep", None, "rep"),
            P("ep", None, "rep"),
        ),
        check_vma=False,
    )
```
